256 devices in a mesh: ctx: 64 (over x_lo, z, y), tp: 4 (over x_hi, core).
Axes of the slice: x: 4 (x_hi: 2, x_lo: 2; x = x_hi * 2 + x_lo), y: 4, z: 8, core: 2. Of those that a mesh axis runs over, the one named last changes fastest.
Arguments:
- queries: bfloat16 [8192, 4096], P('ctx', 'tp'), may hold values from -64 to 64
- keys: bfloat16 [8192, 1024], P('ctx', 'tp'), may hold values from -4 to 4
- values: bfloat16 [8192, 1024], P('ctx', 'tp'), may hold values from -6 to 6
- grad_out: bfloat16 [8192, 4096], P('ctx', 'tp'), may hold values from -6 to 6
- out_weight: bfloat16 [4096, 4096], P(None, 'tp'), may hold values from -0.09375 to 0.09375
- segments: int32 [8192], P('ctx'), may hold values from 0 to 1, as said below
Outputs:
- query_grad: bfloat16 [8192, 4096], P('ctx', 'tp')
- key_gradient: bfloat16 [8192, 1024], P('ctx', 'tp')
- value_gradient: bfloat16 [8192, 1024], P('ctx', 'tp')
The draws below stay inside these ranges and needn't reach their ends.
Inputs may be any that keep to these rules, and one draw needn't show every extreme that they name: `segments`: document numbers never fall along the tokens, start at 0, and every document starts at a multiple of 8 tokens; there are exactly 2 documents.
All inputs are finite; a program needn't handle non-finite values.
Results may differ from the reference program's by a relative error of at most 0.015.
Values may be sent and summed in bfloat16 or wider, within the bound.
No kernel may reach another device: no remote copies, remote signals or barrier semaphores. Data moves between devices by JAX's collectives and lax.ppermute only.
A program may use at most 128 MiB of HBM per device.

```python
import jax
import jax.numpy as jnp
from jax import lax

D = 4096
QUERY_HEADS = 32
KEY_VALUE_HEADS = 8
HEAD_SIZE = 128
DOCS = 2
SEQUENCE_TOKENS = 8192


def draw_keys(key, part):
    owned_part = jax.random.fold_in(key, 3)
    final_result = jnp.clip(jax.random.normal(owned_part, (SEQUENCE_TOKENS, KEY_VALUE_HEADS * HEAD_SIZE), jnp.float32), -4.0, 4.0)
    return final_result.astype(jnp.bfloat16)


def draw_queries(key, part):
    owned_part = jax.random.fold_in(key, 5)
    final_result = jnp.clip(jax.random.normal(owned_part, (SEQUENCE_TOKENS, QUERY_HEADS * HEAD_SIZE), jnp.float32), -4.0, 4.0)
    return final_result.astype(jnp.bfloat16)


def draw_segments(key, part):
    key = jax.random.fold_in(key, 9)
    groups = SEQUENCE_TOKENS // 8
    order = jax.random.permutation(key, groups - 1) + 1
    chosen = order[:DOCS - 1]
    flags = jnp.zeros((groups,), jnp.int32).at[chosen].set(1)
    numbers = jnp.cumsum(flags).astype(jnp.int32)
    return jnp.repeat(numbers, 8)


def steps_of(own_key, dims, cuts, smallest, high):
    def one(dim, parts):
        heights = jax.random.uniform(jax.random.fold_in(jax.random.fold_in(own_key, 6), dim), (parts,), jnp.float32, smallest / len(cuts), high / len(cuts))
        return jnp.repeat(jnp.exp(heights), dims[dim] // parts).reshape((-1,) + (1,) * (len(dims) - dim - 1))

    level = one(*cuts[0])
    for cut in cuts[1:]:
        level = level * one(*cut)
    return level


def scatter_about(key, dims, deviation, limit, cuts=(), kind=jnp.bfloat16):
    values = deviation * jax.random.normal(key, dims, jnp.float32)
    if cuts:
        values = values * steps_of(key, dims, cuts, -0.22, 0.18)
    return jnp.clip(values, -limit, limit).astype(kind)


def setup_inputs(seed: int = 0) -> dict:
    key_of = jax.random.split(jax.random.key(seed), 7)
    return {
        "queries": draw_queries(jax.random.fold_in(key_of[6], 71), 0),
        "keys": draw_keys(jax.random.fold_in(key_of[6], 71), 0),
        "values": scatter_about(key_of[2], (SEQUENCE_TOKENS, KEY_VALUE_HEADS * HEAD_SIZE), 1.0, 6.0, ((0, 64), (1, 4))),
        "grad_out": scatter_about(key_of[3], (SEQUENCE_TOKENS, D), 1.0, 6.0, ((0, 64), (1, 4))),
        "out_weight": scatter_about(key_of[4], (D, QUERY_HEADS * HEAD_SIZE), D ** -0.5, 0.09375, ((1, 4),)),
        "segments": draw_segments(jax.random.fold_in(key_of[6], 71), 0),
    }


def reference(queries, keys, values, grad_out, out_weight, segments):
    group_ratio = QUERY_HEADS // KEY_VALUE_HEADS
    scale = HEAD_SIZE ** -0.5
    upstream = jnp.dot(grad_out, out_weight, preferred_element_type=jnp.float32).astype(jnp.bfloat16)
    block = min(512, SEQUENCE_TOKENS)
    count = SEQUENCE_TOKENS // block
    positions = jnp.arange(SEQUENCE_TOKENS, dtype=jnp.int32)

    def single_group(group):
        col_q = (group * group_ratio * HEAD_SIZE).astype(jnp.int32)
        col_k = (group * HEAD_SIZE).astype(jnp.int32)
        query_all = lax.dynamic_slice_in_dim(queries, col_q, group_ratio * HEAD_SIZE, 1).reshape(SEQUENCE_TOKENS, group_ratio, HEAD_SIZE)
        upstream_all = lax.dynamic_slice_in_dim(upstream, col_q, group_ratio * HEAD_SIZE, 1).reshape(SEQUENCE_TOKENS, group_ratio, HEAD_SIZE)
        key_all = lax.dynamic_slice_in_dim(keys, col_k, HEAD_SIZE, 1).astype(jnp.float32)
        value_all = lax.dynamic_slice_in_dim(values, col_k, HEAD_SIZE, 1).astype(jnp.float32)

        def step(carry, index):
            key_acc, value_acc = carry
            start = (index * block).astype(jnp.int32)
            query_blk = lax.dynamic_slice_in_dim(query_all, start, block, 0).astype(jnp.float32)
            up_blk = lax.dynamic_slice_in_dim(upstream_all, start, block, 0).astype(jnp.float32)
            qpos = lax.dynamic_slice_in_dim(positions, start, block, 0)
            qseg = lax.dynamic_slice_in_dim(segments, start, block, 0)
            allowed = (positions[None, :] <= qpos[:, None]) & (segments[None, :] == qseg[:, None])
            scores = jnp.einsum("qrd,kd->rqk", query_blk, key_all) * scale
            scores = jnp.where(allowed[None], scores, jnp.float32(-1e30))
            top = jnp.max(scores, axis=-1, keepdims=True)
            lse = top + jnp.log(jnp.sum(jnp.where(allowed[None], jnp.exp(scores - top), 0.0), axis=-1, keepdims=True))
            probs = jnp.where(allowed[None], jnp.exp(scores - lse), 0.0)
            dprobs = jnp.einsum("qrd,kd->rqk", up_blk, value_all)
            delta = jnp.sum(probs * dprobs, axis=-1, keepdims=True)
            dscores = probs * (dprobs - delta)
            probs_low = probs.astype(jnp.bfloat16).astype(jnp.float32)
            dscores_low = dscores.astype(jnp.bfloat16).astype(jnp.float32)
            query_grad = (jnp.einsum("rqk,kd->qrd", dscores_low, key_all) * scale).astype(jnp.bfloat16)
            key_acc = key_acc + jnp.einsum("rqk,qrd->kd", dscores_low, query_blk)
            value_acc = value_acc + jnp.einsum("rqk,qrd->kd", probs_low, up_blk)
            return (key_acc, value_acc), query_grad

        zeros = jnp.zeros((SEQUENCE_TOKENS, HEAD_SIZE), jnp.float32)
        (key_acc, value_acc), query_parts = lax.scan(step, (zeros, zeros), jnp.arange(count, dtype=jnp.int32))
        query_grad = query_parts.reshape(SEQUENCE_TOKENS, group_ratio, HEAD_SIZE)
        return query_grad, (key_acc * scale).astype(jnp.bfloat16), value_acc.astype(jnp.bfloat16)

    query_grad_local, key_grad_local, value_grad_local = lax.map(single_group, jnp.arange(KEY_VALUE_HEADS, dtype=jnp.int32))
    query_grad = jnp.transpose(query_grad_local, (1, 0, 2, 3)).reshape(SEQUENCE_TOKENS, QUERY_HEADS * HEAD_SIZE)
    key_gradient = jnp.transpose(key_grad_local, (1, 0, 2)).reshape(SEQUENCE_TOKENS, KEY_VALUE_HEADS * HEAD_SIZE)
    value_gradient = jnp.transpose(value_grad_local, (1, 0, 2)).reshape(SEQUENCE_TOKENS, KEY_VALUE_HEADS * HEAD_SIZE)
    return query_grad, key_gradient, value_gradient
```

```python
import functools
import math

import jax
import jax.numpy as jnp
from jax import lax
from jax.experimental import pallas as pl
from jax.experimental.pallas import tpu as pltpu
from jax.sharding import Mesh, PartitionSpec as P

HEAD = 128
RATIO = 4
CHUNK = 128
XL, NZ, NY = 2, 8, 4
HALF = NZ * NY * CHUNK
PLANE = NY * CHUNK
KEYS = XL * NZ * CHUNK
KT = 256
ROWS = 1024
PAIRS = 4
GROUP = RATIO * HEAD
SCALE = HEAD**-0.5
C2 = SCALE * math.log2(math.e)
NEG = -1e30
WIDE = jnp.float32
LOW = jnp.bfloat16
NT = (((1,), (1,)), ((), ()))
NN = (((1,), (0,)), ((), ()))
VMEM_LIMIT = 48 * 1024 * 1024


def dot(a, b, dims=NN):
    return lax.dot_general(a, b, dims, preferred_element_type=WIDE)


def vspec():
    return pl.BlockSpec(memory_space=pltpu.VMEM)


def sspec():
    return pl.BlockSpec(memory_space=pltpu.SMEM)


def params():
    return pltpu.CompilerParams(vmem_limit_bytes=VMEM_LIMIT)


def up_first(pos, own, mate, weight):
    def kernel(pos_ref, g0, g1, w_ref, out_ref):
        @pl.when(pl.program_id(0) == 0)
        def _():
            out_ref[...] = dot(g0[...], w_ref[...])

        @pl.when(pl.program_id(0) == 1)
        def _():
            out_ref[...] += dot(g1[...], w_ref[...])

    full = pl.BlockSpec((CHUNK, 1024), lambda r, pos: (0, 0))
    return pl.pallas_call(
        kernel,
        grid_spec=pltpu.PrefetchScalarGridSpec(
            num_scalar_prefetch=1,
            grid=(2,),
            in_specs=[
                full,
                full,
                pl.BlockSpec((1024, 1024), lambda r, pos: (jnp.bitwise_xor(pos[0], r), 0)),
            ],
            out_specs=pl.BlockSpec((CHUNK, 1024), lambda r, pos: (0, 0)),
        ),
        out_shape=jax.ShapeDtypeStruct((CHUNK, 1024), WIDE),
        compiler_params=params(),
        name="upstream_first",
    )(pos, own, mate, weight)


def up_second(pos, part, far, far_mate, weight):
    def kernel(pos_ref, part_ref, g0, g1, w_ref, own_ref, oth_ref, acc):
        @pl.when(pl.program_id(0) == 0)
        def _():
            acc[...] = part_ref[...] + dot(g0[...], w_ref[...])

        @pl.when(pl.program_id(0) == 1)
        def _():
            acc[...] += dot(g1[...], w_ref[...])
            xl = pos_ref[1]
            own_ref[...] = acc[:, pl.ds(pl.multiple_of(xl * GROUP, GROUP), GROUP)].astype(LOW)
            oth_ref[...] = acc[:, pl.ds(pl.multiple_of((1 - xl) * GROUP, GROUP), GROUP)].astype(LOW)

    full = pl.BlockSpec((CHUNK, 1024), lambda r, pos: (0, 0))
    half = pl.BlockSpec((CHUNK, GROUP), lambda r, pos: (0, 0))
    return pl.pallas_call(
        kernel,
        grid_spec=pltpu.PrefetchScalarGridSpec(
            num_scalar_prefetch=1,
            grid=(2,),
            in_specs=[
                full,
                full,
                full,
                pl.BlockSpec((1024, 1024), lambda r, pos: (jnp.bitwise_xor(pos[0], 2 + r), 0)),
            ],
            out_specs=[half, half],
            scratch_shapes=[pltpu.VMEM((CHUNK, 1024), WIDE)],
        ),
        out_shape=[jax.ShapeDtypeStruct((CHUNK, GROUP), LOW)] * 2,
        compiler_params=params(),
        name="upstream_second",
    )(pos, part, far, far_mate, weight)


def stack_rows(dst, blocks):
    for o in range(2):
        for dy in range(NY):
            for h in range(RATIO):
                start = (dy % 2) * GROUP + h * CHUNK
                dst[o * 2 + dy // 2, start : start + CHUNK, :] = blocks[o][dy][
                    :, h * HEAD : (h + 1) * HEAD
                ]


def key_chunk(xl, z, o, d):
    half = xl if o == 0 else 1 - xl
    return half * NZ + lax.rem(z + d, NZ)


def row_limits(pair, xl, z, y, b):
    o = pair // 2
    h = jnp.where(o == 0, xl, 1 - xl)
    dy0 = (pair % 2) * 2
    y0 = lax.rem(y + dy0, NY)
    y1 = lax.rem(y + dy0 + 1, NY)
    base = h * HALF + z * PLANE
    lane = lax.broadcasted_iota(jnp.int32, (1, ROWS), 1)
    off = jnp.where(lane < GROUP, y0, y1) * CHUNK + jnp.bitwise_and(lane, CHUNK - 1)
    key_base = h * NZ * CHUNK + z * CHUNK
    high = key_base + jnp.clip(off - y * CHUNK + 1, 0, CHUNK)
    bh = b // HALF
    bz = (b - bh * HALF) // PLANE
    cb = (
        bh * NZ * CHUNK
        + bz * CHUNK
        + jnp.clip(b - bh * HALF - bz * PLANE - y * CHUNK, 0, CHUNK)
    )
    low = jnp.where(base + off >= b, cb, 0)
    first = base + jnp.minimum(y0, y1) * CHUNK
    t_low = jnp.where(first >= b, cb // KT, 0)
    top = key_base + jnp.where(jnp.maximum(y0, y1) >= y, CHUNK, 0)
    t_high = (top + KT - 1) // KT
    return low, high, t_low, t_high


def masked_scores(k, q, t, low, high):
    s = dot(k, q, NT) * C2
    kk = t * KT + lax.broadcasted_iota(jnp.int32, (KT, ROWS), 0)
    return jnp.where((kk >= low) & (kk < high), s, NEG)


def forward(scalars, q_blocks, kv_blocks):
    def kernel(sc, *refs):
        q = [refs[0:4], refs[4:8]]
        kv = refs[8:16]
        o_ref, ml_ref, qs, kc, vt = refs[16:]
        xl, z, y, b = sc[0], sc[1], sc[2], sc[3]
        stack_rows(qs, q)
        for d in range(NZ):
            for o in range(2):
                at = key_chunk(xl, z, o, d)
                rows = slice(o * CHUNK, (o + 1) * CHUNK)
                kc[at] = kv[d][rows, :HEAD]
                vt[at, :HEAD, :] = kv[d][rows, HEAD:].T
                vt[at, HEAD:, :] = jnp.ones((16, CHUNK), LOW)

        def one_pair(pair, _):
            low, high, t_low, t_high = row_limits(pair, xl, z, y, b)
            o_ref[pair] = jnp.zeros((HEAD + 16, ROWS), WIDE)
            qp = qs[pair]

            def tile(t, top):
                k = kc[pl.ds(2 * t, 2)].reshape(KT, HEAD)
                s = masked_scores(k, qp, t, low, high)
                new = jnp.maximum(top, jnp.max(s, axis=0, keepdims=True))
                p = jnp.exp2(s - new).astype(LOW)
                v = jnp.concatenate([vt[2 * t], vt[2 * t + 1]], axis=1)
                o_ref[pair] = o_ref[pair] * jnp.exp2(top - new) + dot(v, p)
                return new

            top = lax.fori_loop(t_low, t_high, tile, jnp.full((1, ROWS), NEG, WIDE))
            ml_ref[pl.ds(pair, 1), :] = top
            return 0

        lax.fori_loop(0, PAIRS, one_pair, 0)
        for pair in range(PAIRS):
            ml_ref[PAIRS + pair : PAIRS + pair + 1, :] = o_ref[pair, HEAD : HEAD + 1, :]

    return pl.pallas_call(
        kernel,
        in_specs=[sspec()] + [vspec()] * 16,
        out_specs=[vspec()] * 2,
        out_shape=[
            jax.ShapeDtypeStruct((PAIRS, HEAD + 16, ROWS), WIDE),
            jax.ShapeDtypeStruct((2 * PAIRS, ROWS), WIDE),
        ],
        scratch_shapes=[
            pltpu.VMEM((PAIRS, ROWS, HEAD), LOW),
            pltpu.VMEM((XL * NZ, CHUNK, HEAD), LOW),
            pltpu.VMEM((XL * NZ, HEAD + 16, CHUNK), LOW),
        ],
        compiler_params=params(),
        cost_estimate=pl.CostEstimate(
            flops=8 * 10**9, bytes_accessed=6 * 2**20, transcendentals=4 * 2**20
        ),
        name="forward",
    )(scalars, *q_blocks[0], *q_blocks[1], *kv_blocks)


def weighted(o_part, ml, u_blocks):
    def kernel(o_ref, ml_ref, *refs):
        u = [refs[0:4], refs[4:8]]
        out_ref = refs[8]
        out_ref[: 2 * PAIRS, :] = ml_ref[...]
        for o in range(2):
            for dy in range(NY):
                pair = o * 2 + dy // 2
                for h in range(RATIO):
                    start = (dy % 2) * GROUP + h * CHUNK
                    ut = u[o][dy][:, h * HEAD : (h + 1) * HEAD].astype(WIDE).T
                    part = ut * o_ref[pair, :HEAD, start : start + CHUNK]
                    out_ref[
                        2 * PAIRS + pair : 2 * PAIRS + pair + 1, start : start + CHUNK
                    ] = jnp.sum(part, axis=0, keepdims=True)

    return pl.pallas_call(
        kernel,
        in_specs=[vspec()] * 10,
        out_specs=vspec(),
        out_shape=jax.ShapeDtypeStruct((3 * PAIRS, ROWS), WIDE),
        compiler_params=params(),
        name="weighted",
    )(o_part, ml, *u_blocks[0], *u_blocks[1])


def backward(scalars, stats, q_blocks, u_blocks, kv_blocks):
    def kernel(sc, *refs):
        st = refs[0:4]
        q = [refs[4:8], refs[8:12]]
        u = [refs[12:16], refs[16:20]]
        kv = refs[20:28]
        dq_out = refs[28:32]
        dkv_out = refs[32:40]
        qs, us, kc, vc, kt, dk, dv, dqt, al, lse_s, delta_s = refs[40:]
        xl, z, y, b = sc[0], sc[1], sc[2], sc[3]
        stack_rows(qs, q)
        stack_rows(us, u)
        for d in range(NZ):
            for o in range(2):
                at = key_chunk(xl, z, o, d)
                rows = slice(o * CHUNK, (o + 1) * CHUNK)
                key = kv[d][rows, :HEAD]
                kc[at] = key
                vc[at] = kv[d][rows, HEAD:]
                kt[at] = key.T
        dk[...] = jnp.zeros(dk.shape, WIDE)
        dv[...] = jnp.zeros(dv.shape, WIDE)
        dqt[...] = jnp.zeros(dqt.shape, WIDE)

        for i in range(NY):
            for row in range(0, 3 * PAIRS, 2):
                for dy in range(NY):
                    e = (dy - i) % NY
                    to, frm = (dy % 2) * GROUP, (e % 2) * GROUP
                    al[i, row + dy // 2 : row + dy // 2 + 1, to : to + GROUP] = st[i][
                        row + e // 2 : row + e // 2 + 1, frm : frm + GROUP
                    ]
        tops = [al[i, :PAIRS] for i in range(NY)]
        top = functools.reduce(jnp.maximum, tops)
        factors = [jnp.exp2(t - top) for t in tops]
        mass = sum(f * al[i, PAIRS : 2 * PAIRS] for i, f in enumerate(factors))
        share = sum(f * al[i, 2 * PAIRS :] for i, f in enumerate(factors))
        lse_s[...] = top + jnp.log2(mass)
        delta_s[...] = share / mass

        def one_pair(pair, _):
            low, high, t_low, t_high = row_limits(pair, xl, z, y, b)
            lse = lse_s[pl.ds(pair, 1), :]
            delta = delta_s[pl.ds(pair, 1), :]
            qp = qs[pair]
            up = us[pair]

            def tile(t, _):
                k = kc[pl.ds(2 * t, 2)].reshape(KT, HEAD)
                v = vc[pl.ds(2 * t, 2)].reshape(KT, HEAD)
                p = jnp.exp2(masked_scores(k, qp, t, low, high) - lse)
                ds = (p * (dot(v, up, NT) - delta)).astype(LOW)
                p = p.astype(LOW)
                dv[pl.ds(2 * t, 2)] += dot(p, up).reshape(2, CHUNK, HEAD)
                dk[pl.ds(2 * t, 2)] += dot(ds, qp).reshape(2, CHUNK, HEAD)
                kt_tile = jnp.concatenate([kt[2 * t], kt[2 * t + 1]], axis=1)
                dqt[pair] += dot(kt_tile, ds)
                return 0

            lax.fori_loop(t_low, t_high, tile, 0)
            return 0

        lax.fori_loop(0, PAIRS, one_pair, 0)

        for dy in range(NY):
            for o in range(2):
                for h in range(RATIO):
                    start = (dy % 2) * GROUP + h * CHUNK
                    part = dqt[o * 2 + dy // 2, :, start : start + CHUNK].T * SCALE
                    dq_out[dy][
                        o * CHUNK : (o + 1) * CHUNK, h * HEAD : (h + 1) * HEAD
                    ] = part.astype(dq_out[dy].dtype)
        for d in range(NZ):
            for o in range(2):
                at = key_chunk(xl, z, o, d)
                rows = slice(o * CHUNK, (o + 1) * CHUNK)
                dkv_out[d][rows, :HEAD] = (dk[at] * SCALE).astype(dkv_out[d].dtype)
                dkv_out[d][rows, HEAD:] = dv[at].astype(dkv_out[d].dtype)

    kept = (0, 2, NZ - 2)
    out = pl.pallas_call(
        kernel,
        in_specs=[sspec()] + [vspec()] * 28,
        out_specs=[vspec()] * 12,
        out_shape=[
            jax.ShapeDtypeStruct((2 * CHUNK, GROUP), WIDE if dy == 0 else LOW)
            for dy in range(NY)
        ]
        + [
            jax.ShapeDtypeStruct((2 * CHUNK, 2 * HEAD), WIDE if d in kept else LOW)
            for d in range(NZ)
        ],
        scratch_shapes=[
            pltpu.VMEM((PAIRS, ROWS, HEAD), LOW),
            pltpu.VMEM((PAIRS, ROWS, HEAD), LOW),
            pltpu.VMEM((XL * NZ, CHUNK, HEAD), LOW),
            pltpu.VMEM((XL * NZ, CHUNK, HEAD), LOW),
            pltpu.VMEM((XL * NZ, HEAD, CHUNK), LOW),
            pltpu.VMEM((XL * NZ, CHUNK, HEAD), WIDE),
            pltpu.VMEM((XL * NZ, CHUNK, HEAD), WIDE),
            pltpu.VMEM((PAIRS, HEAD, ROWS), WIDE),
            pltpu.VMEM((NY, 3 * PAIRS, ROWS), WIDE),
            pltpu.VMEM((PAIRS, ROWS), WIDE),
            pltpu.VMEM((PAIRS, ROWS), WIDE),
        ],
        compiler_params=params(),
        cost_estimate=pl.CostEstimate(
            flops=16 * 10**9, bytes_accessed=8 * 2**20, transcendentals=4 * 2**20
        ),
        name="backward",
    )(scalars, *stats, *q_blocks[0], *q_blocks[1], *u_blocks[0], *u_blocks[1], *kv_blocks)
    return out[:NY], out[NY:]


def shift(x, axis, size, d):
    return lax.ppermute(x, axis, [(i, (i - d) % size) for i in range(size)])


def per_device(queries, keys, values, grad_out, out_weight, segments):
    xl, z, y = lax.axis_index("xl"), lax.axis_index("z"), lax.axis_index("y")
    tp = lax.axis_index("xh") * 2 + lax.axis_index("core")

    def part(x, group, width):
        return lax.dynamic_slice_in_dim(x, group * width, width, 1)

    def key_value(group):
        return jnp.concatenate([part(keys, group, HEAD), part(values, group, HEAD)], axis=1)

    pos = jnp.stack([tp, xl]).astype(jnp.int32)
    far = shift(grad_out, "xh", 2, 1)
    mate = shift(grad_out, "core", 2, 1)
    kv_in = shift(key_value(1 - xl), "xl", 2, 1)
    q_in = shift(part(queries, 1 - xl, GROUP), "xl", 2, 1)
    q_own = part(queries, xl, GROUP)
    bound = lax.psum(jnp.sum((segments == 0).astype(jnp.int32)), ("xl", "z", "y"))
    scalars = jnp.stack([xl, z, y, bound]).astype(jnp.int32)

    kv_mine = jnp.concatenate([key_value(xl), kv_in], axis=0)
    kv_blocks = [kv_mine] + [None] * 7
    for d in (1, 7, 2, 6, 4):
        kv_blocks[d] = shift(kv_mine, "z", NZ, d)
    kv_blocks[3] = shift(kv_blocks[2], "z", NZ, 1)
    kv_blocks[5] = shift(kv_blocks[6], "z", NZ, -1)

    def along_y(x):
        return [x] + [shift(x, "y", NY, d) for d in (1, 2, 3)]

    q_blocks = [along_y(q_own), along_y(q_in)]

    u_part = up_first(pos, grad_out, mate, out_weight)
    far_mate = shift(far, "core", 2, 1)
    u_own, u_oth = up_second(pos, u_part, far, far_mate, out_weight)
    u_in = shift(u_oth, "xl", 2, 1)
    u_blocks = [along_y(u_own), along_y(u_in)]

    o_part, ml = forward(scalars, q_blocks, kv_blocks)
    mine = weighted(o_part, ml, u_blocks)
    stats = along_y(mine)
    dq, dkv = backward(scalars, stats, q_blocks, u_blocks, kv_blocks)

    up3 = shift(dkv[3], "z", NZ, -1)
    down3 = shift(dkv[5], "z", NZ, 1)
    got4 = shift(dkv[4], "z", NZ, 4)
    up2 = (dkv[2] + up3.astype(WIDE)).astype(LOW)
    down2 = (dkv[6] + down3.astype(WIDE)).astype(LOW)
    got = [
        shift(dkv[1], "z", NZ, -1),
        shift(dkv[7], "z", NZ, 1),
        shift(up2, "z", NZ, -2),
        shift(down2, "z", NZ, 2),
        got4,
    ]
    dkv_sum = dkv[0]
    for g in got:
        dkv_sum = dkv_sum + g.astype(WIDE)

    dq_sum = dq[0]
    for d in (1, 2, 3):
        dq_sum = dq_sum + shift(dq[d], "y", NY, -d).astype(WIDE)

    dq_back = shift(dq_sum[CHUNK:].astype(LOW), "xl", 2, 1)
    dkv_back = shift(dkv_sum[CHUNK:].astype(LOW), "xl", 2, 1)
    dq_own = dq_sum[:CHUNK].astype(LOW)
    dkv_own = dkv_sum[:CHUNK].astype(LOW)

    def join(a, c):
        return jnp.where(
            xl == 0, jnp.concatenate([a, c], axis=1), jnp.concatenate([c, a], axis=1)
        )

    return (
        join(dq_own, dq_back),
        join(dkv_own[:, :HEAD], dkv_back[:, :HEAD]),
        join(dkv_own[:, HEAD:], dkv_back[:, HEAD:]),
    )


def solution(mesh):
    fine = Mesh(mesh.devices.reshape(XL, NZ, NY, 2, 2), ("xl", "z", "y", "xh", "core"))
    ctx, tp = ("xl", "z", "y"), ("xh", "core")
    in_specs = (P(ctx, tp), P(ctx, tp), P(ctx, tp), P(ctx, tp), P(None, tp), P(ctx))
    out_specs = (P(ctx, tp), P(ctx, tp), P(ctx, tp))
    return jax.shard_map(
        per_device, mesh=fine, in_specs=in_specs, out_specs=out_specs, check_vma=False
    )
```

```python
import functools
import math

import jax
import jax.numpy as jnp
from jax import lax
from jax.experimental import pallas as pl
from jax.experimental.pallas import tpu as pltpu
from jax.sharding import Mesh, PartitionSpec as P

HEAD = 128
RATIO = 4
CHUNK = 128
XL, NZ, NY = 2, 8, 4
HALF = NZ * NY * CHUNK
PLANE = NY * CHUNK
PIECE = CHUNK + 16
KEYS = NZ * CHUNK
KT = 256
ROWS = 1024
PAIRS = 4
GROUP = RATIO * HEAD
SCALE = HEAD**-0.5
C2 = SCALE * math.log2(math.e)
NEG = -1e30
WIDE = jnp.float32
LOW = jnp.bfloat16
NT = (((1,), (1,)), ((), ()))
NN = (((1,), (0,)), ((), ()))
VMEM_LIMIT = 48 * 1024 * 1024


def dot(a, b, dims=NN):
    return lax.dot_general(a, b, dims, preferred_element_type=WIDE)


def vspec():
    return pl.BlockSpec(memory_space=pltpu.VMEM)


def sspec():
    return pl.BlockSpec(memory_space=pltpu.SMEM)


def params():
    return pltpu.CompilerParams(vmem_limit_bytes=VMEM_LIMIT)


def up_first(pos, own, mate, weight):
    def kernel(pos_ref, g0, g1, w_ref, out_ref):
        @pl.when(pl.program_id(0) == 0)
        def _():
            out_ref[...] = dot(g0[...], w_ref[...])

        @pl.when(pl.program_id(0) == 1)
        def _():
            out_ref[...] += dot(g1[...], w_ref[...])

    full = pl.BlockSpec((CHUNK, 1024), lambda r, pos: (0, 0))
    return pl.pallas_call(
        kernel,
        grid_spec=pltpu.PrefetchScalarGridSpec(
            num_scalar_prefetch=1,
            grid=(2,),
            in_specs=[
                full,
                full,
                pl.BlockSpec((1024, 1024), lambda r, pos: (jnp.bitwise_xor(pos[0], r), 0)),
            ],
            out_specs=pl.BlockSpec((CHUNK, 1024), lambda r, pos: (0, 0)),
        ),
        out_shape=jax.ShapeDtypeStruct((CHUNK, 1024), WIDE),
        compiler_params=params(),
        name="upstream_first",
    )(pos, own, mate, weight)


def up_second(pos, part, far, far_mate, weight):
    def kernel(pos_ref, part_ref, g0, g1, w_ref, own_ref, oth_ref, acc):
        @pl.when(pl.program_id(0) == 0)
        def _():
            acc[...] = part_ref[...] + dot(g0[...], w_ref[...])

        @pl.when(pl.program_id(0) == 1)
        def _():
            acc[...] += dot(g1[...], w_ref[...])
            xl = pos_ref[1]
            own_ref[...] = acc[:, pl.ds(pl.multiple_of(xl * GROUP, GROUP), GROUP)].astype(LOW)
            oth_ref[...] = acc[:, pl.ds(pl.multiple_of((1 - xl) * GROUP, GROUP), GROUP)].astype(LOW)

    full = pl.BlockSpec((CHUNK, 1024), lambda r, pos: (0, 0))
    half = pl.BlockSpec((CHUNK, GROUP), lambda r, pos: (0, 0))
    return pl.pallas_call(
        kernel,
        grid_spec=pltpu.PrefetchScalarGridSpec(
            num_scalar_prefetch=1,
            grid=(2,),
            in_specs=[
                full,
                full,
                full,
                pl.BlockSpec((1024, 1024), lambda r, pos: (jnp.bitwise_xor(pos[0], 2 + r), 0)),
            ],
            out_specs=[half, half],
            scratch_shapes=[pltpu.VMEM((CHUNK, 1024), WIDE)],
        ),
        out_shape=[jax.ShapeDtypeStruct((CHUNK, GROUP), LOW)] * 2,
        compiler_params=params(),
        name="upstream_second",
    )(pos, part, far, far_mate, weight)


def stack_rows(dst, blocks, step):
    for o in range(2):
        for dy in range(NY):
            for h in range(RATIO):
                start = (dy % 2) * GROUP + h * CHUNK
                dst[o * 2 + dy // 2, start : start + CHUNK, :] = blocks[dy][
                    o * step : o * step + CHUNK, h * HEAD : (h + 1) * HEAD
                ]


def key_chunk(xl, z, o, d):
    plane = lax.rem(z + d, NZ)
    if o == 0:
        return xl * 4 + plane // 2
    return (1 - xl) * 4 + (NZ - 1 - plane) // 2


def count_row(ref, o):
    at = o * PIECE + CHUNK
    return ref[at : at + 16, :HEAD].astype(WIDE)[:1]


def fill_low(low_s, q, kv):
    zeros = sum(count_row(ref, o) for ref in kv for o in range(2))
    tok = lax.broadcasted_iota(jnp.int32, (1, CHUNK), 1).astype(WIDE)
    for o in range(2):
        for dy in range(NY):
            low = jnp.where(tok >= count_row(q[dy], o), zeros, 0.0)
            for h in range(RATIO):
                start = (dy % 2) * GROUP + h * CHUNK
                pair = o * 2 + dy // 2
                low_s[pair : pair + 1, start : start + CHUNK] = low


def row_limits(cls, pair, xl, z, y, low_s):
    o = pair // 2
    h = jnp.where(o == 0, xl, 1 - xl)
    plane = jnp.where(o == 0, z, NZ - 1 - z)
    dy0 = (pair % 2) * 2
    y0 = lax.rem(y + dy0, NY)
    y1 = lax.rem(y + dy0 + 1, NY)
    parity = lax.rem(plane + cls, 2)
    full = h * (KEYS // 2) + ((plane + 1 - parity) // 2) * CHUNK
    if cls == 0:
        lane = lax.broadcasted_iota(jnp.int32, (1, ROWS), 1)
        off = jnp.where(lane < GROUP, y0, y1) * CHUNK + jnp.bitwise_and(lane, CHUNK - 1)
        high = full + jnp.clip(off - y * CHUNK + 1, 0, CHUNK)
        top = full + jnp.where(jnp.maximum(y0, y1) >= y, CHUNK, 0)
    else:
        high = jnp.full((1, ROWS), full, jnp.int32)
        top = full
    low_f = low_s[pl.ds(pair, 1), :]
    low = low_f.astype(jnp.int32)
    t_low = jnp.min(low_f).astype(jnp.int32) // KT
    t_high = (top + KT - 1) // KT
    return low, high, t_low, t_high


def masked_scores(k, q, t, low, high):
    s = dot(k, q, NT) * C2
    kk = t * KT + lax.broadcasted_iota(jnp.int32, (KT, ROWS), 0)
    return jnp.where((kk >= low) & (kk < high), s, NEG)


def forward(cls, scalars, q_blocks, kv_views):
    def kernel(sc, *refs):
        q = refs[0:4]
        kv = refs[4:8]
        o_ref, ml_ref, qs, kc, vt, low_s = refs[8:]
        xl, z, y = sc[0], sc[1], sc[2]
        stack_rows(qs, q, PIECE)
        fill_low(low_s, q, kv)
        for i in range(4):
            for o in range(2):
                at = key_chunk(xl, z, o, 2 * i + cls)
                rows = slice(o * PIECE, o * PIECE + CHUNK)
                kc[at] = kv[i][rows, :HEAD]
                vt[at, :HEAD, :] = kv[i][rows, HEAD:].T
                vt[at, HEAD:, :] = jnp.ones((16, CHUNK), LOW)

        def one_pair(pair, _):
            low, high, t_low, t_high = row_limits(cls, pair, xl, z, y, low_s)
            o_ref[pair] = jnp.zeros((HEAD + 16, ROWS), WIDE)
            qp = qs[pair]

            def tile(t, top):
                k = kc[pl.ds(2 * t, 2)].reshape(KT, HEAD)
                s = masked_scores(k, qp, t, low, high)
                new = jnp.maximum(top, jnp.max(s, axis=0, keepdims=True))
                p = jnp.exp2(s - new).astype(LOW)
                v = jnp.concatenate([vt[2 * t], vt[2 * t + 1]], axis=1)
                o_ref[pair] = o_ref[pair] * jnp.exp2(top - new) + dot(v, p)
                return new

            top = lax.fori_loop(t_low, t_high, tile, jnp.full((1, ROWS), NEG, WIDE))
            ml_ref[pl.ds(pair, 1), :] = top
            return 0

        lax.fori_loop(0, PAIRS, one_pair, 0)
        for pair in range(PAIRS):
            ml_ref[PAIRS + pair : PAIRS + pair + 1, :] = o_ref[pair, HEAD : HEAD + 1, :]

    return pl.pallas_call(
        kernel,
        grid=(1,),
        in_specs=[sspec()] + [vspec()] * 4 + [view_spec(i) for _, i in kv_views],
        out_specs=[vspec()] * 2,
        out_shape=[
            jax.ShapeDtypeStruct((PAIRS, HEAD + 16, ROWS), WIDE),
            jax.ShapeDtypeStruct((2 * PAIRS, ROWS), WIDE),
        ],
        scratch_shapes=[
            pltpu.VMEM((PAIRS, ROWS, HEAD), LOW),
            pltpu.VMEM((NZ, CHUNK, HEAD), LOW),
            pltpu.VMEM((NZ, HEAD + 16, CHUNK), LOW),
            pltpu.VMEM((PAIRS, ROWS), WIDE),
        ],
        compiler_params=params(),
        cost_estimate=pl.CostEstimate(
            flops=4 * 10**9, bytes_accessed=4 * 2**20, transcendentals=2 * 2**20
        ),
        name="forward%d" % cls,
    )(scalars, *q_blocks, *[a for a, _ in kv_views])


def view_spec(i):
    return pl.BlockSpec((2 * PIECE, 2 * HEAD), lambda s: (i, 0))


def weighted(parts, u_blocks):
    def kernel(o0, ml0, o1, ml1, *refs):
        u = refs[0:4]
        out_ref = refs[4]
        top = jnp.maximum(ml0[:PAIRS], ml1[:PAIRS])
        f0 = jnp.exp2(ml0[:PAIRS] - top)
        f1 = jnp.exp2(ml1[:PAIRS] - top)
        out_ref[:PAIRS, :] = top
        out_ref[PAIRS : 2 * PAIRS, :] = f0 * ml0[PAIRS:] + f1 * ml1[PAIRS:]
        for o in range(2):
            for dy in range(NY):
                pair = o * 2 + dy // 2
                for h in range(RATIO):
                    start = (dy % 2) * GROUP + h * CHUNK
                    at = slice(start, start + CHUNK)
                    ut = u[dy][o * CHUNK : (o + 1) * CHUNK, h * HEAD : (h + 1) * HEAD]
                    ut = ut.astype(WIDE).T
                    one = jnp.sum(ut * o0[pair, :HEAD, at], axis=0, keepdims=True)
                    two = jnp.sum(ut * o1[pair, :HEAD, at], axis=0, keepdims=True)
                    out_ref[2 * PAIRS + pair : 2 * PAIRS + pair + 1, at] = (
                        f0[pair : pair + 1, at] * one + f1[pair : pair + 1, at] * two
                    )

    return pl.pallas_call(
        kernel,
        in_specs=[vspec()] * 8,
        out_specs=vspec(),
        out_shape=jax.ShapeDtypeStruct((3 * PAIRS, ROWS), WIDE),
        compiler_params=params(),
        name="weighted",
    )(*parts[0], *parts[1], *u_blocks)


def backward(cls, scalars, stats, q_blocks, u_blocks, kv_views, dq_before):
    last = dq_before is not None

    def kernel(sc, *refs):
        st = refs[0:4]
        q = refs[4:8]
        u = refs[8:12]
        kv = refs[12:16]
        refs = refs[16:]
        if last:
            before, refs = refs[0], refs[1:]
            dq_out, dkv_out, refs = refs[0:4], refs[4:8], refs[8:]
        else:
            dq_out, dkv_out, refs = refs[0:1], refs[1:3], refs[3:]
        qs, us, kc, vc, kt, dk, dv, al, lse_s, delta_s, low_s = refs[:11]
        dqt = refs[11] if last else dq_out[0]
        xl, z, y = sc[0], sc[1], sc[2]
        stack_rows(qs, q, PIECE)
        stack_rows(us, u, CHUNK)
        fill_low(low_s, q, kv)
        for i in range(4):
            for o in range(2):
                at = key_chunk(xl, z, o, 2 * i + cls)
                rows = slice(o * PIECE, o * PIECE + CHUNK)
                key = kv[i][rows, :HEAD]
                kc[at] = key
                vc[at] = kv[i][rows, HEAD:]
                kt[at] = key.T
        dk[...] = jnp.zeros(dk.shape, WIDE)
        dv[...] = jnp.zeros(dv.shape, WIDE)
        dqt[...] = before[...] if last else jnp.zeros(dqt.shape, WIDE)

        for i in range(NY):
            for row in range(0, 3 * PAIRS, 2):
                for dy in range(NY):
                    e = (dy - i) % NY
                    to, frm = (dy % 2) * GROUP, (e % 2) * GROUP
                    al[i, row + dy // 2 : row + dy // 2 + 1, to : to + GROUP] = st[i][
                        row + e // 2 : row + e // 2 + 1, frm : frm + GROUP
                    ]
        tops = [al[i, :PAIRS] for i in range(NY)]
        top = functools.reduce(jnp.maximum, tops)
        factors = [jnp.exp2(t - top) for t in tops]
        mass = sum(f * al[i, PAIRS : 2 * PAIRS] for i, f in enumerate(factors))
        share = sum(f * al[i, 2 * PAIRS :] for i, f in enumerate(factors))
        lse_s[...] = top + jnp.log2(mass)
        delta_s[...] = share / mass

        def one_pair(pair, _):
            low, high, t_low, t_high = row_limits(cls, pair, xl, z, y, low_s)
            lse = lse_s[pl.ds(pair, 1), :]
            delta = delta_s[pl.ds(pair, 1), :]
            qp = qs[pair]
            up = us[pair]

            def tile(t, _):
                k = kc[pl.ds(2 * t, 2)].reshape(KT, HEAD)
                v = vc[pl.ds(2 * t, 2)].reshape(KT, HEAD)
                p = jnp.exp2(masked_scores(k, qp, t, low, high) - lse)
                ds = (p * (dot(v, up, NT) - delta)).astype(LOW)
                p = p.astype(LOW)
                dv[pl.ds(2 * t, 2)] += dot(p, up).reshape(2, CHUNK, HEAD)
                dk[pl.ds(2 * t, 2)] += dot(ds, qp).reshape(2, CHUNK, HEAD)
                kt_tile = jnp.concatenate([kt[2 * t], kt[2 * t + 1]], axis=1)
                dqt[pair] += dot(kt_tile, ds)
                return 0

            lax.fori_loop(t_low, t_high, tile, 0)
            return 0

        lax.fori_loop(0, PAIRS, one_pair, 0)

        def write(out, first, d):
            for o in range(2):
                at = key_chunk(xl, z, o, d)
                rows = slice(first + o * CHUNK, first + (o + 1) * CHUNK)
                out[rows, :HEAD] = (dk[at] * SCALE).astype(out.dtype)
                out[rows, HEAD:] = dv[at].astype(out.dtype)

        if last:
            for i in range(4):
                write(dkv_out[i], 0, 2 * i)
            for dy in range(NY):
                for o in range(2):
                    for h in range(RATIO):
                        start = (dy % 2) * GROUP + h * CHUNK
                        part = dqt[o * 2 + dy // 2, :, start : start + CHUNK].T * SCALE
                        dq_out[dy][
                            o * CHUNK : (o + 1) * CHUNK, h * HEAD : (h + 1) * HEAD
                        ] = part.astype(dq_out[dy].dtype)
        else:
            write(dkv_out[0], 0, 1)
            write(dkv_out[0], 2 * CHUNK, 3)
            write(dkv_out[1], 0, 7)
            write(dkv_out[1], 2 * CHUNK, 5)

    dq_state = jax.ShapeDtypeStruct((PAIRS, HEAD, ROWS), WIDE)
    if last:
        out_shape = [
            jax.ShapeDtypeStruct((2 * CHUNK, GROUP), WIDE if dy == 0 else LOW)
            for dy in range(NY)
        ] + [
            jax.ShapeDtypeStruct((2 * CHUNK, 2 * HEAD), LOW if i == 2 else WIDE)
            for i in range(4)
        ]
    else:
        out_shape = [dq_state] + [jax.ShapeDtypeStruct((4 * CHUNK, 2 * HEAD), LOW)] * 2
    state = [dq_before] if last else []
    return pl.pallas_call(
        kernel,
        grid=(1,),
        in_specs=[sspec()]
        + [vspec()] * 12
        + [view_spec(i) for _, i in kv_views]
        + [vspec()] * len(state),
        out_specs=[vspec()] * len(out_shape),
        out_shape=out_shape,
        scratch_shapes=[
            pltpu.VMEM((PAIRS, ROWS, HEAD), LOW),
            pltpu.VMEM((PAIRS, ROWS, HEAD), LOW),
            pltpu.VMEM((NZ, CHUNK, HEAD), LOW),
            pltpu.VMEM((NZ, CHUNK, HEAD), LOW),
            pltpu.VMEM((NZ, HEAD, CHUNK), LOW),
            pltpu.VMEM((NZ, CHUNK, HEAD), WIDE),
            pltpu.VMEM((NZ, CHUNK, HEAD), WIDE),
            pltpu.VMEM((NY, 3 * PAIRS, ROWS), WIDE),
            pltpu.VMEM((PAIRS, ROWS), WIDE),
            pltpu.VMEM((PAIRS, ROWS), WIDE),
            pltpu.VMEM((PAIRS, ROWS), WIDE),
        ]
        + ([pltpu.VMEM((PAIRS, HEAD, ROWS), WIDE)] if last else []),
        compiler_params=params(),
        cost_estimate=pl.CostEstimate(
            flops=8 * 10**9, bytes_accessed=6 * 2**20, transcendentals=2 * 2**20
        ),
        name="backward%d" % cls,
    )(scalars, *stats, *q_blocks, *u_blocks, *[a for a, _ in kv_views], *state)


def shift(x, axis, size, d):
    return lax.ppermute(x, axis, [(i, (i - d) % size) for i in range(size)])


def swap(x):
    last = XL * NZ - 1
    return lax.ppermute(x, ("xl", "z"), [(i, last - i) for i in range(last + 1)])


def per_device(queries, keys, values, grad_out, out_weight, segments):
    xl, z, y = lax.axis_index("xl"), lax.axis_index("z"), lax.axis_index("y")
    tp = lax.axis_index("xh") * 2 + lax.axis_index("core")

    def part(x, group, width):
        return lax.dynamic_slice_in_dim(x, group * width, width, 1)

    count = jnp.sum((segments == 0).astype(WIDE)).astype(LOW)

    def key_value(group):
        both = jnp.concatenate([part(keys, group, HEAD), part(values, group, HEAD)], axis=1)
        return jnp.concatenate([both, jnp.full((16, 2 * HEAD), count, LOW)], axis=0)

    def query(group):
        return jnp.concatenate([part(queries, group, GROUP), jnp.full((16, GROUP), count, LOW)], axis=0)

    pos = jnp.stack([tp, xl]).astype(jnp.int32)
    scalars = jnp.stack([xl, z, y]).astype(jnp.int32)
    kv_in = swap(key_value(1 - xl))
    q_in = swap(query(1 - xl))
    far = shift(grad_out, "xh", 2, 1)
    mate = shift(grad_out, "core", 2, 1)

    def along_y(x):
        return [x] + [shift(x, "y", NY, d) for d in (1, 2, 3)]

    kv = jnp.concatenate([key_value(xl), kv_in], axis=0)
    kv_up2 = shift(kv, "z", NZ, 2)
    kv_down2 = shift(kv, "z", NZ, -2)
    kv_4 = shift(kv, "z", NZ, 4)
    q_blocks = along_y(jnp.concatenate([query(xl), q_in], axis=0))
    kv_up = shift(jnp.concatenate([kv, kv_up2], axis=0), "z", NZ, 1)
    kv_down = shift(jnp.concatenate([kv, kv_down2], axis=0), "z", NZ, -1)
    even = [(kv, 0), (kv_up2, 0), (kv_4, 0), (kv_down2, 0)]
    odd = [(kv_up, 0), (kv_up, 1), (kv_down, 1), (kv_down, 0)]

    u_part = up_first(pos, grad_out, mate, out_weight)
    far_mate = shift(far, "core", 2, 1)
    u_own, u_oth = up_second(pos, u_part, far, far_mate, out_weight)
    u_blocks = along_y(jnp.concatenate([u_own, swap(u_oth)], axis=0))

    parts = [forward(0, scalars, q_blocks, even), forward(1, scalars, q_blocks, odd)]
    stats = along_y(weighted(parts, u_blocks))
    dq_state, bundle_up, bundle_down = backward(
        1, scalars, stats, q_blocks, u_blocks, odd, None
    )
    got_up = shift(bundle_up, "z", NZ, -1)
    got_down = shift(bundle_down, "z", NZ, 1)
    *dq, dkv, dkv_up2, dkv_4, dkv_down2 = backward(
        0, scalars, stats, q_blocks, u_blocks, even, dq_state
    )

    near, further = slice(0, 2 * CHUNK), slice(2 * CHUNK, None)
    dkv = dkv + got_up[near].astype(WIDE) + got_down[near].astype(WIDE)
    up2 = (dkv_up2 + got_up[further].astype(WIDE)).astype(LOW)
    down2 = (dkv_down2 + got_down[further].astype(WIDE)).astype(LOW)
    for g in (
        shift(dkv_4, "z", NZ, 4),
        shift(up2, "z", NZ, -2),
        shift(down2, "z", NZ, 2),
    ):
        dkv = dkv + g.astype(WIDE)

    dq_sum = dq[0]
    for d in (1, 2, 3):
        dq_sum = dq_sum + shift(dq[d], "y", NY, -d).astype(WIDE)

    dq_back = swap(dq_sum[CHUNK:].astype(LOW))
    dkv_back = swap(dkv[CHUNK:].astype(LOW))
    dq_own = dq_sum[:CHUNK].astype(LOW)
    dkv_own = dkv[:CHUNK].astype(LOW)

    def join(a, c):
        return jnp.where(
            xl == 0, jnp.concatenate([a, c], axis=1), jnp.concatenate([c, a], axis=1)
        )

    return (
        join(dq_own, dq_back),
        join(dkv_own[:, :HEAD], dkv_back[:, :HEAD]),
        join(dkv_own[:, HEAD:], dkv_back[:, HEAD:]),
    )


def solution(mesh):
    fine = Mesh(mesh.devices.reshape(XL, NZ, NY, 2, 2), ("xl", "z", "y", "xh", "core"))
    ctx, tp = ("xl", "z", "y"), ("xh", "core")
    in_specs = (P(ctx, tp), P(ctx, tp), P(ctx, tp), P(ctx, tp), P(None, tp), P(ctx))
    out_specs = (P(ctx, tp), P(ctx, tp), P(ctx, tp))
    return jax.shard_map(
        per_device, mesh=fine, in_specs=in_specs, out_specs=out_specs, check_vma=False
    )
```

```python
import functools
import math

import jax
import jax.numpy as jnp
from jax import lax
from jax.experimental import pallas as pl
from jax.experimental.pallas import tpu as pltpu
from jax.sharding import Mesh, PartitionSpec as P

HEAD = 128
RATIO = 4
CHUNK = 128
XL, NZ, NY = 2, 8, 4
PIECE = CHUNK + 16
KEYS = NZ * CHUNK
KT = 256
GROUP = RATIO * HEAD
DP = 4
ROWS = DP * GROUP
BLOCKS = 2 * NY // DP
SCALE = HEAD**-0.5
C2 = SCALE * math.log2(math.e)
NEG = -1e30
WIDE = jnp.float32
LOW = jnp.bfloat16
NT = (((1,), (1,)), ((), ()))
NN = (((1,), (0,)), ((), ()))
MIB = 1024 * 1024


def dot(a, b, dims=NN):
    return lax.dot_general(a, b, dims, preferred_element_type=WIDE)


def vspec():
    return pl.BlockSpec(memory_space=pltpu.VMEM)


def hspec():
    return pl.BlockSpec(memory_space=pltpu.HBM)


def sspec():
    return pl.BlockSpec(memory_space=pltpu.SMEM)


def params(mib):
    return pltpu.CompilerParams(vmem_limit_bytes=mib * MIB)


def prepare(scalars, queries, keys, values, segments):
    def kernel(sc, q_ref, k_ref, v_ref, seg_ref, q_own, q_oth, kv_own, kv_oth, seg, sems):
        xl = sc[0]
        top = pl.ds(0, CHUNK)
        copies = [pltpu.make_async_copy(seg_ref, seg, sems.at[0])]
        for i, (g, q, kv) in enumerate(((1 - xl, q_oth, kv_oth), (xl, q_own, kv_own))):
            at = pl.ds(pl.multiple_of(g * GROUP, GROUP), GROUP)
            copies.append(
                pltpu.make_async_copy(q_ref.at[:, at], q.at[top], sems.at[3 * i + 1])
            )
            at = pl.ds(pl.multiple_of(g * HEAD, HEAD), HEAD)
            for j, ref in enumerate((k_ref, v_ref)):
                copies.append(
                    pltpu.make_async_copy(
                        ref.at[:, at],
                        kv.at[top, pl.ds(j * HEAD, HEAD)],
                        sems.at[3 * i + 2 + j],
                    )
                )
        for copy in copies:
            copy.start()
        copies[0].wait()
        count = jnp.sum(jnp.where(seg[...] == 0, 1.0, 0.0), axis=1, keepdims=True)
        count = jnp.broadcast_to(count, (16, HEAD)).astype(LOW)
        for q, kv in ((q_own, kv_own), (q_oth, kv_oth)):
            q[CHUNK:, :] = jnp.concatenate([count] * RATIO, axis=1)
            kv[CHUNK:, :] = jnp.concatenate([count] * 2, axis=1)
        for copy in copies[1:]:
            copy.wait()

    return pl.pallas_call(
        kernel,
        in_specs=[sspec()] + [hspec()] * 4,
        out_specs=[vspec()] * 4,
        out_shape=[jax.ShapeDtypeStruct((PIECE, GROUP), LOW)] * 2
        + [jax.ShapeDtypeStruct((PIECE, 2 * HEAD), LOW)] * 2,
        scratch_shapes=[pltpu.VMEM((1, CHUNK), jnp.int32), pltpu.SemaphoreType.DMA((7,))],
        compiler_params=params(8),
        name="prepare",
    )(scalars, queries, keys, values, segments.reshape(1, CHUNK))


def upstream(scalars, grad, weight):
    parts, rows, depth = grad.shape
    width = weight.shape[1]

    def kernel(sc, g_hbm, w_hbm, own_ref, oth_ref, g_ref, w_ref, acc, sems):
        xl = sc[0]
        copies = [pltpu.make_async_copy(g_hbm, g_ref, sems.at[parts])]
        for i in range(parts):
            at = pl.ds(i * depth, depth)
            copies.append(pltpu.make_async_copy(w_hbm.at[at], w_ref.at[at], sems.at[i]))
        for copy in copies:
            copy.start()
        copies[0].wait()
        for i in range(parts):
            copies[i + 1].wait()
            term = dot(g_ref[i], w_ref[i * depth : (i + 1) * depth, :])
            acc[...] = term if i == 0 else acc[...] + term
        for g, out in ((1 - xl, oth_ref), (xl, own_ref)):
            at = pl.ds(pl.multiple_of(g * GROUP, GROUP), GROUP)
            out[...] = acc[:, at].astype(LOW)

    return pl.pallas_call(
        kernel,
        in_specs=[sspec(), hspec(), hspec()],
        out_specs=[vspec()] * 2,
        out_shape=[jax.ShapeDtypeStruct((rows, GROUP), LOW)] * 2,
        scratch_shapes=[
            pltpu.VMEM(grad.shape, LOW),
            pltpu.VMEM(weight.shape, LOW),
            pltpu.VMEM((rows, width), WIDE),
            pltpu.SemaphoreType.DMA((parts + 1,)),
        ],
        compiler_params=params(56),
        cost_estimate=pl.CostEstimate(
            flops=2 * rows * parts * depth * width,
            bytes_accessed=2 * parts * depth * (rows + width),
            transcendentals=0,
        ),
        name="upstream",
    )(scalars, grad, weight)


def place(o, dy):
    return o * (NY // DP) + dy // DP, (dy % DP) * GROUP


def stack_rows(dst, blocks, step):
    for o in range(2):
        for dy in range(NY):
            block, first = place(o, dy)
            for h in range(RATIO):
                start = first + h * CHUNK
                dst[block, start : start + CHUNK, :] = blocks[dy][
                    o * step : o * step + CHUNK, h * HEAD : (h + 1) * HEAD
                ]


def key_chunk(xl, z, o, d):
    plane = lax.rem(z + d, NZ)
    if o == 0:
        return xl * 4 + plane // 2
    return (1 - xl) * 4 + (NZ - 1 - plane) // 2


def count_row(ref, first):
    return ref[first + CHUNK : first + PIECE, :HEAD].astype(WIDE)[:1]


def fill_low(low_s, q, views):
    zeros = sum(count_row(ref, first + o * PIECE) for ref, first in views for o in range(2))
    tok = lax.broadcasted_iota(jnp.int32, (1, CHUNK), 1).astype(WIDE)
    for o in range(2):
        for dy in range(NY):
            low = jnp.where(tok >= count_row(q[dy], o * PIECE), zeros, 0.0)
            block, first = place(o, dy)
            for h in range(RATIO):
                start = first + h * CHUNK
                low_s[block : block + 1, start : start + CHUNK] = low


def limits(cls, block, xl, z, y, low_s):
    o = block // (NY // DP)
    h = jnp.where(o == 0, xl, 1 - xl)
    plane = jnp.where(o == 0, z, NZ - 1 - z)
    dy0 = lax.rem(block, NY // DP) * DP
    ys = [lax.rem(y + dy0 + i, NY) for i in range(DP)]
    parity = lax.rem(plane + cls, 2)
    full = h * (KEYS // 2) + ((plane + 1 - parity) // 2) * CHUNK
    if cls == 0:
        lane = lax.broadcasted_iota(jnp.int32, (1, ROWS), 1)
        yy = jnp.full((1, ROWS), ys[-1], jnp.int32)
        for i in reversed(range(DP - 1)):
            yy = jnp.where(lane < (i + 1) * GROUP, ys[i], yy)
        off = (yy - y) * CHUNK + jnp.bitwise_and(lane, CHUNK - 1)
        high = full + jnp.clip(off + 1, 0, CHUNK)
        top = full + jnp.where(functools.reduce(jnp.maximum, ys) >= y, CHUNK, 0)
    else:
        high = jnp.full((1, ROWS), full, jnp.int32)
        top = full
    low_f = low_s[pl.ds(block, 1), :]
    low = low_f.astype(jnp.int32)
    t_low = jnp.min(low_f).astype(jnp.int32) // KT
    t_high = (top + KT - 1) // KT
    return low, high, t_low, t_high, jnp.max(low_f).astype(jnp.int32), full


def over_tiles(lim, body):
    low, high, t_low, t_high, max_low, full = lim

    def mask(t, s):
        kk = t * KT + lax.broadcasted_iota(jnp.int32, (KT, ROWS), 0)
        return jnp.where((kk >= low) & (kk < high), s, NEG)

    def step(t, _):
        inside = (t * KT >= max_low) & ((t + 1) * KT <= full)

        @pl.when(inside)
        def _():
            body(t, lambda s: s)

        @pl.when(jnp.logical_not(inside))
        def _():
            body(t, functools.partial(mask, t))

        return 0

    lax.fori_loop(t_low, t_high, step, 0)


def forward(scalars, q_blocks, arrays, views):
    def kernel(sc, *refs):
        q = refs[0:4]
        kv = refs[4 : 4 + len(arrays)]
        o_ref, ml_ref, qs, kc, vt, low_s = refs[4 + len(arrays) :]
        xl, z, y = sc[0], sc[1], sc[2]
        stack_rows(qs, q, PIECE)
        for cls in range(2):
            here = [(kv[a], first) for a, first in views[cls]]
            fill_low(low_s.at[cls], q, here)
            for i, (ref, first) in enumerate(here):
                for o in range(2):
                    at = key_chunk(xl, z, o, 2 * i + cls)
                    rows = slice(first + o * PIECE, first + o * PIECE + CHUNK)
                    kc[cls, at] = ref[rows, :HEAD]
                    vt[cls, at, :HEAD, :] = ref[rows, HEAD:].T
                    vt[cls, at, HEAD:, :] = jnp.ones((16, CHUNK), LOW)

        def one_block(block, _):
            qp = qs[block]
            o_ref[block] = jnp.zeros((HEAD + 16, ROWS), WIDE)
            ml_ref[pl.ds(block, 1), :] = jnp.full((1, ROWS), NEG, WIDE)
            for cls in range(2):

                def tile(t, mask):
                    k = kc[cls, pl.ds(2 * t, 2)].reshape(KT, HEAD)
                    s = mask(dot(k, qp, NT) * C2)
                    old = ml_ref[pl.ds(block, 1), :]
                    new = jnp.maximum(old, jnp.max(s, axis=0, keepdims=True))
                    p = jnp.exp2(s - new).astype(LOW)
                    v = jnp.concatenate([vt[cls, 2 * t], vt[cls, 2 * t + 1]], axis=1)
                    o_ref[block] = o_ref[block] * jnp.exp2(old - new) + dot(v, p)
                    ml_ref[pl.ds(block, 1), :] = new

                over_tiles(limits(cls, block, xl, z, y, low_s.at[cls]), tile)
            return 0

        lax.fori_loop(0, BLOCKS, one_block, 0)
        for block in range(BLOCKS):
            ml_ref[BLOCKS + block : BLOCKS + block + 1, :] = o_ref[block, HEAD : HEAD + 1, :]

    return pl.pallas_call(
        kernel,
        in_specs=[sspec()] + [vspec()] * (4 + len(arrays)),
        out_specs=[vspec()] * 2,
        out_shape=[
            jax.ShapeDtypeStruct((BLOCKS, HEAD + 16, ROWS), WIDE),
            jax.ShapeDtypeStruct((2 * BLOCKS, ROWS), WIDE),
        ],
        scratch_shapes=[
            pltpu.VMEM((BLOCKS, ROWS, HEAD), LOW),
            pltpu.VMEM((2, NZ, CHUNK, HEAD), LOW),
            pltpu.VMEM((2, NZ, HEAD + 16, CHUNK), LOW),
            pltpu.VMEM((2, BLOCKS, ROWS), WIDE),
        ],
        compiler_params=params(32),
        cost_estimate=pl.CostEstimate(
            flops=8 * 10**9, bytes_accessed=4 * 2**20, transcendentals=2 * 2**20
        ),
        name="forward",
    )(scalars, *q_blocks, *arrays)


def weighted(o_part, ml, u_blocks):
    def kernel(o_ref, ml_ref, *refs):
        u = refs[0:4]
        out_ref = refs[4]
        out_ref[: 2 * BLOCKS, :] = ml_ref[...]
        for o in range(2):
            for dy in range(NY):
                block, first = place(o, dy)
                for h in range(RATIO):
                    at = slice(first + h * CHUNK, first + (h + 1) * CHUNK)
                    ut = u[dy][o * CHUNK : (o + 1) * CHUNK, h * HEAD : (h + 1) * HEAD]
                    out_ref[2 * BLOCKS + block : 2 * BLOCKS + block + 1, at] = jnp.sum(
                        ut.astype(WIDE).T * o_ref[block, :HEAD, at], axis=0, keepdims=True
                    )

    return pl.pallas_call(
        kernel,
        in_specs=[vspec()] * 6,
        out_specs=vspec(),
        out_shape=jax.ShapeDtypeStruct((3 * BLOCKS, ROWS), WIDE),
        compiler_params=params(16),
        name="weighted",
    )(o_part, ml, *u_blocks)


def backward(cls, scalars, stats, q_blocks, u_blocks, arrays, views, dq_before):
    last = dq_before is not None
    n = len(arrays)

    def kernel(sc, *refs):
        st = refs[0:4]
        q = refs[4:8]
        u = refs[8:12]
        kv = refs[12 : 12 + n]
        refs = refs[12 + n :]
        if last:
            before, refs = refs[0], refs[1:]
            dq_out, dkv_out, refs = refs[0:4], refs[4:8], refs[8:]
        else:
            dq_out, dkv_out, refs = refs[0:1], refs[1:3], refs[3:]
        qs, us, kc, vc, kt, dk, dv, al, lse_s, delta_s, low_s = refs[:11]
        dqt = refs[11] if last else dq_out[0]
        xl, z, y = sc[0], sc[1], sc[2]
        here = [(kv[a], first) for a, first in views]
        stack_rows(qs, q, PIECE)
        stack_rows(us, u, CHUNK)
        fill_low(low_s, q, here)
        for i, (ref, first) in enumerate(here):
            for o in range(2):
                at = key_chunk(xl, z, o, 2 * i + cls)
                rows = slice(first + o * PIECE, first + o * PIECE + CHUNK)
                key = ref[rows, :HEAD]
                kc[at] = key
                vc[at] = ref[rows, HEAD:]
                kt[at] = key.T
        dk[...] = jnp.zeros(dk.shape, WIDE)
        dv[...] = jnp.zeros(dv.shape, WIDE)
        dqt[...] = before[...] if last else jnp.zeros(dqt.shape, WIDE)

        for i in range(NY):
            for kind in range(3):
                for o in range(2):
                    for dy in range(NY):
                        b, to = place(o, dy)
                        c, frm = place(o, (dy - i) % NY)
                        b, c = kind * BLOCKS + b, kind * BLOCKS + c
                        al[i, b : b + 1, to : to + GROUP] = st[i][c : c + 1, frm : frm + GROUP]
        tops = [al[i, :BLOCKS] for i in range(NY)]
        top = functools.reduce(jnp.maximum, tops)
        factors = [jnp.exp2(t - top) for t in tops]
        mass = sum(f * al[i, BLOCKS : 2 * BLOCKS] for i, f in enumerate(factors))
        share = sum(f * al[i, 2 * BLOCKS :] for i, f in enumerate(factors))
        lse_s[...] = top + jnp.log2(mass)
        delta_s[...] = share / mass

        def one_block(block, _):
            lse = lse_s[pl.ds(block, 1), :]
            delta = delta_s[pl.ds(block, 1), :]
            qp = qs[block]
            up = us[block]

            def tile(t, mask):
                k = kc[pl.ds(2 * t, 2)].reshape(KT, HEAD)
                v = vc[pl.ds(2 * t, 2)].reshape(KT, HEAD)
                p = jnp.exp2(mask(dot(k, qp, NT) * C2) - lse)
                ds = (p * (dot(v, up, NT) - delta)).astype(LOW)
                p = p.astype(LOW)
                dv[pl.ds(2 * t, 2)] += dot(p, up).reshape(2, CHUNK, HEAD)
                dk[pl.ds(2 * t, 2)] += dot(ds, qp).reshape(2, CHUNK, HEAD)
                kt_tile = jnp.concatenate([kt[2 * t], kt[2 * t + 1]], axis=1)
                dqt[block] += dot(kt_tile, ds)

            over_tiles(limits(cls, block, xl, z, y, low_s), tile)
            return 0

        lax.fori_loop(0, BLOCKS, one_block, 0)

        def write(out, first, d):
            for o in range(2):
                at = key_chunk(xl, z, o, d)
                rows = slice(first + o * CHUNK, first + (o + 1) * CHUNK)
                out[rows, :HEAD] = (dk[at] * SCALE).astype(out.dtype)
                out[rows, HEAD:] = dv[at].astype(out.dtype)

        if last:
            for i in range(4):
                write(dkv_out[i], 0, 2 * i)
            for dy in range(NY):
                for o in range(2):
                    block, first = place(o, dy)
                    for h in range(RATIO):
                        start = first + h * CHUNK
                        part = dqt[block, :, start : start + CHUNK].T * SCALE
                        dq_out[dy][
                            o * CHUNK : (o + 1) * CHUNK, h * HEAD : (h + 1) * HEAD
                        ] = part.astype(dq_out[dy].dtype)
        else:
            write(dkv_out[0], 0, 1)
            write(dkv_out[0], 2 * CHUNK, 3)
            write(dkv_out[1], 0, 7)
            write(dkv_out[1], 2 * CHUNK, 5)

    dq_state = jax.ShapeDtypeStruct((BLOCKS, HEAD, ROWS), WIDE)
    if last:
        out_shape = [
            jax.ShapeDtypeStruct((2 * CHUNK, GROUP), WIDE if dy == 0 else LOW)
            for dy in range(NY)
        ] + [
            jax.ShapeDtypeStruct((2 * CHUNK, 2 * HEAD), LOW if i == 2 else WIDE)
            for i in range(4)
        ]
    else:
        out_shape = [dq_state] + [jax.ShapeDtypeStruct((4 * CHUNK, 2 * HEAD), LOW)] * 2
    state = [dq_before] if last else []
    return pl.pallas_call(
        kernel,
        in_specs=[sspec()] + [vspec()] * (12 + n + len(state)),
        out_specs=[vspec()] * len(out_shape),
        out_shape=out_shape,
        scratch_shapes=[
            pltpu.VMEM((BLOCKS, ROWS, HEAD), LOW),
            pltpu.VMEM((BLOCKS, ROWS, HEAD), LOW),
            pltpu.VMEM((NZ, CHUNK, HEAD), LOW),
            pltpu.VMEM((NZ, CHUNK, HEAD), LOW),
            pltpu.VMEM((NZ, HEAD, CHUNK), LOW),
            pltpu.VMEM((NZ, CHUNK, HEAD), WIDE),
            pltpu.VMEM((NZ, CHUNK, HEAD), WIDE),
            pltpu.VMEM((NY, 3 * BLOCKS, ROWS), WIDE),
            pltpu.VMEM((BLOCKS, ROWS), WIDE),
            pltpu.VMEM((BLOCKS, ROWS), WIDE),
            pltpu.VMEM((BLOCKS, ROWS), WIDE),
        ]
        + ([pltpu.VMEM((BLOCKS, HEAD, ROWS), WIDE)] if last else []),
        compiler_params=params(32),
        cost_estimate=pl.CostEstimate(
            flops=8 * 10**9, bytes_accessed=6 * 2**20, transcendentals=2 * 2**20
        ),
        name="backward%d" % cls,
    )(scalars, *stats, *q_blocks, *u_blocks, *arrays, *state)


def settle(dq, dq_got, dkv, dkv_got):
    def kernel(*refs):
        dq_ref, a, b, c, dkv_ref, d, e, f, keep, send = refs
        for out, first in ((keep, 0), (send, CHUNK)):
            rows = slice(first, first + CHUNK)
            total = dq_ref[rows, :]
            for g in (a, b, c):
                total += g[rows, :].astype(WIDE)
            out[:, :GROUP] = total.astype(LOW)
            total = dkv_ref[rows, :]
            for g in (d, e, f):
                total += g[rows, :].astype(WIDE)
            out[:, GROUP:] = total.astype(LOW)

    return pl.pallas_call(
        kernel,
        in_specs=[vspec()] * 8,
        out_specs=[vspec()] * 2,
        out_shape=[jax.ShapeDtypeStruct((CHUNK, GROUP + 2 * HEAD), LOW)] * 2,
        compiler_params=params(8),
        name="settle",
    )(dq, *dq_got, dkv, *dkv_got)


def join(scalars, keep, back):
    def kernel(sc, keep_ref, back_ref, q_ref, k_ref, v_ref):
        xl = sc[0]
        for g, ref in ((xl, keep_ref), (1 - xl, back_ref)):
            q_ref[:, pl.ds(pl.multiple_of(g * GROUP, GROUP), GROUP)] = ref[:, :GROUP]
            at = pl.ds(pl.multiple_of(g * HEAD, HEAD), HEAD)
            k_ref[:, at] = ref[:, GROUP : GROUP + HEAD]
            v_ref[:, at] = ref[:, GROUP + HEAD :]

    return pl.pallas_call(
        kernel,
        in_specs=[sspec(), vspec(), vspec()],
        out_specs=[vspec()] * 3,
        out_shape=[
            jax.ShapeDtypeStruct((CHUNK, 2 * GROUP), LOW),
            jax.ShapeDtypeStruct((CHUNK, 2 * HEAD), LOW),
            jax.ShapeDtypeStruct((CHUNK, 2 * HEAD), LOW),
        ],
        compiler_params=params(8),
        name="join",
    )(scalars, keep, back)


def shift(x, axis, size, d):
    return lax.ppermute(x, axis, [(i, (i - d) % size) for i in range(size)])


def swap(x):
    last = XL * NZ - 1
    return lax.ppermute(x, ("xl", "z"), [(i, last - i) for i in range(last + 1)])


def along_y(x):
    return [x] + [shift(x, "y", NY, d) for d in (1, 2, 3)]


def per_device(queries, keys, values, grad_out, out_weight, segments):
    xl, z, y = lax.axis_index("xl"), lax.axis_index("z"), lax.axis_index("y")
    scalars = jnp.stack([xl, z, y]).astype(jnp.int32)

    grad = lax.all_gather(grad_out, ("xh", "core"))
    q_own, q_oth, kv_own, kv_oth = prepare(scalars, queries, keys, values, segments)
    kv_in = swap(kv_oth)
    q_in = swap(q_oth)

    kv = jnp.concatenate([kv_own, kv_in], axis=0)
    kv_up2 = shift(kv, "z", NZ, 2)
    kv_down2 = shift(kv, "z", NZ, -2)
    kv_4 = shift(kv, "z", NZ, 4)
    q_blocks = along_y(jnp.concatenate([q_own, q_in], axis=0))
    kv_up = shift(jnp.concatenate([kv, kv_up2], axis=0), "z", NZ, 1)
    kv_down = shift(jnp.concatenate([kv, kv_down2], axis=0), "z", NZ, -1)
    even = [kv, kv_up2, kv_4, kv_down2]
    odd = [kv_up, kv_down]
    second = 2 * PIECE
    even_views = [(i, 0) for i in range(4)]
    odd_views = [(0, 0), (0, second), (1, second), (1, 0)]

    grad, q_blocks = lax.optimization_barrier((grad, q_blocks))
    u_own, u_oth = upstream(scalars, grad, out_weight)
    u_blocks = along_y(jnp.concatenate([u_own, swap(u_oth)], axis=0))

    o_part, ml = forward(
        scalars, q_blocks, even + odd, [even_views, [(4 + a, first) for a, first in odd_views]]
    )
    stats = along_y(weighted(o_part, ml, u_blocks))
    dq_state, bundle_up, bundle_down = backward(
        1, scalars, stats, q_blocks, u_blocks, odd, odd_views, None
    )
    got_up = shift(bundle_up, "z", NZ, -1)
    got_down = shift(bundle_down, "z", NZ, 1)
    *dq, dkv, dkv_up2, dkv_4, dkv_down2 = backward(
        0, scalars, stats, q_blocks, u_blocks, even, even_views, dq_state
    )

    near, further = slice(0, 2 * CHUNK), slice(2 * CHUNK, None)
    dkv = dkv + got_up[near].astype(WIDE) + got_down[near].astype(WIDE)
    up2 = (dkv_up2 + got_up[further].astype(WIDE)).astype(LOW)
    down2 = (dkv_down2 + got_down[further].astype(WIDE)).astype(LOW)
    dq, up2, down2 = lax.optimization_barrier((dq, up2, down2))
    dkv_got = [
        shift(dkv_4, "z", NZ, 4),
        shift(up2, "z", NZ, -2),
        shift(down2, "z", NZ, 2),
    ]
    dq_got = [shift(dq[d], "y", NY, -d) for d in (1, 2, 3)]
    keep, send = settle(dq[0], dq_got, dkv, dkv_got)
    return join(scalars, keep, swap(send))


def solution(mesh):
    fine = Mesh(mesh.devices.reshape(XL, NZ, NY, 2, 2), ("xl", "z", "y", "xh", "core"))
    ctx, tp = ("xl", "z", "y"), ("xh", "core")
    in_specs = (P(ctx, tp), P(ctx, tp), P(ctx, tp), P(ctx, tp), P(None, tp), P(ctx))
    out_specs = (P(ctx, tp), P(ctx, tp), P(ctx, tp))
    return jax.shard_map(
        per_device, mesh=fine, in_specs=in_specs, out_specs=out_specs, check_vma=False
    )
```

```python
import functools
import math

import jax
import jax.numpy as jnp
from jax import lax
from jax.experimental import pallas as pl
from jax.experimental.pallas import tpu as pltpu
from jax.sharding import Mesh, PartitionSpec as P

HEAD = 128
RATIO = 4
CHUNK = 128
XL, NZ, NY = 2, 8, 4
PIECE = CHUNK + 16
KEYS = NZ * CHUNK
KT = 256
GROUP = RATIO * HEAD
DP = 4
ROWS = DP * GROUP
BLOCKS = 2 * NY // DP
SCALE = HEAD**-0.5
C2 = SCALE * math.log2(math.e)
NEG = -1e30
WIDE = jnp.float32
LOW = jnp.bfloat16
NT = (((1,), (1,)), ((), ()))
NN = (((1,), (0,)), ((), ()))
MIB = 1024 * 1024


def dot(a, b, dims=NN):
    return lax.dot_general(a, b, dims, preferred_element_type=WIDE)


def vspec():
    return pl.BlockSpec(memory_space=pltpu.VMEM)


def hspec():
    return pl.BlockSpec(memory_space=pltpu.HBM)


def sspec():
    return pl.BlockSpec(memory_space=pltpu.SMEM)


def params(mib):
    return pltpu.CompilerParams(vmem_limit_bytes=mib * MIB)


def prepare(scalars, queries, keys, values, segments):
    def kernel(sc, q_ref, k_ref, v_ref, seg_ref, q_own, q_oth, kv_own, kv_oth, seg, sems):
        xl = sc[0]
        top = pl.ds(0, CHUNK)
        copies = [pltpu.make_async_copy(seg_ref, seg, sems.at[0])]
        for i, (g, q, kv) in enumerate(((1 - xl, q_oth, kv_oth), (xl, q_own, kv_own))):
            at = pl.ds(pl.multiple_of(g * GROUP, GROUP), GROUP)
            copies.append(
                pltpu.make_async_copy(q_ref.at[:, at], q.at[top], sems.at[3 * i + 1])
            )
            at = pl.ds(pl.multiple_of(g * HEAD, HEAD), HEAD)
            for j, ref in enumerate((k_ref, v_ref)):
                copies.append(
                    pltpu.make_async_copy(
                        ref.at[:, at],
                        kv.at[top, pl.ds(j * HEAD, HEAD)],
                        sems.at[3 * i + 2 + j],
                    )
                )
        for copy in copies:
            copy.start()
        copies[0].wait()
        count = jnp.sum(jnp.where(seg[...] == 0, 1.0, 0.0), axis=1, keepdims=True)
        count = jnp.broadcast_to(count, (16, HEAD)).astype(LOW)
        for q, kv in ((q_own, kv_own), (q_oth, kv_oth)):
            q[CHUNK:, :] = jnp.concatenate([count] * RATIO, axis=1)
            kv[CHUNK:, :] = jnp.concatenate([count] * 2, axis=1)
        for copy in copies[1:]:
            copy.wait()

    return pl.pallas_call(
        kernel,
        in_specs=[sspec()] + [hspec()] * 4,
        out_specs=[vspec()] * 4,
        out_shape=[jax.ShapeDtypeStruct((PIECE, GROUP), LOW)] * 2
        + [jax.ShapeDtypeStruct((PIECE, 2 * HEAD), LOW)] * 2,
        scratch_shapes=[pltpu.VMEM((1, CHUNK), jnp.int32), pltpu.SemaphoreType.DMA((7,))],
        compiler_params=params(60),
        name="prepare",
    )(scalars, queries, keys, values, segments.reshape(1, CHUNK))


def upstream(scalars, grads, weight, before):
    rows, depth = grads[0].shape
    width = weight.shape[1]
    n = len(grads)
    last = before is not None
    first = n if last else 0

    def kernel(sc, *refs):
        gs, refs = refs[:n], refs[n:]
        if last:
            acc_in, refs = refs[0], refs[1:]
        w_hbm, refs = refs[0], refs[1:]
        if last:
            own_ref, oth_ref, w_ref, sems, acc = refs
        else:
            acc, w_ref, sems = refs
        xl, tp = sc[0], sc[3]
        copies = []
        for i in range(n):
            start = pl.multiple_of(jnp.bitwise_xor(tp, first + i) * depth, depth)
            copies.append(
                pltpu.make_async_copy(w_hbm.at[pl.ds(start, depth)], w_ref.at[i], sems.at[i])
            )
        for copy in copies:
            copy.start()
        for i in range(n):
            copies[i].wait()
            term = dot(gs[i][...], w_ref[i])
            if i == 0:
                acc[...] = acc_in[...] + term if last else term
            else:
                acc[...] += term
        if last:
            for g, out in ((1 - xl, oth_ref), (xl, own_ref)):
                at = pl.ds(pl.multiple_of(g * GROUP, GROUP), GROUP)
                out[...] = acc[:, at].astype(LOW)

    state = [before] if last else []
    half = jax.ShapeDtypeStruct((rows, GROUP), LOW)
    whole = jax.ShapeDtypeStruct((rows, width), WIDE)
    return pl.pallas_call(
        kernel,
        in_specs=[sspec()] + [vspec()] * (n + len(state)) + [hspec()],
        out_specs=[vspec()] * 2 if last else vspec(),
        out_shape=[half] * 2 if last else whole,
        scratch_shapes=[
            pltpu.VMEM((n, depth, width), LOW),
            pltpu.SemaphoreType.DMA((n,)),
        ]
        + ([pltpu.VMEM((rows, width), WIDE)] if last else []),
        compiler_params=params(57),
        cost_estimate=pl.CostEstimate(
            flops=2 * rows * n * depth * width,
            bytes_accessed=2 * n * depth * (rows + width),
            transcendentals=0,
        ),
        name="upstream%d" % first,
    )(scalars, *grads, *state, weight)


def place(o, dy):
    return o * (NY // DP) + dy // DP, (dy % DP) * GROUP


def stack_rows(dst, blocks, step):
    for o in range(2):
        for dy in range(NY):
            block, first = place(o, dy)
            for h in range(RATIO):
                start = first + h * CHUNK
                dst[block, start : start + CHUNK, :] = blocks[dy][
                    o * step : o * step + CHUNK, h * HEAD : (h + 1) * HEAD
                ]


def key_chunk(xl, z, o, d):
    half = xl if o == 0 else 1 - xl
    return half * 4 + lax.rem(z + d, NZ) // 2


def count_row(ref, first):
    return ref[first + CHUNK : first + PIECE, :HEAD].astype(WIDE)[:1]


def fill_low(low_s, q, views):
    zeros = sum(count_row(ref, first + o * PIECE) for ref, first in views for o in range(2))
    tok = lax.broadcasted_iota(jnp.int32, (1, CHUNK), 1).astype(WIDE)
    for o in range(2):
        for dy in range(NY):
            low = jnp.where(tok >= count_row(q[dy], o * PIECE), zeros, 0.0)
            block, first = place(o, dy)
            for h in range(RATIO):
                start = first + h * CHUNK
                low_s[block : block + 1, start : start + CHUNK] = low


def limits(cls, block, xl, z, y, low_s):
    o = block // (NY // DP)
    h = jnp.where(o == 0, xl, 1 - xl)
    plane = z
    dy0 = lax.rem(block, NY // DP) * DP
    ys = [lax.rem(y + dy0 + i, NY) for i in range(DP)]
    parity = lax.rem(plane + cls, 2)
    full = h * (KEYS // 2) + ((plane + 1 - parity) // 2) * CHUNK
    if cls == 0:
        lane = lax.broadcasted_iota(jnp.int32, (1, ROWS), 1)
        yy = jnp.full((1, ROWS), ys[-1], jnp.int32)
        for i in reversed(range(DP - 1)):
            yy = jnp.where(lane < (i + 1) * GROUP, ys[i], yy)
        off = (yy - y) * CHUNK + jnp.bitwise_and(lane, CHUNK - 1)
        high = full + jnp.clip(off + 1, 0, CHUNK)
        top = full + jnp.where(functools.reduce(jnp.maximum, ys) >= y, CHUNK, 0)
    else:
        high = jnp.full((1, ROWS), full, jnp.int32)
        top = full
    low_f = low_s[pl.ds(block, 1), :]
    low = low_f.astype(jnp.int32)
    t_low = jnp.min(low_f).astype(jnp.int32) // KT
    t_high = (top + KT - 1) // KT
    return low, high, t_low, t_high, jnp.max(low_f).astype(jnp.int32), full


def over_tiles(lim, body):
    low, high, t_low, t_high, max_low, full = lim

    def mask(t, s):
        kk = t * KT + lax.broadcasted_iota(jnp.int32, (KT, ROWS), 0)
        return jnp.where((kk >= low) & (kk < high), s, NEG)

    def step(t, _):
        inside = (t * KT >= max_low) & ((t + 1) * KT <= full)

        @pl.when(inside)
        def _():
            body(t, lambda s: s)

        @pl.when(jnp.logical_not(inside))
        def _():
            body(t, functools.partial(mask, t))

        return 0

    lax.fori_loop(t_low, t_high, step, 0)


def forward(scalars, q_blocks, arrays, views):
    def kernel(sc, *refs):
        q = refs[0:4]
        kv = refs[4 : 4 + len(arrays)]
        o_ref, ml_ref, qs, kc, vt, low_s = refs[4 + len(arrays) :]
        xl, z, y = sc[0], sc[1], sc[2]
        stack_rows(qs, q, PIECE)
        for cls in range(2):
            here = [(kv[a], first) for a, first in views[cls]]
            fill_low(low_s.at[cls], q, here)
            for i, (ref, first) in enumerate(here):
                for o in range(2):
                    at = key_chunk(xl, z, o, 2 * i + cls)
                    rows = slice(first + o * PIECE, first + o * PIECE + CHUNK)
                    kc[cls, at] = ref[rows, :HEAD]
                    vt[cls, at, :HEAD, :] = ref[rows, HEAD:].T
                    vt[cls, at, HEAD:, :] = jnp.ones((16, CHUNK), LOW)

        def one_block(block, _):
            qp = qs[block]
            o_ref[block] = jnp.zeros((HEAD + 16, ROWS), WIDE)
            ml_ref[pl.ds(block, 1), :] = jnp.full((1, ROWS), NEG, WIDE)
            for cls in range(2):

                def tile(t, mask):
                    k = kc[cls, pl.ds(2 * t, 2)].reshape(KT, HEAD)
                    s = mask(dot(k, qp, NT) * C2)
                    old = ml_ref[pl.ds(block, 1), :]
                    new = jnp.maximum(old, jnp.max(s, axis=0, keepdims=True))
                    p = jnp.exp2(s - new).astype(LOW)
                    v = jnp.concatenate([vt[cls, 2 * t], vt[cls, 2 * t + 1]], axis=1)
                    o_ref[block] = o_ref[block] * jnp.exp2(old - new) + dot(v, p)
                    ml_ref[pl.ds(block, 1), :] = new

                over_tiles(limits(cls, block, xl, z, y, low_s.at[cls]), tile)
            return 0

        lax.fori_loop(0, BLOCKS, one_block, 0)
        for block in range(BLOCKS):
            ml_ref[BLOCKS + block : BLOCKS + block + 1, :] = o_ref[block, HEAD : HEAD + 1, :]

    return pl.pallas_call(
        kernel,
        in_specs=[sspec()] + [vspec()] * (4 + len(arrays)),
        out_specs=[vspec()] * 2,
        out_shape=[
            jax.ShapeDtypeStruct((BLOCKS, HEAD + 16, ROWS), WIDE),
            jax.ShapeDtypeStruct((2 * BLOCKS, ROWS), WIDE),
        ],
        scratch_shapes=[
            pltpu.VMEM((BLOCKS, ROWS, HEAD), LOW),
            pltpu.VMEM((2, NZ, CHUNK, HEAD), LOW),
            pltpu.VMEM((2, NZ, HEAD + 16, CHUNK), LOW),
            pltpu.VMEM((2, BLOCKS, ROWS), WIDE),
        ],
        compiler_params=params(32),
        cost_estimate=pl.CostEstimate(
            flops=8 * 10**9, bytes_accessed=4 * 2**20, transcendentals=2 * 2**20
        ),
        name="forward",
    )(scalars, *q_blocks, *arrays)


def weighted(o_part, ml, u_blocks):
    def kernel(o_ref, ml_ref, *refs):
        u = refs[0:4]
        out_ref = refs[4]
        out_ref[: 2 * BLOCKS, :] = ml_ref[...]
        for o in range(2):
            for dy in range(NY):
                block, first = place(o, dy)
                for h in range(RATIO):
                    at = slice(first + h * CHUNK, first + (h + 1) * CHUNK)
                    ut = u[dy][o * CHUNK : (o + 1) * CHUNK, h * HEAD : (h + 1) * HEAD]
                    out_ref[2 * BLOCKS + block : 2 * BLOCKS + block + 1, at] = jnp.sum(
                        ut.astype(WIDE).T * o_ref[block, :HEAD, at], axis=0, keepdims=True
                    )

    return pl.pallas_call(
        kernel,
        in_specs=[vspec()] * 6,
        out_specs=vspec(),
        out_shape=jax.ShapeDtypeStruct((3 * BLOCKS, ROWS), WIDE),
        compiler_params=params(16),
        name="weighted",
    )(o_part, ml, *u_blocks)


def backward(cls, scalars, stats, q_blocks, u_blocks, arrays, views, dq_before):
    last = dq_before is not None
    n = len(arrays)

    def kernel(sc, *refs):
        st = refs[0:4]
        q = refs[4:8]
        u = refs[8:12]
        kv = refs[12 : 12 + n]
        refs = refs[12 + n :]
        if last:
            before, refs = refs[0], refs[1:]
            dq_out, dkv_out, refs = refs[0:4], refs[4:8], refs[8:]
        else:
            dq_out, dkv_out, refs = refs[0:1], refs[1:3], refs[3:]
        qs, us, kc, vc, kt, dk, dv, al, lse_s, delta_s, low_s = refs[:11]
        dqt = refs[11] if last else dq_out[0]
        xl, z, y = sc[0], sc[1], sc[2]
        here = [(kv[a], first) for a, first in views]
        stack_rows(qs, q, PIECE)
        stack_rows(us, u, CHUNK)
        fill_low(low_s, q, here)
        for i, (ref, first) in enumerate(here):
            for o in range(2):
                at = key_chunk(xl, z, o, 2 * i + cls)
                rows = slice(first + o * PIECE, first + o * PIECE + CHUNK)
                key = ref[rows, :HEAD]
                kc[at] = key
                vc[at] = ref[rows, HEAD:]
                kt[at] = key.T
        dk[...] = jnp.zeros(dk.shape, WIDE)
        dv[...] = jnp.zeros(dv.shape, WIDE)
        dqt[...] = before[...] if last else jnp.zeros(dqt.shape, WIDE)

        for i in range(NY):
            for kind in range(3):
                for o in range(2):
                    for dy in range(NY):
                        b, to = place(o, dy)
                        c, frm = place(o, (dy - i) % NY)
                        b, c = kind * BLOCKS + b, kind * BLOCKS + c
                        al[i, b : b + 1, to : to + GROUP] = st[i][c : c + 1, frm : frm + GROUP]
        tops = [al[i, :BLOCKS] for i in range(NY)]
        top = functools.reduce(jnp.maximum, tops)
        factors = [jnp.exp2(t - top) for t in tops]
        mass = sum(f * al[i, BLOCKS : 2 * BLOCKS] for i, f in enumerate(factors))
        share = sum(f * al[i, 2 * BLOCKS :] for i, f in enumerate(factors))
        lse_s[...] = top + jnp.log2(mass)
        delta_s[...] = share / mass

        def one_block(block, _):
            lse = lse_s[pl.ds(block, 1), :]
            delta = delta_s[pl.ds(block, 1), :]
            qp = qs[block]
            up = us[block]

            def tile(t, mask):
                k = kc[pl.ds(2 * t, 2)].reshape(KT, HEAD)
                v = vc[pl.ds(2 * t, 2)].reshape(KT, HEAD)
                p = jnp.exp2(mask(dot(k, qp, NT) * C2) - lse)
                ds = (p * (dot(v, up, NT) - delta)).astype(LOW)
                p = p.astype(LOW)
                dv[pl.ds(2 * t, 2)] += dot(p, up).reshape(2, CHUNK, HEAD)
                dk[pl.ds(2 * t, 2)] += dot(ds, qp).reshape(2, CHUNK, HEAD)
                kt_tile = jnp.concatenate([kt[2 * t], kt[2 * t + 1]], axis=1)
                dqt[block] += dot(kt_tile, ds)

            over_tiles(limits(cls, block, xl, z, y, low_s), tile)
            return 0

        lax.fori_loop(0, BLOCKS, one_block, 0)

        def write(out, first, d):
            for o in range(2):
                at = key_chunk(xl, z, o, d)
                rows = slice(first + o * CHUNK, first + (o + 1) * CHUNK)
                out[rows, :HEAD] = (dk[at] * SCALE).astype(out.dtype)
                out[rows, HEAD:] = dv[at].astype(out.dtype)

        if last:
            for i in range(4):
                write(dkv_out[i], 0, 2 * i)
            for dy in range(NY):
                for o in range(2):
                    block, first = place(o, dy)
                    for h in range(RATIO):
                        start = first + h * CHUNK
                        part = dqt[block, :, start : start + CHUNK].T * SCALE
                        dq_out[dy][
                            o * CHUNK : (o + 1) * CHUNK, h * HEAD : (h + 1) * HEAD
                        ] = part.astype(dq_out[dy].dtype)
        else:
            write(dkv_out[0], 0, 1)
            write(dkv_out[0], 2 * CHUNK, 3)
            write(dkv_out[1], 0, 7)
            write(dkv_out[1], 2 * CHUNK, 5)

    dq_state = jax.ShapeDtypeStruct((BLOCKS, HEAD, ROWS), WIDE)
    if last:
        out_shape = [
            jax.ShapeDtypeStruct((2 * CHUNK, GROUP), WIDE if dy == 0 else LOW)
            for dy in range(NY)
        ] + [
            jax.ShapeDtypeStruct((2 * CHUNK, 2 * HEAD), LOW if i == 2 else WIDE)
            for i in range(4)
        ]
    else:
        out_shape = [dq_state] + [jax.ShapeDtypeStruct((4 * CHUNK, 2 * HEAD), LOW)] * 2
    state = [dq_before] if last else []
    return pl.pallas_call(
        kernel,
        in_specs=[sspec()] + [vspec()] * (12 + n + len(state)),
        out_specs=[vspec()] * len(out_shape),
        out_shape=out_shape,
        scratch_shapes=[
            pltpu.VMEM((BLOCKS, ROWS, HEAD), LOW),
            pltpu.VMEM((BLOCKS, ROWS, HEAD), LOW),
            pltpu.VMEM((NZ, CHUNK, HEAD), LOW),
            pltpu.VMEM((NZ, CHUNK, HEAD), LOW),
            pltpu.VMEM((NZ, HEAD, CHUNK), LOW),
            pltpu.VMEM((NZ, CHUNK, HEAD), WIDE),
            pltpu.VMEM((NZ, CHUNK, HEAD), WIDE),
            pltpu.VMEM((NY, 3 * BLOCKS, ROWS), WIDE),
            pltpu.VMEM((BLOCKS, ROWS), WIDE),
            pltpu.VMEM((BLOCKS, ROWS), WIDE),
            pltpu.VMEM((BLOCKS, ROWS), WIDE),
        ]
        + ([pltpu.VMEM((BLOCKS, HEAD, ROWS), WIDE)] if last else []),
        compiler_params=params(32),
        cost_estimate=pl.CostEstimate(
            flops=8 * 10**9, bytes_accessed=6 * 2**20, transcendentals=2 * 2**20
        ),
        name="backward%d" % cls,
    )(scalars, *stats, *q_blocks, *u_blocks, *arrays, *state)


def settle(dq, dq_got, dkv, dkv_got):
    def kernel(*refs):
        dq_ref, a, b, c, dkv_ref, d, e, f, keep, send = refs
        for out, first in ((keep, 0), (send, CHUNK)):
            rows = slice(first, first + CHUNK)
            total = dq_ref[rows, :]
            for g in (a, b, c):
                total += g[rows, :].astype(WIDE)
            out[:, :GROUP] = total.astype(LOW)
            total = dkv_ref[rows, :]
            for g in (d, e, f):
                total += g[rows, :].astype(WIDE)
            out[:, GROUP:] = total.astype(LOW)

    return pl.pallas_call(
        kernel,
        in_specs=[vspec()] * 8,
        out_specs=[vspec()] * 2,
        out_shape=[jax.ShapeDtypeStruct((CHUNK, GROUP + 2 * HEAD), LOW)] * 2,
        compiler_params=params(8),
        name="settle",
    )(dq, *dq_got, dkv, *dkv_got)


def join(scalars, keep, back):
    def kernel(sc, keep_ref, back_ref, q_ref, k_ref, v_ref):
        xl = sc[0]
        for g, ref in ((xl, keep_ref), (1 - xl, back_ref)):
            q_ref[:, pl.ds(pl.multiple_of(g * GROUP, GROUP), GROUP)] = ref[:, :GROUP]
            at = pl.ds(pl.multiple_of(g * HEAD, HEAD), HEAD)
            k_ref[:, at] = ref[:, GROUP : GROUP + HEAD]
            v_ref[:, at] = ref[:, GROUP + HEAD :]

    return pl.pallas_call(
        kernel,
        in_specs=[sspec(), vspec(), vspec()],
        out_specs=[vspec()] * 3,
        out_shape=[
            jax.ShapeDtypeStruct((CHUNK, 2 * GROUP), LOW),
            jax.ShapeDtypeStruct((CHUNK, 2 * HEAD), LOW),
            jax.ShapeDtypeStruct((CHUNK, 2 * HEAD), LOW),
        ],
        compiler_params=params(8),
        name="join",
    )(scalars, keep, back)


def shift(x, axis, size, d):
    return lax.ppermute(x, axis, [(i, (i - d) % size) for i in range(size)])


def swap(x):
    return shift(x, "xl", XL, 1)


def along_y(x):
    return [x] + [shift(x, "y", NY, d) for d in (1, 2, 3)]


def per_device(queries, keys, values, grad_out, out_weight, segments):
    xl, z, y = lax.axis_index("xl"), lax.axis_index("z"), lax.axis_index("y")
    tp = lax.axis_index("xh") * 2 + lax.axis_index("core")
    scalars = jnp.stack([xl, z, y, tp]).astype(jnp.int32)

    far = shift(grad_out, "xh", 2, 1)
    mate = shift(grad_out, "core", 2, 1)
    q_own, q_oth, kv_own, kv_oth = prepare(scalars, queries, keys, values, segments)
    kv_in = swap(kv_oth)
    q_in = swap(q_oth)

    kv = jnp.concatenate([kv_own, kv_in], axis=0)
    kv_up2 = shift(kv, "z", NZ, 2)
    kv_down2 = shift(kv, "z", NZ, -2)
    kv_4 = shift(kv, "z", NZ, 4)
    q_blocks = along_y(jnp.concatenate([q_own, q_in], axis=0))
    kv_up = shift(jnp.concatenate([kv, kv_up2], axis=0), "z", NZ, 1)
    kv_down = shift(jnp.concatenate([kv, kv_down2], axis=0), "z", NZ, -1)
    even = [kv, kv_up2, kv_4, kv_down2]
    odd = [kv_up, kv_down]
    second = 2 * PIECE
    even_views = [(i, 0) for i in range(4)]
    odd_views = [(0, 0), (0, second), (1, second), (1, 0)]

    part = upstream(scalars, [grad_out, mate], out_weight, None)
    far_mate = shift(far, "core", 2, 1)
    u_own, u_oth = upstream(scalars, [far, far_mate], out_weight, part)
    u_blocks = along_y(jnp.concatenate([u_own, swap(u_oth)], axis=0))

    o_part, ml = forward(
        scalars, q_blocks, even + odd, [even_views, [(4 + a, first) for a, first in odd_views]]
    )
    stats = along_y(weighted(o_part, ml, u_blocks))
    dq_state, bundle_up, bundle_down = backward(
        1, scalars, stats, q_blocks, u_blocks, odd, odd_views, None
    )
    got_up = shift(bundle_up, "z", NZ, -1)
    got_down = shift(bundle_down, "z", NZ, 1)
    *dq, dkv, dkv_up2, dkv_4, dkv_down2 = backward(
        0, scalars, stats, q_blocks, u_blocks, even, even_views, dq_state
    )

    near, further = slice(0, 2 * CHUNK), slice(2 * CHUNK, None)
    dkv = dkv + got_up[near].astype(WIDE) + got_down[near].astype(WIDE)
    up2 = (dkv_up2 + got_up[further].astype(WIDE)).astype(LOW)
    down2 = (dkv_down2 + got_down[further].astype(WIDE)).astype(LOW)
    dq, up2, down2 = lax.optimization_barrier((dq, up2, down2))
    dkv_got = [
        shift(dkv_4, "z", NZ, 4),
        shift(up2, "z", NZ, -2),
        shift(down2, "z", NZ, 2),
    ]
    dq_got = [shift(dq[d], "y", NY, -d) for d in (1, 2, 3)]
    keep, send = settle(dq[0], dq_got, dkv, dkv_got)
    return join(scalars, keep, swap(send))


def solution(mesh):
    fine = Mesh(mesh.devices.reshape(XL, NZ, NY, 2, 2), ("xl", "z", "y", "xh", "core"))
    ctx, tp = ("xl", "z", "y"), ("xh", "core")
    in_specs = (P(ctx, tp), P(ctx, tp), P(ctx, tp), P(ctx, tp), P(None, tp), P(ctx))
    out_specs = (P(ctx, tp), P(ctx, tp), P(ctx, tp))
    return jax.shard_map(
        per_device, mesh=fine, in_specs=in_specs, out_specs=out_specs, check_vma=False
    )
```

```python
import functools
import math

import jax
import jax.numpy as jnp
from jax import lax
from jax.experimental import pallas as pl
from jax.experimental.pallas import tpu as pltpu
from jax.sharding import Mesh, PartitionSpec as P

HEAD = 128
RATIO = 4
CHUNK = 128
XL, NZ, NY = 2, 8, 4
PIECE = CHUNK + 16
KEYS = NZ * CHUNK
KT = 256
GROUP = RATIO * HEAD
DP = 4
ROWS = DP * GROUP
BLOCKS = 2 * NY // DP
SCALE = HEAD**-0.5
C2 = SCALE * math.log2(math.e)
NEG = -1e30
WIDE = jnp.float32
LOW = jnp.bfloat16
NT = (((1,), (1,)), ((), ()))
NN = (((1,), (0,)), ((), ()))
MIB = 1024 * 1024


def dot(a, b, dims=NN):
    return lax.dot_general(a, b, dims, preferred_element_type=WIDE)


def vspec():
    return pl.BlockSpec(memory_space=pltpu.VMEM)


def hspec():
    return pl.BlockSpec(memory_space=pltpu.HBM)


def in_hbm(x):
    return pltpu.with_memory_space_constraint(x, pltpu.HBM)


def sspec():
    return pl.BlockSpec(memory_space=pltpu.SMEM)


def params(mib):
    return pltpu.CompilerParams(vmem_limit_bytes=mib * MIB)


def prepare(scalars, queries, keys, values, segments):
    def kernel(sc, q_ref, k_ref, v_ref, seg_ref, q_own, q_oth, kv_own, kv_oth, seg, sems):
        xl = sc[0]
        top = pl.ds(0, CHUNK)
        copies = [pltpu.make_async_copy(seg_ref, seg, sems.at[0])]
        for i, (g, q, kv) in enumerate(((1 - xl, q_oth, kv_oth), (xl, q_own, kv_own))):
            at = pl.ds(pl.multiple_of(g * GROUP, GROUP), GROUP)
            copies.append(
                pltpu.make_async_copy(q_ref.at[:, at], q.at[top], sems.at[3 * i + 1])
            )
            at = pl.ds(pl.multiple_of(g * HEAD, HEAD), HEAD)
            for j, ref in enumerate((k_ref, v_ref)):
                copies.append(
                    pltpu.make_async_copy(
                        ref.at[:, at],
                        kv.at[top, pl.ds(j * HEAD, HEAD)],
                        sems.at[3 * i + 2 + j],
                    )
                )
        for copy in copies:
            copy.start()
        copies[0].wait()
        count = jnp.sum(jnp.where(seg[...] == 0, 1.0, 0.0), axis=1, keepdims=True)
        count = jnp.broadcast_to(count, (16, HEAD)).astype(LOW)
        for q, kv in ((q_own, kv_own), (q_oth, kv_oth)):
            q[CHUNK:PIECE, :] = jnp.concatenate([count] * RATIO, axis=1)
            kv[CHUNK:PIECE, :] = jnp.concatenate([count] * 2, axis=1)
        for copy in copies[1:]:
            copy.wait()

    return pl.pallas_call(
        kernel,
        in_specs=[sspec()] + [hspec()] * 4,
        out_specs=[vspec()] * 4,
        out_shape=[
            jax.ShapeDtypeStruct((2 * PIECE, GROUP), LOW),
            jax.ShapeDtypeStruct((PIECE, GROUP), LOW),
            jax.ShapeDtypeStruct((2 * PIECE, 2 * HEAD), LOW),
            jax.ShapeDtypeStruct((PIECE, 2 * HEAD), LOW),
        ],
        scratch_shapes=[pltpu.VMEM((1, CHUNK), jnp.int32), pltpu.SemaphoreType.DMA((7,))],
        compiler_params=params(8),
        name="prepare",
    )(scalars, *[in_hbm(x) for x in (queries, keys, values, segments.reshape(1, CHUNK))])


def stage(weight, grad):
    def kernel(w_hbm, g_hbm, w_ref, g_ref, sems):
        copies = [
            pltpu.make_async_copy(w_hbm, w_ref, sems.at[0]),
            pltpu.make_async_copy(g_hbm, g_ref, sems.at[1]),
        ]
        for copy in copies:
            copy.start()
        for copy in copies:
            copy.wait()

    return pl.pallas_call(
        kernel,
        in_specs=[hspec()] * 2,
        out_specs=[vspec()] * 2,
        out_shape=[jax.ShapeDtypeStruct(x.shape, x.dtype) for x in (weight, grad)],
        scratch_shapes=[pltpu.SemaphoreType.DMA((2,))],
        compiler_params=params(12),
        name="stage",
    )(in_hbm(weight), in_hbm(grad))


def upstream(scalars, grads, weight):
    rows, depth = grads[0].shape
    width = weight.shape[1]

    def kernel(sc, *refs):
        gs = refs[:4]
        w_ref, own_ref, oth_ref, acc = refs[4:]
        xl, tp = sc[0], sc[3]
        for i in range(4):
            start = pl.multiple_of(jnp.bitwise_xor(tp, i) * depth, depth)
            term = dot(gs[i][...], w_ref[pl.ds(start, depth), :])
            acc[...] = term if i == 0 else acc[...] + term
        for g, out in ((1 - xl, oth_ref), (xl, own_ref)):
            at = pl.ds(pl.multiple_of(g * GROUP, GROUP), GROUP)
            out[:rows, :] = acc[:, at].astype(LOW)

    return pl.pallas_call(
        kernel,
        in_specs=[sspec()] + [vspec()] * 5,
        out_specs=[vspec()] * 2,
        out_shape=[
            jax.ShapeDtypeStruct((2 * rows, GROUP), LOW),
            jax.ShapeDtypeStruct((rows, GROUP), LOW),
        ],
        scratch_shapes=[pltpu.VMEM((rows, width), WIDE)],
        compiler_params=params(16),
        name="upstream",
    )(scalars, *grads, weight)


def place(o, dy):
    return o * (NY // DP) + dy // DP, (dy % DP) * GROUP


def stack_rows(dst, blocks, step):
    for o in range(2):
        for dy in range(NY):
            block, first = place(o, dy)
            for h in range(RATIO):
                start = first + h * CHUNK
                dst[block, start : start + CHUNK, :] = blocks[dy][
                    o * step : o * step + CHUNK, h * HEAD : (h + 1) * HEAD
                ]


def key_chunk(xl, z, o, d):
    half = xl if o == 0 else 1 - xl
    return half * 4 + lax.rem(z + d, NZ) // 2


def count_row(ref, first):
    return ref[first + CHUNK : first + PIECE, :HEAD].astype(WIDE)[:1]


def fill_low(low_s, q, views):
    zeros = sum(count_row(ref, first + o * PIECE) for ref, first in views for o in range(2))
    tok = lax.broadcasted_iota(jnp.int32, (1, CHUNK), 1).astype(WIDE)
    for o in range(2):
        for dy in range(NY):
            low = jnp.where(tok >= count_row(q[dy], o * PIECE), zeros, 0.0)
            block, first = place(o, dy)
            for h in range(RATIO):
                start = first + h * CHUNK
                low_s[block : block + 1, start : start + CHUNK] = low


def limits(cls, block, xl, z, y, low_s):
    o = block // (NY // DP)
    h = jnp.where(o == 0, xl, 1 - xl)
    plane = z
    dy0 = lax.rem(block, NY // DP) * DP
    ys = [lax.rem(y + dy0 + i, NY) for i in range(DP)]
    parity = lax.rem(plane + cls, 2)
    full = h * (KEYS // 2) + ((plane + 1 - parity) // 2) * CHUNK
    if cls == 0:
        lane = lax.broadcasted_iota(jnp.int32, (1, ROWS), 1)
        yy = jnp.full((1, ROWS), ys[-1], jnp.int32)
        for i in reversed(range(DP - 1)):
            yy = jnp.where(lane < (i + 1) * GROUP, ys[i], yy)
        off = (yy - y) * CHUNK + jnp.bitwise_and(lane, CHUNK - 1)
        high = full + jnp.clip(off + 1, 0, CHUNK)
        top = full + jnp.where(functools.reduce(jnp.maximum, ys) >= y, CHUNK, 0)
    else:
        high = jnp.full((1, ROWS), full, jnp.int32)
        top = full
    low_f = low_s[pl.ds(block, 1), :]
    low = low_f.astype(jnp.int32)
    t_low = jnp.min(low_f).astype(jnp.int32) // KT
    t_high = (top + KT - 1) // KT
    return low, high, t_low, t_high, jnp.max(low_f).astype(jnp.int32), full


def over_tiles(lim, body):
    low, high, t_low, t_high, max_low, full = lim

    def mask(t, s):
        kk = t * KT + lax.broadcasted_iota(jnp.int32, (KT, ROWS), 0)
        return jnp.where((kk >= low) & (kk < high), s, NEG)

    def step(t, _):
        inside = (t * KT >= max_low) & ((t + 1) * KT <= full)

        @pl.when(inside)
        def _():
            body(t, lambda s: s)

        @pl.when(jnp.logical_not(inside))
        def _():
            body(t, functools.partial(mask, t))

        return 0

    lax.fori_loop(t_low, t_high, step, 0)


def forward(scalars, q_blocks, arrays, views):
    def kernel(sc, *refs):
        q = refs[0:4]
        kv = refs[4 : 4 + len(arrays)]
        o_ref, ml_ref, qs, kc, vt, low_s = refs[4 + len(arrays) :]
        xl, z, y = sc[0], sc[1], sc[2]
        stack_rows(qs, q, PIECE)
        for cls in range(2):
            here = [(kv[a], first) for a, first in views[cls]]
            fill_low(low_s.at[cls], q, here)
            for i, (ref, first) in enumerate(here):
                for o in range(2):
                    at = key_chunk(xl, z, o, 2 * i + cls)
                    rows = slice(first + o * PIECE, first + o * PIECE + CHUNK)
                    kc[cls, at] = ref[rows, :HEAD]
                    vt[cls, at, :HEAD, :] = ref[rows, HEAD:].T
                    vt[cls, at, HEAD:, :] = jnp.ones((16, CHUNK), LOW)

        def one_block(block, _):
            qp = qs[block]
            o_ref[block] = jnp.zeros((HEAD + 16, ROWS), WIDE)
            ml_ref[pl.ds(block, 1), :] = jnp.full((1, ROWS), NEG, WIDE)
            for cls in range(2):

                def tile(t, mask):
                    k = kc[cls, pl.ds(2 * t, 2)].reshape(KT, HEAD)
                    s = mask(dot(k, qp, NT) * C2)
                    old = ml_ref[pl.ds(block, 1), :]
                    new = jnp.maximum(old, jnp.max(s, axis=0, keepdims=True))
                    p = jnp.exp2(s - new).astype(LOW)
                    v = jnp.concatenate([vt[cls, 2 * t], vt[cls, 2 * t + 1]], axis=1)
                    o_ref[block] = o_ref[block] * jnp.exp2(old - new) + dot(v, p)
                    ml_ref[pl.ds(block, 1), :] = new

                over_tiles(limits(cls, block, xl, z, y, low_s.at[cls]), tile)
            return 0

        lax.fori_loop(0, BLOCKS, one_block, 0)
        for block in range(BLOCKS):
            ml_ref[BLOCKS + block : BLOCKS + block + 1, :] = o_ref[block, HEAD : HEAD + 1, :]

    return pl.pallas_call(
        kernel,
        in_specs=[sspec()] + [vspec()] * (4 + len(arrays)),
        out_specs=[vspec()] * 2,
        out_shape=[
            jax.ShapeDtypeStruct((BLOCKS, HEAD + 16, ROWS), WIDE),
            jax.ShapeDtypeStruct((2 * BLOCKS, ROWS), WIDE),
        ],
        scratch_shapes=[
            pltpu.VMEM((BLOCKS, ROWS, HEAD), LOW),
            pltpu.VMEM((2, NZ, CHUNK, HEAD), LOW),
            pltpu.VMEM((2, NZ, HEAD + 16, CHUNK), LOW),
            pltpu.VMEM((2, BLOCKS, ROWS), WIDE),
        ],
        compiler_params=params(32),
        cost_estimate=pl.CostEstimate(
            flops=8 * 10**9, bytes_accessed=4 * 2**20, transcendentals=2 * 2**20
        ),
        name="forward",
    )(scalars, *q_blocks, *arrays)


def weighted(o_part, ml, u_blocks):
    def kernel(o_ref, ml_ref, *refs):
        u = refs[0:4]
        out_ref = refs[4]
        out_ref[: 2 * BLOCKS, :] = ml_ref[...]
        for o in range(2):
            for dy in range(NY):
                block, first = place(o, dy)
                for h in range(RATIO):
                    at = slice(first + h * CHUNK, first + (h + 1) * CHUNK)
                    ut = u[dy][o * CHUNK : (o + 1) * CHUNK, h * HEAD : (h + 1) * HEAD]
                    out_ref[2 * BLOCKS + block : 2 * BLOCKS + block + 1, at] = jnp.sum(
                        ut.astype(WIDE).T * o_ref[block, :HEAD, at], axis=0, keepdims=True
                    )

    return pl.pallas_call(
        kernel,
        in_specs=[vspec()] * 6,
        out_specs=vspec(),
        out_shape=jax.ShapeDtypeStruct((3 * BLOCKS, ROWS), WIDE),
        compiler_params=params(16),
        name="weighted",
    )(o_part, ml, *u_blocks)


def backward(cls, scalars, stats, q_blocks, u_blocks, arrays, views, dq_before):
    last = dq_before is not None
    n = len(arrays)

    def kernel(sc, *refs):
        st = refs[0:4]
        q = refs[4:8]
        u = refs[8:12]
        kv = refs[12 : 12 + n]
        refs = refs[12 + n :]
        if last:
            before, refs = refs[0], refs[1:]
            dq_out, dkv_out, refs = refs[0:4], refs[4:8], refs[8:]
        else:
            dq_out, dkv_out, refs = refs[0:1], refs[1:3], refs[3:]
        qs, us, kc, vc, kt, dk, dv, al, lse_s, delta_s, low_s = refs[:11]
        dqt = refs[11] if last else dq_out[0]
        xl, z, y = sc[0], sc[1], sc[2]
        here = [(kv[a], first) for a, first in views]
        stack_rows(qs, q, PIECE)
        stack_rows(us, u, CHUNK)
        fill_low(low_s, q, here)
        for i, (ref, first) in enumerate(here):
            for o in range(2):
                at = key_chunk(xl, z, o, 2 * i + cls)
                rows = slice(first + o * PIECE, first + o * PIECE + CHUNK)
                key = ref[rows, :HEAD]
                kc[at] = key
                vc[at] = ref[rows, HEAD:]
                kt[at] = key.T
        dk[...] = jnp.zeros(dk.shape, WIDE)
        dv[...] = jnp.zeros(dv.shape, WIDE)
        dqt[...] = before[...] if last else jnp.zeros(dqt.shape, WIDE)

        for i in range(NY):
            for kind in range(3):
                for o in range(2):
                    for dy in range(NY):
                        b, to = place(o, dy)
                        c, frm = place(o, (dy - i) % NY)
                        b, c = kind * BLOCKS + b, kind * BLOCKS + c
                        al[i, b : b + 1, to : to + GROUP] = st[i][c : c + 1, frm : frm + GROUP]
        tops = [al[i, :BLOCKS] for i in range(NY)]
        top = functools.reduce(jnp.maximum, tops)
        factors = [jnp.exp2(t - top) for t in tops]
        mass = sum(f * al[i, BLOCKS : 2 * BLOCKS] for i, f in enumerate(factors))
        share = sum(f * al[i, 2 * BLOCKS :] for i, f in enumerate(factors))
        lse_s[...] = top + jnp.log2(mass)
        delta_s[...] = share / mass

        def one_block(block, _):
            lse = lse_s[pl.ds(block, 1), :]
            delta = delta_s[pl.ds(block, 1), :]
            qp = qs[block]
            up = us[block]

            def tile(t, mask):
                k = kc[pl.ds(2 * t, 2)].reshape(KT, HEAD)
                v = vc[pl.ds(2 * t, 2)].reshape(KT, HEAD)
                p = jnp.exp2(mask(dot(k, qp, NT) * C2) - lse)
                ds = (p * (dot(v, up, NT) - delta)).astype(LOW)
                p = p.astype(LOW)
                dv[pl.ds(2 * t, 2)] += dot(p, up).reshape(2, CHUNK, HEAD)
                dk[pl.ds(2 * t, 2)] += dot(ds, qp).reshape(2, CHUNK, HEAD)
                kt_tile = jnp.concatenate([kt[2 * t], kt[2 * t + 1]], axis=1)
                dqt[block] += dot(kt_tile, ds)

            over_tiles(limits(cls, block, xl, z, y, low_s), tile)
            return 0

        lax.fori_loop(0, BLOCKS, one_block, 0)

        def write(out, first, d):
            for o in range(2):
                at = key_chunk(xl, z, o, d)
                rows = slice(first + o * CHUNK, first + (o + 1) * CHUNK)
                out[rows, :HEAD] = (dk[at] * SCALE).astype(out.dtype)
                out[rows, HEAD:] = dv[at].astype(out.dtype)

        if last:
            for i in range(4):
                write(dkv_out[i], 0, 2 * i)
            for dy in range(NY):
                for o in range(2):
                    block, first = place(o, dy)
                    for h in range(RATIO):
                        start = first + h * CHUNK
                        part = dqt[block, :, start : start + CHUNK].T * SCALE
                        dq_out[dy][
                            o * CHUNK : (o + 1) * CHUNK, h * HEAD : (h + 1) * HEAD
                        ] = part.astype(dq_out[dy].dtype)
        else:
            write(dkv_out[0], 0, 1)
            write(dkv_out[0], 2 * CHUNK, 3)
            write(dkv_out[1], 0, 7)
            write(dkv_out[1], 2 * CHUNK, 5)

    dq_state = jax.ShapeDtypeStruct((BLOCKS, HEAD, ROWS), WIDE)
    if last:
        out_shape = [
            jax.ShapeDtypeStruct((2 * CHUNK, GROUP), WIDE if dy == 0 else LOW)
            for dy in range(NY)
        ] + [
            jax.ShapeDtypeStruct((2 * CHUNK, 2 * HEAD), LOW if i == 2 else WIDE)
            for i in range(4)
        ]
    else:
        out_shape = [dq_state] + [jax.ShapeDtypeStruct((4 * CHUNK, 2 * HEAD), LOW)] * 2
    state = [dq_before] if last else []
    return pl.pallas_call(
        kernel,
        in_specs=[sspec()] + [vspec()] * (12 + n + len(state)),
        out_specs=[vspec()] * len(out_shape),
        out_shape=out_shape,
        scratch_shapes=[
            pltpu.VMEM((BLOCKS, ROWS, HEAD), LOW),
            pltpu.VMEM((BLOCKS, ROWS, HEAD), LOW),
            pltpu.VMEM((NZ, CHUNK, HEAD), LOW),
            pltpu.VMEM((NZ, CHUNK, HEAD), LOW),
            pltpu.VMEM((NZ, HEAD, CHUNK), LOW),
            pltpu.VMEM((NZ, CHUNK, HEAD), WIDE),
            pltpu.VMEM((NZ, CHUNK, HEAD), WIDE),
            pltpu.VMEM((NY, 3 * BLOCKS, ROWS), WIDE),
            pltpu.VMEM((BLOCKS, ROWS), WIDE),
            pltpu.VMEM((BLOCKS, ROWS), WIDE),
            pltpu.VMEM((BLOCKS, ROWS), WIDE),
        ]
        + ([pltpu.VMEM((BLOCKS, HEAD, ROWS), WIDE)] if last else []),
        compiler_params=params(32),
        cost_estimate=pl.CostEstimate(
            flops=8 * 10**9, bytes_accessed=6 * 2**20, transcendentals=2 * 2**20
        ),
        name="backward%d" % cls,
    )(scalars, *stats, *q_blocks, *u_blocks, *arrays, *state)


def settle(dq, dq_got, dkv, dkv_got):
    def kernel(*refs):
        dq_ref, a, b, c, dkv_ref, d, e, f, keep, send = refs
        for out, first in ((keep, 0), (send, CHUNK)):
            rows = slice(first, first + CHUNK)
            total = dq_ref[rows, :]
            for g in (a, b, c):
                total += g[rows, :].astype(WIDE)
            out[:, :GROUP] = total.astype(LOW)
            total = dkv_ref[rows, :]
            for g in (d, e, f):
                total += g[rows, :].astype(WIDE)
            out[:, GROUP:] = total.astype(LOW)

    return pl.pallas_call(
        kernel,
        in_specs=[vspec()] * 8,
        out_specs=[vspec()] * 2,
        out_shape=[jax.ShapeDtypeStruct((CHUNK, GROUP + 2 * HEAD), LOW)] * 2,
        compiler_params=params(8),
        name="settle",
    )(dq, *dq_got, dkv, *dkv_got)


def join(scalars, keep, back):
    def kernel(sc, keep_ref, back_ref, q_ref, k_ref, v_ref):
        xl = sc[0]
        for g, ref in ((xl, keep_ref), (1 - xl, back_ref)):
            q_ref[:, pl.ds(pl.multiple_of(g * GROUP, GROUP), GROUP)] = ref[:, :GROUP]
            at = pl.ds(pl.multiple_of(g * HEAD, HEAD), HEAD)
            k_ref[:, at] = ref[:, GROUP : GROUP + HEAD]
            v_ref[:, at] = ref[:, GROUP + HEAD :]

    return pl.pallas_call(
        kernel,
        in_specs=[sspec(), vspec(), vspec()],
        out_specs=[vspec()] * 3,
        out_shape=[
            jax.ShapeDtypeStruct((CHUNK, 2 * GROUP), LOW),
            jax.ShapeDtypeStruct((CHUNK, 2 * HEAD), LOW),
            jax.ShapeDtypeStruct((CHUNK, 2 * HEAD), LOW),
        ],
        compiler_params=params(8),
        name="join",
    )(scalars, keep, back)


def shift(x, axis, size, d):
    return lax.ppermute(x, axis, [(i, (i - d) % size) for i in range(size)])


def swap(x):
    return shift(x, "xl", XL, 1)


def below(whole, x):
    return lax.dynamic_update_slice(whole, x, (whole.shape[0] - x.shape[0], 0))


def along_y(x):
    return [x] + [shift(x, "y", NY, d) for d in (1, 2, 3)]


def per_device(queries, keys, values, grad_out, out_weight, segments):
    xl, z, y = lax.axis_index("xl"), lax.axis_index("z"), lax.axis_index("y")
    tp = lax.axis_index("xh") * 2 + lax.axis_index("core")
    scalars = jnp.stack([xl, z, y, tp]).astype(jnp.int32)

    far = shift(grad_out, "xh", 2, 1)
    mate = shift(grad_out, "core", 2, 1)
    q_own, q_oth, kv_own, kv_oth = prepare(scalars, queries, keys, values, segments)
    kv_in = swap(kv_oth)
    q_in = swap(q_oth)

    kv = below(kv_own, kv_in)
    kv_up2 = shift(kv, "z", NZ, 2)
    kv_down2 = shift(kv, "z", NZ, -2)
    kv_4 = shift(kv, "z", NZ, 4)
    q_blocks = along_y(below(q_own, q_in))
    kv_up = shift(jnp.concatenate([kv, kv_up2], axis=0), "z", NZ, 1)
    kv_down = shift(jnp.concatenate([kv, kv_down2], axis=0), "z", NZ, -1)
    even = [kv, kv_up2, kv_4, kv_down2]
    odd = [kv_up, kv_down]
    second = 2 * PIECE
    even_views = [(i, 0) for i in range(4)]
    odd_views = [(0, 0), (0, second), (1, second), (1, 0)]

    relay, _ = lax.optimization_barrier((far, kv))
    far_mate = shift(relay, "core", 2, 1)
    weight, grad = stage(out_weight, grad_out)
    u_own, u_oth = upstream(scalars, [grad, mate, far, far_mate], weight)
    u_blocks = along_y(below(u_own, swap(u_oth)))

    o_part, ml = forward(
        scalars, q_blocks, even + odd, [even_views, [(4 + a, first) for a, first in odd_views]]
    )
    stats = along_y(weighted(o_part, ml, u_blocks))
    dq_state, bundle_up, bundle_down = backward(
        1, scalars, stats, q_blocks, u_blocks, odd, odd_views, None
    )
    got_up = shift(bundle_up, "z", NZ, -1)
    got_down = shift(bundle_down, "z", NZ, 1)
    *dq, dkv, dkv_up2, dkv_4, dkv_down2 = backward(
        0, scalars, stats, q_blocks, u_blocks, even, even_views, dq_state
    )

    near, further = slice(0, 2 * CHUNK), slice(2 * CHUNK, None)
    dkv = dkv + got_up[near].astype(WIDE) + got_down[near].astype(WIDE)
    up2 = (dkv_up2 + got_up[further].astype(WIDE)).astype(LOW)
    down2 = (dkv_down2 + got_down[further].astype(WIDE)).astype(LOW)
    dq, up2, down2 = lax.optimization_barrier((dq, up2, down2))
    dkv_got = [
        shift(dkv_4, "z", NZ, 4),
        shift(up2, "z", NZ, -2),
        shift(down2, "z", NZ, 2),
    ]
    dq_got = [shift(dq[d], "y", NY, -d) for d in (1, 2, 3)]
    keep, send = settle(dq[0], dq_got, dkv, dkv_got)
    return join(scalars, keep, swap(send))


def solution(mesh):
    fine = Mesh(mesh.devices.reshape(XL, NZ, NY, 2, 2), ("xl", "z", "y", "xh", "core"))
    ctx, tp = ("xl", "z", "y"), ("xh", "core")
    in_specs = (P(ctx, tp), P(ctx, tp), P(ctx, tp), P(ctx, tp), P(None, tp), P(ctx))
    out_specs = (P(ctx, tp), P(ctx, tp), P(ctx, tp))
    return jax.shard_map(
        per_device, mesh=fine, in_specs=in_specs, out_specs=out_specs, check_vma=False
    )
```

```python
import functools
import math

import jax
import jax.numpy as jnp
from jax import lax
from jax.experimental import pallas as pl
from jax.experimental.pallas import tpu as pltpu
from jax.sharding import Mesh, PartitionSpec as P

HEAD = 128
RATIO = 4
CHUNK = 128
XL, NZ, NY = 2, 8, 4
PIECE = CHUNK + 16
KEYS = NZ * CHUNK
KT = 256
GROUP = RATIO * HEAD
DP = 4
ROWS = DP * GROUP
BLOCKS = 2 * NY // DP
SCALE = HEAD**-0.5
C2 = SCALE * math.log2(math.e)
NEG = -1e30
WIDE = jnp.float32
LOW = jnp.bfloat16
NT = (((1,), (1,)), ((), ()))
NN = (((1,), (0,)), ((), ()))
MIB = 1024 * 1024


def dot(a, b, dims=NN):
    return lax.dot_general(a, b, dims, preferred_element_type=WIDE)


def vspec():
    return pl.BlockSpec(memory_space=pltpu.VMEM)


def hspec():
    return pl.BlockSpec(memory_space=pltpu.HBM)


def in_hbm(x):
    return pltpu.with_memory_space_constraint(x, pltpu.HBM)


def sspec():
    return pl.BlockSpec(memory_space=pltpu.SMEM)


def params(mib):
    return pltpu.CompilerParams(vmem_limit_bytes=mib * MIB)


def prepare(scalars, queries, keys, values, segments):
    def kernel(sc, q_ref, k_ref, v_ref, seg_ref, q_own, q_oth, kv_own, kv_oth, seg, sems):
        xl = sc[0]
        top = pl.ds(0, CHUNK)
        copies = [pltpu.make_async_copy(seg_ref, seg, sems.at[0])]
        for i, (g, q, kv) in enumerate(((1 - xl, q_oth, kv_oth), (xl, q_own, kv_own))):
            at = pl.ds(pl.multiple_of(g * GROUP, GROUP), GROUP)
            copies.append(
                pltpu.make_async_copy(q_ref.at[:, at], q.at[top], sems.at[3 * i + 1])
            )
            at = pl.ds(pl.multiple_of(g * HEAD, HEAD), HEAD)
            for j, ref in enumerate((k_ref, v_ref)):
                copies.append(
                    pltpu.make_async_copy(
                        ref.at[:, at],
                        kv.at[top, pl.ds(j * HEAD, HEAD)],
                        sems.at[3 * i + 2 + j],
                    )
                )
        for copy in copies:
            copy.start()
        copies[0].wait()
        count = jnp.sum(jnp.where(seg[...] == 0, 1.0, 0.0), axis=1, keepdims=True)
        count = jnp.broadcast_to(count, (16, HEAD)).astype(LOW)
        for q, kv in ((q_own, kv_own), (q_oth, kv_oth)):
            q[CHUNK:PIECE, :] = jnp.concatenate([count] * RATIO, axis=1)
            kv[CHUNK:PIECE, :] = jnp.concatenate([count] * 2, axis=1)
        for copy in copies[1:]:
            copy.wait()

    return pl.pallas_call(
        kernel,
        in_specs=[sspec()] + [hspec()] * 4,
        out_specs=[vspec()] * 4,
        out_shape=[
            jax.ShapeDtypeStruct((2 * PIECE, GROUP), LOW),
            jax.ShapeDtypeStruct((PIECE, GROUP), LOW),
            jax.ShapeDtypeStruct((2 * PIECE, 2 * HEAD), LOW),
            jax.ShapeDtypeStruct((PIECE, 2 * HEAD), LOW),
        ],
        scratch_shapes=[pltpu.VMEM((1, CHUNK), jnp.int32), pltpu.SemaphoreType.DMA((7,))],
        compiler_params=params(8),
        name="prepare",
    )(scalars, *[in_hbm(x) for x in (queries, keys, values, segments.reshape(1, CHUNK))])


def stage(weight, grad):
    def kernel(w_hbm, g_hbm, w_ref, g_ref, sems):
        copies = [
            pltpu.make_async_copy(w_hbm, w_ref, sems.at[0]),
            pltpu.make_async_copy(g_hbm, g_ref, sems.at[1]),
        ]
        for copy in copies:
            copy.start()
        for copy in copies:
            copy.wait()

    return pl.pallas_call(
        kernel,
        in_specs=[hspec()] * 2,
        out_specs=[vspec()] * 2,
        out_shape=[jax.ShapeDtypeStruct(x.shape, x.dtype) for x in (weight, grad)],
        scratch_shapes=[pltpu.SemaphoreType.DMA((2,))],
        compiler_params=params(12),
        cost_estimate=pl.CostEstimate(
            flops=0, bytes_accessed=4 * weight.size, transcendentals=0
        ),
        name="stage",
    )(in_hbm(weight), in_hbm(grad))


def upstream(scalars, grads, weight):
    rows, depth = grads[0].shape
    width = weight.shape[1]

    def kernel(sc, *refs):
        gs = refs[:4]
        w_ref, own_ref, oth_ref, acc = refs[4:]
        xl, tp = sc[0], sc[3]
        for i in range(4):
            start = pl.multiple_of(jnp.bitwise_xor(tp, i) * depth, depth)
            term = dot(gs[i][...], w_ref[pl.ds(start, depth), :])
            acc[...] = term if i == 0 else acc[...] + term
        for g, out in ((1 - xl, oth_ref), (xl, own_ref)):
            at = pl.ds(pl.multiple_of(g * GROUP, GROUP), GROUP)
            out[:rows, :] = acc[:, at].astype(LOW)

    return pl.pallas_call(
        kernel,
        in_specs=[sspec()] + [vspec()] * 5,
        out_specs=[vspec()] * 2,
        out_shape=[
            jax.ShapeDtypeStruct((2 * rows, GROUP), LOW),
            jax.ShapeDtypeStruct((rows, GROUP), LOW),
        ],
        scratch_shapes=[pltpu.VMEM((rows, width), WIDE)],
        compiler_params=params(16),
        name="upstream",
    )(scalars, *grads, weight)


DISTANCES = {None: tuple(range(NZ)), 0: (0, 2, 6), 1: (1, 3, 5, 7, 4)}


def place(o, dy):
    return o * (NY // DP) + dy // DP, (dy % DP) * GROUP


def stack_rows(dst, blocks, step):
    for o in range(2):
        for dy in range(NY):
            block, first = place(o, dy)
            for h in range(RATIO):
                start = first + h * CHUNK
                dst[block, start : start + CHUNK, :] = blocks[dy][
                    o * step : o * step + CHUNK, h * HEAD : (h + 1) * HEAD
                ]


def rank(cls, plane, z):
    if cls is None:
        return plane
    odd = (plane + 1 - lax.rem(z + 1, 2)) // 2
    fourth = jnp.where(lax.rem(z + 4, NZ) < plane, 1, 0)
    return odd + fourth if cls == 1 else plane - odd - fourth


def key_chunk(cls, xl, z, o, d):
    half = xl if o == 0 else 1 - xl
    return half * len(DISTANCES[cls]) + rank(cls, lax.rem(z + d, NZ), z)


def count_row(ref, first):
    return ref[first + CHUNK : first + PIECE, :HEAD].astype(WIDE)[:1]


def fill_low(low_s, q, views):
    zeros = sum(count_row(ref, first + o * PIECE) for ref, first in views for o in range(2))
    tok = lax.broadcasted_iota(jnp.int32, (1, CHUNK), 1).astype(WIDE)
    for o in range(2):
        for dy in range(NY):
            low = jnp.where(tok >= count_row(q[dy], o * PIECE), zeros, 0.0)
            block, first = place(o, dy)
            for h in range(RATIO):
                start = first + h * CHUNK
                low_s[block : block + 1, start : start + CHUNK] = low


def limits(cls, block, xl, z, y, low_s):
    o = block // (NY // DP)
    h = jnp.where(o == 0, xl, 1 - xl)
    plane = z
    dy0 = lax.rem(block, NY // DP) * DP
    ys = [lax.rem(y + dy0 + i, NY) for i in range(DP)]
    full = (h * len(DISTANCES[cls]) + rank(cls, plane, z)) * CHUNK
    if cls != 1:
        lane = lax.broadcasted_iota(jnp.int32, (1, ROWS), 1)
        yy = jnp.full((1, ROWS), ys[-1], jnp.int32)
        for i in reversed(range(DP - 1)):
            yy = jnp.where(lane < (i + 1) * GROUP, ys[i], yy)
        off = (yy - y) * CHUNK + jnp.bitwise_and(lane, CHUNK - 1)
        high = full + jnp.clip(off + 1, 0, CHUNK)
        top = full + jnp.where(functools.reduce(jnp.maximum, ys) >= y, CHUNK, 0)
    else:
        high = jnp.full((1, ROWS), full, jnp.int32)
        top = full
    low_f = low_s[pl.ds(block, 1), :]
    low = low_f.astype(jnp.int32)
    t_low = jnp.min(low_f).astype(jnp.int32) // KT
    t_high = (top + KT - 1) // KT
    return low, high, t_low, t_high, jnp.max(low_f).astype(jnp.int32), full


def over_tiles(lim, body):
    low, high, t_low, t_high, max_low, full = lim

    def mask(t, s):
        kk = t * KT + lax.broadcasted_iota(jnp.int32, (KT, ROWS), 0)
        return jnp.where((kk >= low) & (kk < high), s, NEG)

    def step(t, _):
        inside = (t * KT >= max_low) & ((t + 1) * KT <= full)

        @pl.when(inside)
        def _():
            body(t, lambda s: s)

        @pl.when(jnp.logical_not(inside))
        def _():
            body(t, functools.partial(mask, t))

        return 0

    lax.fori_loop(t_low, t_high, step, 0)


def forward(scalars, q_blocks, arrays, views):
    def kernel(sc, *refs):
        q = refs[0:4]
        kv = refs[4 : 4 + len(arrays)]
        o_ref, ml_ref, qs, kc, vt, low_s = refs[4 + len(arrays) :]
        xl, z, y = sc[0], sc[1], sc[2]
        stack_rows(qs, q, PIECE)
        here = [(kv[a], first) for a, first, _ in views]
        fill_low(low_s, q, here)
        for (ref, first), (_, _, d) in zip(here, views):
            for o in range(2):
                at = key_chunk(None, xl, z, o, d)
                rows = slice(first + o * PIECE, first + o * PIECE + CHUNK)
                kc[at] = ref[rows, :HEAD]
                vt[at, :HEAD, :] = ref[rows, HEAD:].T
                vt[at, HEAD:, :] = jnp.ones((16, CHUNK), LOW)

        def one_block(block, _):
            qp = qs[block]
            o_ref[block] = jnp.zeros((HEAD + 16, ROWS), WIDE)
            ml_ref[pl.ds(block, 1), :] = jnp.full((1, ROWS), NEG, WIDE)

            def tile(t, mask):
                k = kc[pl.ds(2 * t, 2)].reshape(KT, HEAD)
                s = mask(dot(k, qp, NT) * C2)
                old = ml_ref[pl.ds(block, 1), :]
                new = jnp.maximum(old, jnp.max(s, axis=0, keepdims=True))
                p = jnp.exp2(s - new).astype(LOW)
                v = jnp.concatenate([vt[2 * t], vt[2 * t + 1]], axis=1)
                o_ref[block] = o_ref[block] * jnp.exp2(old - new) + dot(v, p)
                ml_ref[pl.ds(block, 1), :] = new

            over_tiles(limits(None, block, xl, z, y, low_s), tile)
            return 0

        lax.fori_loop(0, BLOCKS, one_block, 0)
        for block in range(BLOCKS):
            ml_ref[BLOCKS + block : BLOCKS + block + 1, :] = o_ref[block, HEAD : HEAD + 1, :]

    return pl.pallas_call(
        kernel,
        in_specs=[sspec()] + [vspec()] * (4 + len(arrays)),
        out_specs=[vspec()] * 2,
        out_shape=[
            jax.ShapeDtypeStruct((BLOCKS, HEAD + 16, ROWS), WIDE),
            jax.ShapeDtypeStruct((2 * BLOCKS, ROWS), WIDE),
        ],
        scratch_shapes=[
            pltpu.VMEM((BLOCKS, ROWS, HEAD), LOW),
            pltpu.VMEM((2 * NZ, CHUNK, HEAD), LOW),
            pltpu.VMEM((2 * NZ, HEAD + 16, CHUNK), LOW),
            pltpu.VMEM((BLOCKS, ROWS), WIDE),
        ],
        compiler_params=params(32),
        cost_estimate=pl.CostEstimate(
            flops=8 * 10**9, bytes_accessed=4 * 2**20, transcendentals=2 * 2**20
        ),
        name="forward",
    )(scalars, *q_blocks, *arrays)


def weighted(o_part, ml, u_blocks):
    def kernel(o_ref, ml_ref, *refs):
        u = refs[0:4]
        out_ref = refs[4]
        out_ref[: 2 * BLOCKS, :] = ml_ref[...]
        for o in range(2):
            for dy in range(NY):
                block, first = place(o, dy)
                for h in range(RATIO):
                    at = slice(first + h * CHUNK, first + (h + 1) * CHUNK)
                    ut = u[dy][o * CHUNK : (o + 1) * CHUNK, h * HEAD : (h + 1) * HEAD]
                    out_ref[2 * BLOCKS + block : 2 * BLOCKS + block + 1, at] = jnp.sum(
                        ut.astype(WIDE).T * o_ref[block, :HEAD, at], axis=0, keepdims=True
                    )

    return pl.pallas_call(
        kernel,
        in_specs=[vspec()] * 6,
        out_specs=vspec(),
        out_shape=jax.ShapeDtypeStruct((3 * BLOCKS, ROWS), WIDE),
        compiler_params=params(16),
        name="weighted",
    )(o_part, ml, *u_blocks)


def backward(cls, scalars, stats, q_blocks, u_blocks, arrays, views, dq_before):
    last = dq_before is not None
    n = len(arrays)
    chunks = 2 * len(DISTANCES[cls])

    def kernel(sc, *refs):
        st = refs[0:4]
        q = refs[4:8]
        u = refs[8:12]
        kv = refs[12 : 12 + n]
        refs = refs[12 + n :]
        if last:
            before, refs = refs[0], refs[1:]
            dq_out, dkv_out, refs = refs[0:4], refs[4:7], refs[7:]
        else:
            dq_out, dkv_out, refs = refs[0:1], refs[1:4], refs[4:]
        qs, us, kc, vc, kt, dk, dv, al, lse_s, delta_s, low_s = refs[:11]
        dqt = refs[11] if last else dq_out[0]
        xl, z, y = sc[0], sc[1], sc[2]
        here = [(kv[a], first) for a, first, _ in views]
        stack_rows(qs, q, PIECE)
        stack_rows(us, u, CHUNK)
        fill_low(low_s, q, here)
        for (ref, first), (_, _, d) in zip(here, views):
            for o in range(2):
                at = key_chunk(cls, xl, z, o, d)
                rows = slice(first + o * PIECE, first + o * PIECE + CHUNK)
                key = ref[rows, :HEAD]
                kc[at] = key
                vc[at] = ref[rows, HEAD:]
                kt[at] = key.T
        dk[...] = jnp.zeros(dk.shape, WIDE)
        dv[...] = jnp.zeros(dv.shape, WIDE)
        dqt[...] = before[...] if last else jnp.zeros(dqt.shape, WIDE)

        for i in range(NY):
            for kind in range(3):
                for o in range(2):
                    for dy in range(NY):
                        b, to = place(o, dy)
                        c, frm = place(o, (dy - i) % NY)
                        b, c = kind * BLOCKS + b, kind * BLOCKS + c
                        al[i, b : b + 1, to : to + GROUP] = st[i][c : c + 1, frm : frm + GROUP]
        tops = [al[i, :BLOCKS] for i in range(NY)]
        top = functools.reduce(jnp.maximum, tops)
        factors = [jnp.exp2(t - top) for t in tops]
        mass = sum(f * al[i, BLOCKS : 2 * BLOCKS] for i, f in enumerate(factors))
        share = sum(f * al[i, 2 * BLOCKS :] for i, f in enumerate(factors))
        lse_s[...] = top + jnp.log2(mass)
        delta_s[...] = share / mass

        def one_block(block, _):
            lse = lse_s[pl.ds(block, 1), :]
            delta = delta_s[pl.ds(block, 1), :]
            qp = qs[block]
            up = us[block]

            def tile(t, mask):
                k = kc[pl.ds(2 * t, 2)].reshape(KT, HEAD)
                v = vc[pl.ds(2 * t, 2)].reshape(KT, HEAD)
                p = jnp.exp2(mask(dot(k, qp, NT) * C2) - lse)
                ds = (p * (dot(v, up, NT) - delta)).astype(LOW)
                p = p.astype(LOW)
                dv[pl.ds(2 * t, 2)] += dot(p, up).reshape(2, CHUNK, HEAD)
                dk[pl.ds(2 * t, 2)] += dot(ds, qp).reshape(2, CHUNK, HEAD)
                kt_tile = jnp.concatenate([kt[2 * t], kt[2 * t + 1]], axis=1)
                dqt[block] += dot(kt_tile, ds)

            over_tiles(limits(cls, block, xl, z, y, low_s), tile)
            return 0

        lax.fori_loop(0, BLOCKS, one_block, 0)

        def write(out, first, d):
            for o in range(2):
                at = key_chunk(cls, xl, z, o, d)
                rows = slice(first + o * CHUNK, first + (o + 1) * CHUNK)
                out[rows, :HEAD] = (dk[at] * SCALE).astype(out.dtype)
                out[rows, HEAD:] = dv[at].astype(out.dtype)

        if last:
            for out, d in zip(dkv_out, DISTANCES[cls]):
                write(out, 0, d)
            for dy in range(NY):
                for o in range(2):
                    block, first = place(o, dy)
                    for h in range(RATIO):
                        start = first + h * CHUNK
                        part = dqt[block, :, start : start + CHUNK].T * SCALE
                        dq_out[dy][
                            o * CHUNK : (o + 1) * CHUNK, h * HEAD : (h + 1) * HEAD
                        ] = part.astype(dq_out[dy].dtype)
        else:
            write(dkv_out[0], 0, 1)
            write(dkv_out[0], 2 * CHUNK, 3)
            write(dkv_out[1], 0, 7)
            write(dkv_out[1], 2 * CHUNK, 5)
            write(dkv_out[2], 0, 4)

    dq_state = jax.ShapeDtypeStruct((BLOCKS, HEAD, ROWS), WIDE)
    if last:
        out_shape = [
            jax.ShapeDtypeStruct((2 * CHUNK, GROUP), WIDE if dy == 0 else LOW)
            for dy in range(NY)
        ] + [
            jax.ShapeDtypeStruct((2 * CHUNK, 2 * HEAD), WIDE) for d in DISTANCES[cls]
        ]
    else:
        out_shape = [dq_state] + [
            jax.ShapeDtypeStruct((n * CHUNK, 2 * HEAD), LOW) for n in (4, 4, 2)
        ]
    state = [dq_before] if last else []
    return pl.pallas_call(
        kernel,
        in_specs=[sspec()] + [vspec()] * (12 + n + len(state)),
        out_specs=[vspec()] * len(out_shape),
        out_shape=out_shape,
        scratch_shapes=[
            pltpu.VMEM((BLOCKS, ROWS, HEAD), LOW),
            pltpu.VMEM((BLOCKS, ROWS, HEAD), LOW),
            pltpu.VMEM((chunks, CHUNK, HEAD), LOW),
            pltpu.VMEM((chunks, CHUNK, HEAD), LOW),
            pltpu.VMEM((chunks, HEAD, CHUNK), LOW),
            pltpu.VMEM((chunks, CHUNK, HEAD), WIDE),
            pltpu.VMEM((chunks, CHUNK, HEAD), WIDE),
            pltpu.VMEM((NY, 3 * BLOCKS, ROWS), WIDE),
            pltpu.VMEM((BLOCKS, ROWS), WIDE),
            pltpu.VMEM((BLOCKS, ROWS), WIDE),
            pltpu.VMEM((BLOCKS, ROWS), WIDE),
        ]
        + ([pltpu.VMEM((BLOCKS, HEAD, ROWS), WIDE)] if last else []),
        compiler_params=params(32),
        cost_estimate=pl.CostEstimate(
            flops=8 * 10**9, bytes_accessed=6 * 2**20, transcendentals=2 * 2**20
        ),
        name="backward%d" % cls,
    )(scalars, *stats, *q_blocks, *u_blocks, *arrays, *state)


def settle(dq, dq_got, dkv, dkv_got):
    def kernel(*refs):
        dq_ref, a, b, c, dkv_ref, d, e, f, keep, send = refs
        for out, first in ((keep, 0), (send, CHUNK)):
            rows = slice(first, first + CHUNK)
            total = dq_ref[rows, :]
            for g in (a, b, c):
                total += g[rows, :].astype(WIDE)
            out[:, :GROUP] = total.astype(LOW)
            total = dkv_ref[rows, :]
            for g in (d, e, f):
                total += g[rows, :].astype(WIDE)
            out[:, GROUP:] = total.astype(LOW)

    return pl.pallas_call(
        kernel,
        in_specs=[vspec()] * 8,
        out_specs=[vspec()] * 2,
        out_shape=[jax.ShapeDtypeStruct((CHUNK, GROUP + 2 * HEAD), LOW)] * 2,
        compiler_params=params(8),
        name="settle",
    )(dq, *dq_got, dkv, *dkv_got)


def join(scalars, keep, back):
    def kernel(sc, keep_ref, back_ref, q_ref, k_ref, v_ref):
        xl = sc[0]
        for g, ref in ((xl, keep_ref), (1 - xl, back_ref)):
            q_ref[:, pl.ds(pl.multiple_of(g * GROUP, GROUP), GROUP)] = ref[:, :GROUP]
            at = pl.ds(pl.multiple_of(g * HEAD, HEAD), HEAD)
            k_ref[:, at] = ref[:, GROUP : GROUP + HEAD]
            v_ref[:, at] = ref[:, GROUP + HEAD :]

    return pl.pallas_call(
        kernel,
        in_specs=[sspec(), vspec(), vspec()],
        out_specs=[vspec()] * 3,
        out_shape=[
            jax.ShapeDtypeStruct((CHUNK, 2 * GROUP), LOW),
            jax.ShapeDtypeStruct((CHUNK, 2 * HEAD), LOW),
            jax.ShapeDtypeStruct((CHUNK, 2 * HEAD), LOW),
        ],
        compiler_params=params(8),
        name="join",
    )(scalars, keep, back)


def shift(x, axis, size, d):
    return lax.ppermute(x, axis, [(i, (i - d) % size) for i in range(size)])


def swap(x):
    return shift(x, "xl", XL, 1)


def below(whole, x):
    return lax.dynamic_update_slice(whole, x, (whole.shape[0] - x.shape[0], 0))


def along_y(x):
    return [x] + [shift(x, "y", NY, d) for d in (1, 2, 3)]


def per_device(queries, keys, values, grad_out, out_weight, segments):
    xl, z, y = lax.axis_index("xl"), lax.axis_index("z"), lax.axis_index("y")
    tp = lax.axis_index("xh") * 2 + lax.axis_index("core")
    scalars = jnp.stack([xl, z, y, tp]).astype(jnp.int32)

    far = shift(grad_out, "xh", 2, 1)
    mate = shift(grad_out, "core", 2, 1)
    q_own, q_oth, kv_own, kv_oth = prepare(scalars, queries, keys, values, segments)
    kv_in = swap(kv_oth)
    q_in = swap(q_oth)

    weight, grad = stage(out_weight, grad_out)
    kv_in, _ = lax.optimization_barrier((kv_in, grad))
    kv = below(kv_own, kv_in)
    kv_up2 = shift(kv, "z", NZ, 2)
    kv_down2 = shift(kv, "z", NZ, -2)
    kv_4 = shift(kv, "z", NZ, 4)
    q_blocks = along_y(below(q_own, q_in))
    kv_up = shift(jnp.concatenate([kv, kv_up2], axis=0), "z", NZ, 1)
    kv_down = shift(jnp.concatenate([kv, kv_down2], axis=0), "z", NZ, -1)
    second = 2 * PIECE
    odd = [kv_up, kv_down, kv_4]
    odd_views = [(0, 0, 1), (0, second, 3), (1, second, 5), (1, 0, 7), (2, 0, 4)]
    even = [kv, kv_up2, kv_down2]
    even_views = [(0, 0, 0), (1, 0, 2), (2, 0, 6)]

    relay, _ = lax.optimization_barrier((far, kv))
    far_mate = shift(relay, "core", 2, 1)
    u_own, u_oth = upstream(scalars, [grad, mate, far, far_mate], weight)
    u_blocks = along_y(below(u_own, swap(u_oth)))

    o_part, ml = forward(
        scalars, q_blocks, even + odd, even_views + [(3 + a, f, d) for a, f, d in odd_views]
    )
    stats = along_y(weighted(o_part, ml, u_blocks))
    dq_state, bundle_up, bundle_down, dkv_4 = backward(
        1, scalars, stats, q_blocks, u_blocks, odd, odd_views, None
    )
    got_up = shift(bundle_up, "z", NZ, -1)
    got_down = shift(bundle_down, "z", NZ, 1)
    got_4 = shift(dkv_4, "z", NZ, 4)
    *dq, dkv, dkv_up2, dkv_down2 = backward(
        0, scalars, stats, q_blocks, u_blocks, even, even_views, dq_state
    )

    near, further = slice(0, 2 * CHUNK), slice(2 * CHUNK, None)
    dkv = dkv + got_up[near].astype(WIDE) + got_down[near].astype(WIDE)
    up2 = (dkv_up2 + got_up[further].astype(WIDE)).astype(LOW)
    down2 = (dkv_down2 + got_down[further].astype(WIDE)).astype(LOW)
    dq, up2, down2 = lax.optimization_barrier((dq, up2, down2))
    dkv_got = [
        got_4,
        shift(up2, "z", NZ, -2),
        shift(down2, "z", NZ, 2),
    ]
    dq_got = [shift(dq[d], "y", NY, -d) for d in (1, 2, 3)]
    keep, send = settle(dq[0], dq_got, dkv, dkv_got)
    return join(scalars, keep, swap(send))


def solution(mesh):
    fine = Mesh(mesh.devices.reshape(XL, NZ, NY, 2, 2), ("xl", "z", "y", "xh", "core"))
    ctx, tp = ("xl", "z", "y"), ("xh", "core")
    in_specs = (P(ctx, tp), P(ctx, tp), P(ctx, tp), P(ctx, tp), P(None, tp), P(ctx))
    out_specs = (P(ctx, tp), P(ctx, tp), P(ctx, tp))
    return jax.shard_map(
        per_device, mesh=fine, in_specs=in_specs, out_specs=out_specs, check_vma=False
    )
```

```python
import functools
import math

import jax
import jax.numpy as jnp
from jax import lax
from jax.experimental import pallas as pl
from jax.experimental.pallas import tpu as pltpu
from jax.sharding import Mesh, PartitionSpec as P

HEAD = 128
RATIO = 4
CHUNK = 128
XL, NZ, NY = 2, 8, 4
PIECE = CHUNK + 16
KEYS = NZ * CHUNK
GROUP = RATIO * HEAD
DP = 4
ROWS = DP * GROUP
BLOCKS = 2 * NY // DP
SCALE = HEAD**-0.5
C2 = SCALE * math.log2(math.e)
NEG = -1e30
WIDE = jnp.float32
LOW = jnp.bfloat16
NT = (((1,), (1,)), ((), ()))
NN = (((1,), (0,)), ((), ()))
MIB = 1024 * 1024


def dot(a, b, dims=NN):
    return lax.dot_general(a, b, dims, preferred_element_type=WIDE)


def vspec():
    return pl.BlockSpec(memory_space=pltpu.VMEM)


def hspec():
    return pl.BlockSpec(memory_space=pltpu.HBM)


def in_hbm(x):
    return pltpu.with_memory_space_constraint(x, pltpu.HBM)


def sspec():
    return pl.BlockSpec(memory_space=pltpu.SMEM)


def params(mib):
    return pltpu.CompilerParams(vmem_limit_bytes=mib * MIB)


def prepare(scalars, queries, keys, values, segments):
    def kernel(sc, q_ref, k_ref, v_ref, seg_ref, q_own, q_oth, kv_own, kv_oth, seg, sems):
        xl = sc[0]
        top = pl.ds(0, CHUNK)
        copies = [pltpu.make_async_copy(seg_ref, seg, sems.at[0])]
        for i, (g, q, kv) in enumerate(((1 - xl, q_oth, kv_oth), (xl, q_own, kv_own))):
            at = pl.ds(pl.multiple_of(g * GROUP, GROUP), GROUP)
            copies.append(
                pltpu.make_async_copy(q_ref.at[:, at], q.at[top], sems.at[3 * i + 1])
            )
            at = pl.ds(pl.multiple_of(g * HEAD, HEAD), HEAD)
            for j, ref in enumerate((k_ref, v_ref)):
                copies.append(
                    pltpu.make_async_copy(
                        ref.at[:, at],
                        kv.at[top, pl.ds(j * HEAD, HEAD)],
                        sems.at[3 * i + 2 + j],
                    )
                )
        for copy in copies:
            copy.start()
        copies[0].wait()
        count = jnp.sum(jnp.where(seg[...] == 0, 1.0, 0.0), axis=1, keepdims=True)
        count = jnp.broadcast_to(count, (16, HEAD)).astype(LOW)
        for q, kv in ((q_own, kv_own), (q_oth, kv_oth)):
            q[CHUNK:PIECE, :] = jnp.concatenate([count] * RATIO, axis=1)
            kv[CHUNK:PIECE, :] = jnp.concatenate([count] * 2, axis=1)
        for copy in copies[1:]:
            copy.wait()

    return pl.pallas_call(
        kernel,
        in_specs=[sspec()] + [hspec()] * 4,
        out_specs=[vspec()] * 4,
        out_shape=[
            jax.ShapeDtypeStruct((2 * PIECE, GROUP), LOW),
            jax.ShapeDtypeStruct((PIECE, GROUP), LOW),
            jax.ShapeDtypeStruct((2 * PIECE, 2 * HEAD), LOW),
            jax.ShapeDtypeStruct((PIECE, 2 * HEAD), LOW),
        ],
        scratch_shapes=[pltpu.VMEM((1, CHUNK), jnp.int32), pltpu.SemaphoreType.DMA((7,))],
        compiler_params=params(8),
        name="prepare",
    )(scalars, *[in_hbm(x) for x in (queries, keys, values, segments.reshape(1, CHUNK))])


def stage(weight, grad):
    def kernel(w_hbm, g_hbm, w_ref, g_ref, sems):
        copies = [
            pltpu.make_async_copy(w_hbm, w_ref, sems.at[0]),
            pltpu.make_async_copy(g_hbm, g_ref, sems.at[1]),
        ]
        for copy in copies:
            copy.start()
        for copy in copies:
            copy.wait()

    return pl.pallas_call(
        kernel,
        in_specs=[hspec()] * 2,
        out_specs=[vspec()] * 2,
        out_shape=[jax.ShapeDtypeStruct(x.shape, x.dtype) for x in (weight, grad)],
        scratch_shapes=[pltpu.SemaphoreType.DMA((2,))],
        compiler_params=params(12),
        cost_estimate=pl.CostEstimate(
            flops=0, bytes_accessed=4 * weight.size, transcendentals=0
        ),
        name="stage",
    )(in_hbm(weight), in_hbm(grad))


def upstream(scalars, grads, weight):
    rows, depth = grads[0].shape
    width = weight.shape[1]

    def kernel(sc, *refs):
        gs = refs[:4]
        w_ref, own_ref, oth_ref, acc = refs[4:]
        xl, tp = sc[0], sc[3]
        for i in range(4):
            start = pl.multiple_of(jnp.bitwise_xor(tp, i) * depth, depth)
            term = dot(gs[i][...], w_ref[pl.ds(start, depth), :])
            acc[...] = term if i == 0 else acc[...] + term
        for g, out in ((1 - xl, oth_ref), (xl, own_ref)):
            at = pl.ds(pl.multiple_of(g * GROUP, GROUP), GROUP)
            out[:rows, :] = acc[:, at].astype(LOW)

    return pl.pallas_call(
        kernel,
        in_specs=[sspec()] + [vspec()] * 5,
        out_specs=[vspec()] * 2,
        out_shape=[
            jax.ShapeDtypeStruct((2 * rows, GROUP), LOW),
            jax.ShapeDtypeStruct((rows, GROUP), LOW),
        ],
        scratch_shapes=[pltpu.VMEM((rows, width), WIDE)],
        compiler_params=params(16),
        name="upstream",
    )(scalars, *grads, weight)


DISTANCES = {None: tuple(range(NZ)), 0: (0, 2, 6), 1: (1, 3, 5, 7, 4)}


def place(o, dy):
    return o * (NY // DP) + dy // DP, (dy % DP) * GROUP


def stack_rows(dst, blocks, step):
    for o in range(2):
        for dy in range(NY):
            block, first = place(o, dy)
            for h in range(RATIO):
                start = first + h * CHUNK
                dst[block, start : start + CHUNK, :] = blocks[dy][
                    o * step : o * step + CHUNK, h * HEAD : (h + 1) * HEAD
                ]


def rank(cls, plane, z):
    if cls is None:
        return plane
    odd = (plane + 1 - lax.rem(z + 1, 2)) // 2
    fourth = jnp.where(lax.rem(z + 4, NZ) < plane, 1, 0)
    return odd + fourth if cls == 1 else plane - odd - fourth


def key_chunk(cls, xl, z, o, d):
    half = xl if o == 0 else 1 - xl
    return half * len(DISTANCES[cls]) + rank(cls, lax.rem(z + d, NZ), z)


def count_row(ref, first):
    return ref[first + CHUNK : first + PIECE, :HEAD].astype(WIDE)[:1]


def fill_low(low_s, q, views):
    zeros = sum(count_row(ref, first + o * PIECE) for ref, first in views for o in range(2))
    tok = lax.broadcasted_iota(jnp.int32, (1, CHUNK), 1).astype(WIDE)
    for o in range(2):
        for dy in range(NY):
            low = jnp.where(tok >= count_row(q[dy], o * PIECE), zeros, 0.0)
            block, first = place(o, dy)
            for h in range(RATIO):
                start = first + h * CHUNK
                low_s[block : block + 1, start : start + CHUNK] = low


def limits(cls, block, xl, z, y, low_s):
    o = block // (NY // DP)
    h = jnp.where(o == 0, xl, 1 - xl)
    plane = z
    dy0 = lax.rem(block, NY // DP) * DP
    ys = [lax.rem(y + dy0 + i, NY) for i in range(DP)]
    full = (h * len(DISTANCES[cls]) + rank(cls, plane, z)) * CHUNK
    if cls != 1:
        lane = lax.broadcasted_iota(jnp.int32, (1, ROWS), 1)
        yy = jnp.full((1, ROWS), ys[-1], jnp.int32)
        for i in reversed(range(DP - 1)):
            yy = jnp.where(lane < (i + 1) * GROUP, ys[i], yy)
        off = (yy - y) * CHUNK + jnp.bitwise_and(lane, CHUNK - 1)
        high = full + jnp.clip(off + 1, 0, CHUNK)
        top = full + jnp.where(functools.reduce(jnp.maximum, ys) >= y, CHUNK, 0)
    else:
        high = jnp.full((1, ROWS), full, jnp.int32)
        top = full
    low_f = low_s[pl.ds(block, 1), :]
    low = low_f.astype(jnp.int32)
    c_low = jnp.min(low_f).astype(jnp.int32) // CHUNK
    return low, high, c_low, top // CHUNK, jnp.max(low_f).astype(jnp.int32), full


def over_tiles(lim, body):
    low, high, c_low, c_high, max_low, full = lim

    def mask(c, s):
        kk = c * CHUNK + lax.broadcasted_iota(jnp.int32, s.shape, 0)
        return jnp.where((kk >= low) & (kk < high), s, NEG)

    def step(i, _):
        c = c_low + 2 * i
        inside = (c * CHUNK >= max_low) & ((c + 2) * CHUNK <= full)

        @pl.when(inside)
        def _():
            body(c, 2, lambda s: s)

        @pl.when(jnp.logical_not(inside))
        def _():
            body(c, 2, functools.partial(mask, c))

        return 0

    count = jnp.maximum(c_high - c_low, 0)
    lax.fori_loop(0, count // 2, step, 0)

    @pl.when(lax.rem(count, 2) == 1)
    def _():
        body(c_high - 1, 1, functools.partial(mask, c_high - 1))


def forward(scalars, q_blocks, arrays, views):
    def kernel(sc, *refs):
        q = refs[0:4]
        kv = refs[4 : 4 + len(arrays)]
        o_ref, ml_ref, qs, kc, vt, low_s = refs[4 + len(arrays) :]
        xl, z, y = sc[0], sc[1], sc[2]
        stack_rows(qs, q, PIECE)
        here = [(kv[a], first) for a, first, _ in views]
        fill_low(low_s, q, here)
        for (ref, first), (_, _, d) in zip(here, views):
            for o in range(2):
                at = key_chunk(None, xl, z, o, d)
                rows = slice(first + o * PIECE, first + o * PIECE + CHUNK)
                kc[at] = ref[rows, :HEAD]
                vt[at, :HEAD, :] = ref[rows, HEAD:].T
                vt[at, HEAD:, :] = jnp.ones((16, CHUNK), LOW)

        def one_block(block, _):
            qp = qs[block]
            o_ref[block] = jnp.zeros((HEAD + 16, ROWS), WIDE)
            ml_ref[pl.ds(block, 1), :] = jnp.full((1, ROWS), NEG, WIDE)

            def tile(c, n, mask):
                k = kc[pl.ds(c, n)].reshape(n * CHUNK, HEAD)
                s = mask(dot(k, qp, NT) * C2)
                old = ml_ref[pl.ds(block, 1), :]
                new = jnp.maximum(old, jnp.max(s, axis=0, keepdims=True))
                p = jnp.exp2(s - new).astype(LOW)
                v = jnp.concatenate([vt[c + i] for i in range(n)], axis=1)
                o_ref[block] = o_ref[block] * jnp.exp2(old - new) + dot(v, p)
                ml_ref[pl.ds(block, 1), :] = new

            over_tiles(limits(None, block, xl, z, y, low_s), tile)
            return 0

        lax.fori_loop(0, BLOCKS, one_block, 0)
        for block in range(BLOCKS):
            ml_ref[BLOCKS + block : BLOCKS + block + 1, :] = o_ref[block, HEAD : HEAD + 1, :]

    return pl.pallas_call(
        kernel,
        in_specs=[sspec()] + [vspec()] * (4 + len(arrays)),
        out_specs=[vspec()] * 2,
        out_shape=[
            jax.ShapeDtypeStruct((BLOCKS, HEAD + 16, ROWS), WIDE),
            jax.ShapeDtypeStruct((2 * BLOCKS, ROWS), WIDE),
        ],
        scratch_shapes=[
            pltpu.VMEM((BLOCKS, ROWS, HEAD), LOW),
            pltpu.VMEM((2 * NZ, CHUNK, HEAD), LOW),
            pltpu.VMEM((2 * NZ, HEAD + 16, CHUNK), LOW),
            pltpu.VMEM((BLOCKS, ROWS), WIDE),
        ],
        compiler_params=params(32),
        cost_estimate=pl.CostEstimate(
            flops=8 * 10**9, bytes_accessed=4 * 2**20, transcendentals=2 * 2**20
        ),
        name="forward",
    )(scalars, *q_blocks, *arrays)


def weighted(o_part, ml, u_blocks):
    def kernel(o_ref, ml_ref, *refs):
        u = refs[0:4]
        out_ref = refs[4]
        out_ref[: 2 * BLOCKS, :] = ml_ref[...]
        for o in range(2):
            for dy in range(NY):
                block, first = place(o, dy)
                for h in range(RATIO):
                    at = slice(first + h * CHUNK, first + (h + 1) * CHUNK)
                    ut = u[dy][o * CHUNK : (o + 1) * CHUNK, h * HEAD : (h + 1) * HEAD]
                    out_ref[2 * BLOCKS + block : 2 * BLOCKS + block + 1, at] = jnp.sum(
                        ut.astype(WIDE).T * o_ref[block, :HEAD, at], axis=0, keepdims=True
                    )

    return pl.pallas_call(
        kernel,
        in_specs=[vspec()] * 6,
        out_specs=vspec(),
        out_shape=jax.ShapeDtypeStruct((3 * BLOCKS, ROWS), WIDE),
        compiler_params=params(16),
        name="weighted",
    )(o_part, ml, *u_blocks)


def backward(cls, scalars, stats, q_blocks, u_blocks, arrays, views, dq_before):
    last = dq_before is not None
    n = len(arrays)
    chunks = 2 * len(DISTANCES[cls])

    def kernel(sc, *refs):
        st = refs[0:4]
        q = refs[4:8]
        u = refs[8:12]
        kv = refs[12 : 12 + n]
        refs = refs[12 + n :]
        if last:
            before, refs = refs[0], refs[1:]
            dq_out, dkv_out, refs = refs[0:4], refs[4:7], refs[7:]
        else:
            dq_out, dkv_out, refs = refs[0:1], refs[1:4], refs[4:]
        qs, us, kc, vc, kt, dk, dv, al, lse_s, delta_s, low_s = refs[:11]
        dqt = refs[11] if last else dq_out[0]
        xl, z, y = sc[0], sc[1], sc[2]
        here = [(kv[a], first) for a, first, _ in views]
        stack_rows(qs, q, PIECE)
        stack_rows(us, u, CHUNK)
        fill_low(low_s, q, here)
        for (ref, first), (_, _, d) in zip(here, views):
            for o in range(2):
                at = key_chunk(cls, xl, z, o, d)
                rows = slice(first + o * PIECE, first + o * PIECE + CHUNK)
                key = ref[rows, :HEAD]
                kc[at] = key
                vc[at] = ref[rows, HEAD:]
                kt[at] = key.T
        dk[...] = jnp.zeros(dk.shape, WIDE)
        dv[...] = jnp.zeros(dv.shape, WIDE)
        dqt[...] = before[...] if last else jnp.zeros(dqt.shape, WIDE)

        for i in range(NY):
            for kind in range(3):
                for o in range(2):
                    for dy in range(NY):
                        b, to = place(o, dy)
                        c, frm = place(o, (dy - i) % NY)
                        b, c = kind * BLOCKS + b, kind * BLOCKS + c
                        al[i, b : b + 1, to : to + GROUP] = st[i][c : c + 1, frm : frm + GROUP]
        tops = [al[i, :BLOCKS] for i in range(NY)]
        top = functools.reduce(jnp.maximum, tops)
        factors = [jnp.exp2(t - top) for t in tops]
        mass = sum(f * al[i, BLOCKS : 2 * BLOCKS] for i, f in enumerate(factors))
        share = sum(f * al[i, 2 * BLOCKS :] for i, f in enumerate(factors))
        lse_s[...] = top + jnp.log2(mass)
        delta_s[...] = share / mass

        def one_block(block, _):
            lse = lse_s[pl.ds(block, 1), :]
            delta = delta_s[pl.ds(block, 1), :]
            qp = qs[block]
            up = us[block]

            def tile(c, n, mask):
                k = kc[pl.ds(c, n)].reshape(n * CHUNK, HEAD)
                v = vc[pl.ds(c, n)].reshape(n * CHUNK, HEAD)
                p = jnp.exp2(mask(dot(k, qp, NT) * C2) - lse)
                ds = (p * (dot(v, up, NT) - delta)).astype(LOW)
                p = p.astype(LOW)
                dv[pl.ds(c, n)] += dot(p, up).reshape(n, CHUNK, HEAD)
                dk[pl.ds(c, n)] += dot(ds, qp).reshape(n, CHUNK, HEAD)
                kt_tile = jnp.concatenate([kt[c + i] for i in range(n)], axis=1)
                dqt[block] += dot(kt_tile, ds)

            over_tiles(limits(cls, block, xl, z, y, low_s), tile)
            return 0

        lax.fori_loop(0, BLOCKS, one_block, 0)

        def write(out, first, d):
            for o in range(2):
                at = key_chunk(cls, xl, z, o, d)
                rows = slice(first + o * CHUNK, first + (o + 1) * CHUNK)
                out[rows, :HEAD] = (dk[at] * SCALE).astype(out.dtype)
                out[rows, HEAD:] = dv[at].astype(out.dtype)

        if last:
            for out, d in zip(dkv_out, DISTANCES[cls]):
                write(out, 0, d)
            for dy in range(NY):
                for o in range(2):
                    block, first = place(o, dy)
                    for h in range(RATIO):
                        start = first + h * CHUNK
                        part = dqt[block, :, start : start + CHUNK].T * SCALE
                        dq_out[dy][
                            o * CHUNK : (o + 1) * CHUNK, h * HEAD : (h + 1) * HEAD
                        ] = part.astype(dq_out[dy].dtype)
        else:
            write(dkv_out[0], 0, 1)
            write(dkv_out[0], 2 * CHUNK, 3)
            write(dkv_out[1], 0, 7)
            write(dkv_out[1], 2 * CHUNK, 5)
            write(dkv_out[2], 0, 4)

    dq_state = jax.ShapeDtypeStruct((BLOCKS, HEAD, ROWS), WIDE)
    if last:
        out_shape = [
            jax.ShapeDtypeStruct((2 * CHUNK, GROUP), WIDE if dy == 0 else LOW)
            for dy in range(NY)
        ] + [
            jax.ShapeDtypeStruct((2 * CHUNK, 2 * HEAD), WIDE) for d in DISTANCES[cls]
        ]
    else:
        out_shape = [dq_state] + [
            jax.ShapeDtypeStruct((n * CHUNK, 2 * HEAD), LOW) for n in (4, 4, 2)
        ]
    state = [dq_before] if last else []
    return pl.pallas_call(
        kernel,
        in_specs=[sspec()] + [vspec()] * (12 + n + len(state)),
        out_specs=[vspec()] * len(out_shape),
        out_shape=out_shape,
        scratch_shapes=[
            pltpu.VMEM((BLOCKS, ROWS, HEAD), LOW),
            pltpu.VMEM((BLOCKS, ROWS, HEAD), LOW),
            pltpu.VMEM((chunks, CHUNK, HEAD), LOW),
            pltpu.VMEM((chunks, CHUNK, HEAD), LOW),
            pltpu.VMEM((chunks, HEAD, CHUNK), LOW),
            pltpu.VMEM((chunks, CHUNK, HEAD), WIDE),
            pltpu.VMEM((chunks, CHUNK, HEAD), WIDE),
            pltpu.VMEM((NY, 3 * BLOCKS, ROWS), WIDE),
            pltpu.VMEM((BLOCKS, ROWS), WIDE),
            pltpu.VMEM((BLOCKS, ROWS), WIDE),
            pltpu.VMEM((BLOCKS, ROWS), WIDE),
        ]
        + ([pltpu.VMEM((BLOCKS, HEAD, ROWS), WIDE)] if last else []),
        compiler_params=params(32),
        cost_estimate=pl.CostEstimate(
            flops=8 * 10**9, bytes_accessed=6 * 2**20, transcendentals=2 * 2**20
        ),
        name="backward%d" % cls,
    )(scalars, *stats, *q_blocks, *u_blocks, *arrays, *state)


def settle(dq, dq_got, dkv, dkv_got):
    def kernel(*refs):
        dq_ref, a, b, c, dkv_ref, d, e, f, keep, send = refs
        for out, first in ((keep, 0), (send, CHUNK)):
            rows = slice(first, first + CHUNK)
            total = dq_ref[rows, :]
            for g in (a, b, c):
                total += g[rows, :].astype(WIDE)
            out[:, :GROUP] = total.astype(LOW)
            total = dkv_ref[rows, :]
            for g in (d, e, f):
                total += g[rows, :].astype(WIDE)
            out[:, GROUP:] = total.astype(LOW)

    return pl.pallas_call(
        kernel,
        in_specs=[vspec()] * 8,
        out_specs=[vspec()] * 2,
        out_shape=[jax.ShapeDtypeStruct((CHUNK, GROUP + 2 * HEAD), LOW)] * 2,
        compiler_params=params(8),
        name="settle",
    )(dq, *dq_got, dkv, *dkv_got)


def join(scalars, keep, back):
    def kernel(sc, keep_ref, back_ref, q_ref, k_ref, v_ref):
        xl = sc[0]
        for g, ref in ((xl, keep_ref), (1 - xl, back_ref)):
            q_ref[:, pl.ds(pl.multiple_of(g * GROUP, GROUP), GROUP)] = ref[:, :GROUP]
            at = pl.ds(pl.multiple_of(g * HEAD, HEAD), HEAD)
            k_ref[:, at] = ref[:, GROUP : GROUP + HEAD]
            v_ref[:, at] = ref[:, GROUP + HEAD :]

    return pl.pallas_call(
        kernel,
        in_specs=[sspec(), vspec(), vspec()],
        out_specs=[vspec()] * 3,
        out_shape=[
            jax.ShapeDtypeStruct((CHUNK, 2 * GROUP), LOW),
            jax.ShapeDtypeStruct((CHUNK, 2 * HEAD), LOW),
            jax.ShapeDtypeStruct((CHUNK, 2 * HEAD), LOW),
        ],
        compiler_params=params(8),
        name="join",
    )(scalars, keep, back)


def shift(x, axis, size, d):
    return lax.ppermute(x, axis, [(i, (i - d) % size) for i in range(size)])


def swap(x):
    return shift(x, "xl", XL, 1)


def below(whole, x):
    return lax.dynamic_update_slice(whole, x, (whole.shape[0] - x.shape[0], 0))


def along_y(x):
    return [x] + [shift(x, "y", NY, d) for d in (1, 2, 3)]


def per_device(queries, keys, values, grad_out, out_weight, segments):
    xl, z, y = lax.axis_index("xl"), lax.axis_index("z"), lax.axis_index("y")
    tp = lax.axis_index("xh") * 2 + lax.axis_index("core")
    scalars = jnp.stack([xl, z, y, tp]).astype(jnp.int32)

    far = shift(grad_out, "xh", 2, 1)
    mate = shift(grad_out, "core", 2, 1)
    q_own, q_oth, kv_own, kv_oth = prepare(scalars, queries, keys, values, segments)
    kv_in = swap(kv_oth)
    q_in = swap(q_oth)

    weight, grad = stage(out_weight, grad_out)
    kv_in, _ = lax.optimization_barrier((kv_in, grad))
    kv = below(kv_own, kv_in)
    kv_up2 = shift(kv, "z", NZ, 2)
    kv_down2 = shift(kv, "z", NZ, -2)
    q_blocks = along_y(below(q_own, q_in))
    kv_late, _ = lax.optimization_barrier((kv, q_blocks[0]))
    kv_4 = shift(kv_late, "z", NZ, 4)
    kv_up = shift(jnp.concatenate([kv, kv_up2], axis=0), "z", NZ, 1)
    kv_down = shift(jnp.concatenate([kv, kv_down2], axis=0), "z", NZ, -1)
    second = 2 * PIECE
    odd = [kv_up, kv_down, kv_4]
    odd_views = [(0, 0, 1), (0, second, 3), (1, second, 5), (1, 0, 7), (2, 0, 4)]
    even = [kv, kv_up2, kv_down2]
    even_views = [(0, 0, 0), (1, 0, 2), (2, 0, 6)]

    relay, _ = lax.optimization_barrier((far, kv))
    far_mate = shift(relay, "core", 2, 1)
    u_own, u_oth = upstream(scalars, [grad, mate, far, far_mate], weight)
    u_blocks = along_y(below(u_own, swap(u_oth)))

    o_part, ml = forward(
        scalars, q_blocks, even + odd, even_views + [(3 + a, f, d) for a, f, d in odd_views]
    )
    stats = along_y(weighted(o_part, ml, u_blocks))
    dq_state, bundle_up, bundle_down, dkv_4 = backward(
        1, scalars, stats, q_blocks, u_blocks, odd, odd_views, None
    )
    got_up = shift(bundle_up, "z", NZ, -1)
    got_down = shift(bundle_down, "z", NZ, 1)
    got_4 = shift(dkv_4, "z", NZ, 4)
    *dq, dkv, dkv_up2, dkv_down2 = backward(
        0, scalars, stats, q_blocks, u_blocks, even, even_views, dq_state
    )

    near, further = slice(0, 2 * CHUNK), slice(2 * CHUNK, None)
    dkv = dkv + got_up[near].astype(WIDE) + got_down[near].astype(WIDE)
    up2 = (dkv_up2 + got_up[further].astype(WIDE)).astype(LOW)
    down2 = (dkv_down2 + got_down[further].astype(WIDE)).astype(LOW)
    dq, up2, down2 = lax.optimization_barrier((dq, up2, down2))
    dkv_got = [
        got_4,
        shift(up2, "z", NZ, -2),
        shift(down2, "z", NZ, 2),
    ]
    dq_got = [shift(dq[d], "y", NY, -d) for d in (1, 2, 3)]
    keep, send = settle(dq[0], dq_got, dkv, dkv_got)
    return join(scalars, keep, swap(send))


def solution(mesh):
    fine = Mesh(mesh.devices.reshape(XL, NZ, NY, 2, 2), ("xl", "z", "y", "xh", "core"))
    ctx, tp = ("xl", "z", "y"), ("xh", "core")
    in_specs = (P(ctx, tp), P(ctx, tp), P(ctx, tp), P(ctx, tp), P(None, tp), P(ctx))
    out_specs = (P(ctx, tp), P(ctx, tp), P(ctx, tp))
    return jax.shard_map(
        per_device, mesh=fine, in_specs=in_specs, out_specs=out_specs, check_vma=False
    )
```

```python
import functools
import math

import jax
import jax.numpy as jnp
from jax import lax
from jax.experimental import pallas as pl
from jax.experimental.pallas import tpu as pltpu
from jax.sharding import Mesh, PartitionSpec as P

HEAD = 128
RATIO = 4
CHUNK = 128
XL, NZ, NY = 2, 8, 4
PIECE = CHUNK + 16
KEYS = NZ * CHUNK
GROUP = RATIO * HEAD
DP = 4
ROWS = DP * GROUP
BLOCKS = 2 * NY // DP
SCALE = HEAD**-0.5
C2 = SCALE * math.log2(math.e)
NEG = -1e30
WIDE = jnp.float32
LOW = jnp.bfloat16
NT = (((1,), (1,)), ((), ()))
NN = (((1,), (0,)), ((), ()))
MIB = 1024 * 1024


def dot(a, b, dims=NN):
    return lax.dot_general(a, b, dims, preferred_element_type=WIDE)


def vspec():
    return pl.BlockSpec(memory_space=pltpu.VMEM)


def hspec():
    return pl.BlockSpec(memory_space=pltpu.HBM)


def in_hbm(x):
    return pltpu.with_memory_space_constraint(x, pltpu.HBM)


def sspec():
    return pl.BlockSpec(memory_space=pltpu.SMEM)


def params(mib):
    return pltpu.CompilerParams(vmem_limit_bytes=mib * MIB)


def prepare(scalars, queries, keys, values, segments):
    def kernel(sc, q_ref, k_ref, v_ref, seg_ref, q_own, q_oth, kv_own, kv_oth, seg, sems):
        xl = sc[0]
        top = pl.ds(0, CHUNK)
        copies = [pltpu.make_async_copy(seg_ref, seg, sems.at[0])]
        for i, (g, q, kv) in enumerate(((1 - xl, q_oth, kv_oth), (xl, q_own, kv_own))):
            at = pl.ds(pl.multiple_of(g * GROUP, GROUP), GROUP)
            copies.append(
                pltpu.make_async_copy(q_ref.at[:, at], q.at[top], sems.at[3 * i + 1])
            )
            at = pl.ds(pl.multiple_of(g * HEAD, HEAD), HEAD)
            for j, ref in enumerate((k_ref, v_ref)):
                copies.append(
                    pltpu.make_async_copy(
                        ref.at[:, at],
                        kv.at[top, pl.ds(j * HEAD, HEAD)],
                        sems.at[3 * i + 2 + j],
                    )
                )
        for copy in copies:
            copy.start()
        copies[0].wait()
        count = jnp.sum(jnp.where(seg[...] == 0, 1.0, 0.0), axis=1, keepdims=True)
        count = jnp.broadcast_to(count, (16, HEAD)).astype(LOW)
        for q, kv in ((q_own, kv_own), (q_oth, kv_oth)):
            q[CHUNK:PIECE, :] = jnp.concatenate([count] * RATIO, axis=1)
            kv[CHUNK:PIECE, :] = jnp.concatenate([count] * 2, axis=1)
        for copy in copies[1:]:
            copy.wait()

    return pl.pallas_call(
        kernel,
        in_specs=[sspec()] + [hspec()] * 4,
        out_specs=[vspec()] * 4,
        out_shape=[
            jax.ShapeDtypeStruct((2 * PIECE, GROUP), LOW),
            jax.ShapeDtypeStruct((PIECE, GROUP), LOW),
            jax.ShapeDtypeStruct((2 * PIECE, 2 * HEAD), LOW),
            jax.ShapeDtypeStruct((PIECE, 2 * HEAD), LOW),
        ],
        scratch_shapes=[pltpu.VMEM((1, CHUNK), jnp.int32), pltpu.SemaphoreType.DMA((7,))],
        compiler_params=params(8),
        name="prepare",
    )(scalars, *[in_hbm(x) for x in (queries, keys, values, segments.reshape(1, CHUNK))])


def stage(weight, grad):
    def kernel(w_hbm, g_hbm, w_ref, g_ref, sems):
        copies = [
            pltpu.make_async_copy(w_hbm, w_ref, sems.at[0]),
            pltpu.make_async_copy(g_hbm, g_ref, sems.at[1]),
        ]
        for copy in copies:
            copy.start()
        for copy in copies:
            copy.wait()

    return pl.pallas_call(
        kernel,
        in_specs=[hspec()] * 2,
        out_specs=[vspec()] * 2,
        out_shape=[jax.ShapeDtypeStruct(x.shape, x.dtype) for x in (weight, grad)],
        scratch_shapes=[pltpu.SemaphoreType.DMA((2,))],
        compiler_params=params(12),
        cost_estimate=pl.CostEstimate(
            flops=0, bytes_accessed=4 * weight.size, transcendentals=0
        ),
        name="stage",
    )(in_hbm(weight), in_hbm(grad))


def upstream(scalars, grads, weight):
    rows, depth = grads[0].shape
    width = weight.shape[1]

    def kernel(sc, *refs):
        gs = refs[:4]
        w_ref, own_ref, oth_ref, acc = refs[4:]
        xl, tp = sc[0], sc[3]
        for i in range(4):
            start = pl.multiple_of(jnp.bitwise_xor(tp, i) * depth, depth)
            term = dot(gs[i][...], w_ref[pl.ds(start, depth), :])
            acc[...] = term if i == 0 else acc[...] + term
        for g, out in ((1 - xl, oth_ref), (xl, own_ref)):
            at = pl.ds(pl.multiple_of(g * GROUP, GROUP), GROUP)
            out[:rows, :] = acc[:, at].astype(LOW)

    return pl.pallas_call(
        kernel,
        in_specs=[sspec()] + [vspec()] * 5,
        out_specs=[vspec()] * 2,
        out_shape=[
            jax.ShapeDtypeStruct((2 * rows, GROUP), LOW),
            jax.ShapeDtypeStruct((rows, GROUP), LOW),
        ],
        scratch_shapes=[pltpu.VMEM((rows, width), WIDE)],
        compiler_params=params(16),
        name="upstream",
    )(scalars, *grads, weight)


DISTANCES = {None: tuple(range(NZ)), 0: (0, 2, 6), 1: (1, 3, 5, 7, 4)}


def place(o, dy):
    return o * (NY // DP) + dy // DP, (dy % DP) * GROUP


def stack_rows(dst, blocks, step):
    for o in range(2):
        for dy in range(NY):
            block, first = place(o, dy)
            for h in range(RATIO):
                start = first + h * CHUNK
                dst[block, start : start + CHUNK, :] = blocks[dy][
                    o * step : o * step + CHUNK, h * HEAD : (h + 1) * HEAD
                ]


def rank(cls, plane, z):
    if cls is None:
        return plane
    odd = (plane + 1 - lax.rem(z + 1, 2)) // 2
    fourth = jnp.where(lax.rem(z + 4, NZ) < plane, 1, 0)
    return odd + fourth if cls == 1 else plane - odd - fourth


def key_chunk(cls, xl, z, o, d):
    half = xl if o == 0 else 1 - xl
    return half * len(DISTANCES[cls]) + rank(cls, lax.rem(z + d, NZ), z)


def count_row(ref, first):
    return ref[first + CHUNK : first + PIECE, :HEAD].astype(WIDE)[:1]


def fill_low(low_s, q, views):
    zeros = sum(count_row(ref, first + o * PIECE) for ref, first in views for o in range(2))
    tok = lax.broadcasted_iota(jnp.int32, (1, CHUNK), 1).astype(WIDE)
    for o in range(2):
        for dy in range(NY):
            low = jnp.where(tok >= count_row(q[dy], o * PIECE), zeros, 0.0)
            block, first = place(o, dy)
            for h in range(RATIO):
                start = first + h * CHUNK
                low_s[block : block + 1, start : start + CHUNK] = low


def limits(cls, block, xl, z, y, low_s):
    o = block // (NY // DP)
    h = jnp.where(o == 0, xl, 1 - xl)
    plane = z
    dy0 = lax.rem(block, NY // DP) * DP
    ys = [lax.rem(y + dy0 + i, NY) for i in range(DP)]
    full = (h * len(DISTANCES[cls]) + rank(cls, plane, z)) * CHUNK
    if cls != 1:
        lane = lax.broadcasted_iota(jnp.int32, (1, ROWS), 1)
        yy = jnp.full((1, ROWS), ys[-1], jnp.int32)
        for i in reversed(range(DP - 1)):
            yy = jnp.where(lane < (i + 1) * GROUP, ys[i], yy)
        off = (yy - y) * CHUNK + jnp.bitwise_and(lane, CHUNK - 1)
        high = full + jnp.clip(off + 1, 0, CHUNK)
        top = full + jnp.where(functools.reduce(jnp.maximum, ys) >= y, CHUNK, 0)
    else:
        high = jnp.full((1, ROWS), full, jnp.int32)
        top = full
    low_f = low_s[pl.ds(block, 1), :]
    low = low_f.astype(jnp.int32)
    c_low = jnp.min(low_f).astype(jnp.int32) // CHUNK
    return low, high, c_low, top // CHUNK, jnp.max(low_f).astype(jnp.int32), full


def over_tiles(lim, body):
    low, high, c_low, c_high, max_low, full = lim

    def mask(c, s):
        kk = c * CHUNK + lax.broadcasted_iota(jnp.int32, s.shape, 0)
        return jnp.where((kk >= low) & (kk < high), s, NEG)

    def step(i, _):
        c = c_low + 2 * i
        inside = (c * CHUNK >= max_low) & ((c + 2) * CHUNK <= full)

        @pl.when(inside)
        def _():
            body(c, 2, lambda s: s)

        @pl.when(jnp.logical_not(inside))
        def _():
            body(c, 2, functools.partial(mask, c))

        return 0

    count = jnp.maximum(c_high - c_low, 0)
    lax.fori_loop(0, count // 2, step, 0)

    @pl.when(lax.rem(count, 2) == 1)
    def _():
        body(c_high - 1, 1, functools.partial(mask, c_high - 1))


def forward(scalars, q_blocks, arrays, views):
    def kernel(sc, *refs):
        q = refs[0:4]
        kv = refs[4 : 4 + len(arrays)]
        o_ref, ml_ref, qs, kc, vt, low_s = refs[4 + len(arrays) :]
        xl, z, y = sc[0], sc[1], sc[2]
        stack_rows(qs, q, PIECE)
        here = [(kv[a], first) for a, first, _ in views]
        fill_low(low_s, q, here)
        for (ref, first), (_, _, d) in zip(here, views):
            for o in range(2):
                at = key_chunk(None, xl, z, o, d)
                rows = slice(first + o * PIECE, first + o * PIECE + CHUNK)
                kc[at] = ref[rows, :HEAD]
                vt[at, :HEAD, :] = ref[rows, HEAD:].T
                vt[at, HEAD:, :] = jnp.ones((16, CHUNK), LOW)

        def one_block(block, _):
            qp = qs[block]
            o_ref[block] = jnp.zeros((HEAD + 16, ROWS), WIDE)
            ml_ref[pl.ds(block, 1), :] = jnp.full((1, ROWS), NEG, WIDE)

            def tile(c, n, mask):
                k = kc[pl.ds(c, n)].reshape(n * CHUNK, HEAD)
                s = mask(dot(k, qp, NT) * C2)
                old = ml_ref[pl.ds(block, 1), :]
                new = jnp.maximum(old, jnp.max(s, axis=0, keepdims=True))
                p = jnp.exp2(s - new).astype(LOW)
                v = jnp.concatenate([vt[c + i] for i in range(n)], axis=1)
                o_ref[block] = o_ref[block] * jnp.exp2(old - new) + dot(v, p)
                ml_ref[pl.ds(block, 1), :] = new

            over_tiles(limits(None, block, xl, z, y, low_s), tile)
            return 0

        lax.fori_loop(0, BLOCKS, one_block, 0)
        for block in range(BLOCKS):
            ml_ref[BLOCKS + block : BLOCKS + block + 1, :] = o_ref[block, HEAD : HEAD + 1, :]

    return pl.pallas_call(
        kernel,
        in_specs=[sspec()] + [vspec()] * (4 + len(arrays)),
        out_specs=[vspec()] * 2,
        out_shape=[
            jax.ShapeDtypeStruct((BLOCKS, HEAD + 16, ROWS), WIDE),
            jax.ShapeDtypeStruct((2 * BLOCKS, ROWS), WIDE),
        ],
        scratch_shapes=[
            pltpu.VMEM((BLOCKS, ROWS, HEAD), LOW),
            pltpu.VMEM((2 * NZ, CHUNK, HEAD), LOW),
            pltpu.VMEM((2 * NZ, HEAD + 16, CHUNK), LOW),
            pltpu.VMEM((BLOCKS, ROWS), WIDE),
        ],
        compiler_params=params(32),
        cost_estimate=pl.CostEstimate(
            flops=8 * 10**9, bytes_accessed=4 * 2**20, transcendentals=2 * 2**20
        ),
        name="forward",
    )(scalars, *q_blocks, *arrays)


def weighted(o_part, ml, u_blocks):
    def kernel(o_ref, ml_ref, *refs):
        u = refs[0:4]
        out_ref = refs[4]
        out_ref[: 2 * BLOCKS, :] = ml_ref[...]
        for o in range(2):
            for dy in range(NY):
                block, first = place(o, dy)
                for h in range(RATIO):
                    at = slice(first + h * CHUNK, first + (h + 1) * CHUNK)
                    ut = u[dy][o * CHUNK : (o + 1) * CHUNK, h * HEAD : (h + 1) * HEAD]
                    out_ref[2 * BLOCKS + block : 2 * BLOCKS + block + 1, at] = jnp.sum(
                        ut.astype(WIDE).T * o_ref[block, :HEAD, at], axis=0, keepdims=True
                    )

    return pl.pallas_call(
        kernel,
        in_specs=[vspec()] * 6,
        out_specs=vspec(),
        out_shape=jax.ShapeDtypeStruct((3 * BLOCKS, ROWS), WIDE),
        compiler_params=params(16),
        name="weighted",
    )(o_part, ml, *u_blocks)


def backward(cls, scalars, stats, q_blocks, u_blocks, arrays, views, dq_before):
    last = dq_before is not None
    n = len(arrays)
    chunks = 2 * len(DISTANCES[cls])

    def kernel(sc, *refs):
        st = refs[0:4]
        q = refs[4:8]
        u = refs[8:12]
        kv = refs[12 : 12 + n]
        refs = refs[12 + n :]
        if last:
            before, refs = refs[0], refs[1:]
            dq_out, dkv_out, refs = refs[0:4], refs[4:7], refs[7:]
        else:
            dq_out, dkv_out, refs = refs[0:1], refs[1:4], refs[4:]
        qs, us, kc, vc, kt, dk, dv, al, lse_s, delta_s, low_s = refs[:11]
        dqt = refs[11] if last else dq_out[0]
        xl, z, y = sc[0], sc[1], sc[2]
        here = [(kv[a], first) for a, first, _ in views]
        stack_rows(qs, q, PIECE)
        stack_rows(us, u, CHUNK)
        fill_low(low_s, q, here)
        for (ref, first), (_, _, d) in zip(here, views):
            for o in range(2):
                at = key_chunk(cls, xl, z, o, d)
                rows = slice(first + o * PIECE, first + o * PIECE + CHUNK)
                key = ref[rows, :HEAD]
                kc[at] = key
                vc[at] = ref[rows, HEAD:]
                kt[at] = key.T
        dk[...] = jnp.zeros(dk.shape, WIDE)
        dv[...] = jnp.zeros(dv.shape, WIDE)
        dqt[...] = before[...] if last else jnp.zeros(dqt.shape, WIDE)

        for i in range(NY):
            for kind in range(3):
                for o in range(2):
                    for dy in range(NY):
                        b, to = place(o, dy)
                        c, frm = place(o, (dy - i) % NY)
                        b, c = kind * BLOCKS + b, kind * BLOCKS + c
                        al[i, b : b + 1, to : to + GROUP] = st[i][c : c + 1, frm : frm + GROUP]
        tops = [al[i, :BLOCKS] for i in range(NY)]
        top = functools.reduce(jnp.maximum, tops)
        factors = [jnp.exp2(t - top) for t in tops]
        mass = sum(f * al[i, BLOCKS : 2 * BLOCKS] for i, f in enumerate(factors))
        share = sum(f * al[i, 2 * BLOCKS :] for i, f in enumerate(factors))
        lse_s[...] = top + jnp.log2(mass)
        delta_s[...] = share / mass

        def one_block(block, _):
            lse = lse_s[pl.ds(block, 1), :]
            delta = delta_s[pl.ds(block, 1), :]
            qp = qs[block]
            up = us[block]

            def tile(c, n, mask):
                k = kc[pl.ds(c, n)].reshape(n * CHUNK, HEAD)
                v = vc[pl.ds(c, n)].reshape(n * CHUNK, HEAD)
                p = jnp.exp2(mask(dot(k, qp, NT) * C2) - lse)
                ds = (p * (dot(v, up, NT) - delta)).astype(LOW)
                p = p.astype(LOW)
                dv[pl.ds(c, n)] += dot(p, up).reshape(n, CHUNK, HEAD)
                dk[pl.ds(c, n)] += dot(ds, qp).reshape(n, CHUNK, HEAD)
                kt_tile = jnp.concatenate([kt[c + i] for i in range(n)], axis=1)
                dqt[block] += dot(kt_tile, ds)

            over_tiles(limits(cls, block, xl, z, y, low_s), tile)
            return 0

        lax.fori_loop(0, BLOCKS, one_block, 0)

        def write(out, first, d):
            for o in range(2):
                at = key_chunk(cls, xl, z, o, d)
                rows = slice(first + o * CHUNK, first + (o + 1) * CHUNK)
                out[rows, :HEAD] = (dk[at] * SCALE).astype(out.dtype)
                out[rows, HEAD:] = dv[at].astype(out.dtype)

        if last:
            for out, d in zip(dkv_out, DISTANCES[cls]):
                write(out, 0, d)
            for dy in range(NY):
                for o in range(2):
                    block, first = place(o, dy)
                    for h in range(RATIO):
                        start = first + h * CHUNK
                        part = dqt[block, :, start : start + CHUNK].T * SCALE
                        dq_out[dy][
                            o * CHUNK : (o + 1) * CHUNK, h * HEAD : (h + 1) * HEAD
                        ] = part.astype(dq_out[dy].dtype)
        else:
            write(dkv_out[0], 0, 1)
            write(dkv_out[0], 2 * CHUNK, 3)
            write(dkv_out[1], 0, 7)
            write(dkv_out[1], 2 * CHUNK, 5)
            write(dkv_out[2], 0, 4)

    dq_state = jax.ShapeDtypeStruct((BLOCKS, HEAD, ROWS), WIDE)
    if last:
        out_shape = [
            jax.ShapeDtypeStruct((2 * CHUNK, GROUP), WIDE if dy == 0 else LOW)
            for dy in range(NY)
        ] + [
            jax.ShapeDtypeStruct((2 * CHUNK, 2 * HEAD), WIDE) for d in DISTANCES[cls]
        ]
    else:
        out_shape = [dq_state] + [
            jax.ShapeDtypeStruct((n * CHUNK, 2 * HEAD), LOW) for n in (4, 4, 2)
        ]
    state = [dq_before] if last else []
    return pl.pallas_call(
        kernel,
        in_specs=[sspec()] + [vspec()] * (12 + n + len(state)),
        out_specs=[vspec()] * len(out_shape),
        out_shape=out_shape,
        scratch_shapes=[
            pltpu.VMEM((BLOCKS, ROWS, HEAD), LOW),
            pltpu.VMEM((BLOCKS, ROWS, HEAD), LOW),
            pltpu.VMEM((chunks, CHUNK, HEAD), LOW),
            pltpu.VMEM((chunks, CHUNK, HEAD), LOW),
            pltpu.VMEM((chunks, HEAD, CHUNK), LOW),
            pltpu.VMEM((chunks, CHUNK, HEAD), WIDE),
            pltpu.VMEM((chunks, CHUNK, HEAD), WIDE),
            pltpu.VMEM((NY, 3 * BLOCKS, ROWS), WIDE),
            pltpu.VMEM((BLOCKS, ROWS), WIDE),
            pltpu.VMEM((BLOCKS, ROWS), WIDE),
            pltpu.VMEM((BLOCKS, ROWS), WIDE),
        ]
        + ([pltpu.VMEM((BLOCKS, HEAD, ROWS), WIDE)] if last else []),
        compiler_params=params(32),
        cost_estimate=pl.CostEstimate(
            flops=8 * 10**9, bytes_accessed=6 * 2**20, transcendentals=2 * 2**20
        ),
        name="backward%d" % cls,
    )(scalars, *stats, *q_blocks, *u_blocks, *arrays, *state)


def settle(dq, dq_got, dkv, dkv_got):
    def kernel(*refs):
        dq_ref, a, b, c, dkv_ref, d, e, f, keep, send = refs
        for out, first in ((keep, 0), (send, CHUNK)):
            rows = slice(first, first + CHUNK)
            total = dq_ref[rows, :]
            for g in (a, b, c):
                total += g[rows, :].astype(WIDE)
            out[:, :GROUP] = total.astype(LOW)
            total = dkv_ref[rows, :]
            for g in (d, e, f):
                total += g[rows, :].astype(WIDE)
            out[:, GROUP:] = total.astype(LOW)

    return pl.pallas_call(
        kernel,
        in_specs=[vspec()] * 8,
        out_specs=[vspec()] * 2,
        out_shape=[jax.ShapeDtypeStruct((CHUNK, GROUP + 2 * HEAD), LOW)] * 2,
        compiler_params=params(8),
        name="settle",
    )(dq, *dq_got, dkv, *dkv_got)


def join(scalars, keep, back):
    def kernel(sc, keep_ref, back_ref, q_ref, k_ref, v_ref):
        xl = sc[0]
        for g, ref in ((xl, keep_ref), (1 - xl, back_ref)):
            q_ref[:, pl.ds(pl.multiple_of(g * GROUP, GROUP), GROUP)] = ref[:, :GROUP]
            at = pl.ds(pl.multiple_of(g * HEAD, HEAD), HEAD)
            k_ref[:, at] = ref[:, GROUP : GROUP + HEAD]
            v_ref[:, at] = ref[:, GROUP + HEAD :]

    return pl.pallas_call(
        kernel,
        in_specs=[sspec(), vspec(), vspec()],
        out_specs=[vspec()] * 3,
        out_shape=[
            jax.ShapeDtypeStruct((CHUNK, 2 * GROUP), LOW),
            jax.ShapeDtypeStruct((CHUNK, 2 * HEAD), LOW),
            jax.ShapeDtypeStruct((CHUNK, 2 * HEAD), LOW),
        ],
        compiler_params=params(8),
        name="join",
    )(scalars, keep, back)


def shift(x, axis, size, d):
    return lax.ppermute(x, axis, [(i, (i - d) % size) for i in range(size)])


def swap(x):
    return shift(x, "xl", XL, 1)


def below(whole, x):
    return lax.dynamic_update_slice(whole, x, (whole.shape[0] - x.shape[0], 0))


def along_y(x):
    return [x] + [shift(x, "y", NY, d) for d in (1, 2, 3)]


def per_device(queries, keys, values, grad_out, out_weight, segments):
    xl, z, y = lax.axis_index("xl"), lax.axis_index("z"), lax.axis_index("y")
    tp = lax.axis_index("xh") * 2 + lax.axis_index("core")
    scalars = jnp.stack([xl, z, y, tp]).astype(jnp.int32)

    far = shift(grad_out, "xh", 2, 1)
    mate = shift(grad_out, "core", 2, 1)
    q_own, q_oth, kv_own, kv_oth = prepare(scalars, queries, keys, values, segments)
    kv_in = swap(kv_oth)
    q_in = swap(q_oth)

    weight, grad = stage(out_weight, grad_out)
    kv_in, _ = lax.optimization_barrier((kv_in, grad))
    kv = below(kv_own, kv_in)
    kv_up2 = shift(kv, "z", NZ, 2)
    kv_down2 = shift(kv, "z", NZ, -2)
    q_blocks = along_y(below(q_own, q_in))
    kv_late, _ = lax.optimization_barrier((kv, q_blocks[0]))
    kv_4 = shift(kv_late, "z", NZ, 4)
    kv_up = shift(jnp.concatenate([kv, kv_up2], axis=0), "z", NZ, 1)
    kv_down = shift(jnp.concatenate([kv, kv_down2], axis=0), "z", NZ, -1)
    second = 2 * PIECE
    odd = [kv_up, kv_down, kv_4]
    odd_views = [(0, 0, 1), (0, second, 3), (1, second, 5), (1, 0, 7), (2, 0, 4)]
    even = [kv, kv_up2, kv_down2]
    even_views = [(0, 0, 0), (1, 0, 2), (2, 0, 6)]

    relay, _ = lax.optimization_barrier((far, kv))
    far_mate = shift(relay, "core", 2, 1)
    u_own, u_oth = upstream(scalars, [grad, mate, far, far_mate], weight)
    u_blocks = along_y(below(u_own, swap(u_oth)))

    o_part, ml = forward(
        scalars, q_blocks, even + odd, even_views + [(3 + a, f, d) for a, f, d in odd_views]
    )
    stats = along_y(weighted(o_part, ml, u_blocks))
    dq_state, bundle_up, bundle_down, dkv_4 = backward(
        1, scalars, stats, q_blocks, u_blocks, odd, odd_views, None
    )
    got_up = shift(bundle_up, "z", NZ, -1)
    got_down = shift(bundle_down, "z", NZ, 1)
    *dq, dkv, dkv_up2, dkv_down2 = backward(
        0, scalars, stats, q_blocks, u_blocks, even, even_views, dq_state
    )

    dkv_4, _ = lax.optimization_barrier((dkv_4, dkv))
    got_4 = shift(dkv_4, "z", NZ, 4)

    near, further = slice(0, 2 * CHUNK), slice(2 * CHUNK, None)
    dkv = dkv + got_up[near].astype(WIDE) + got_down[near].astype(WIDE)
    up2 = (dkv_up2 + got_up[further].astype(WIDE)).astype(LOW)
    down2 = (dkv_down2 + got_down[further].astype(WIDE)).astype(LOW)
    dq, up2, down2 = lax.optimization_barrier((dq, up2, down2))
    dkv_got = [
        got_4,
        shift(up2, "z", NZ, -2),
        shift(down2, "z", NZ, 2),
    ]
    dq_got = [shift(dq[d], "y", NY, -d) for d in (1, 2, 3)]
    keep, send = settle(dq[0], dq_got, dkv, dkv_got)
    return join(scalars, keep, swap(send))


def solution(mesh):
    fine = Mesh(mesh.devices.reshape(XL, NZ, NY, 2, 2), ("xl", "z", "y", "xh", "core"))
    ctx, tp = ("xl", "z", "y"), ("xh", "core")
    in_specs = (P(ctx, tp), P(ctx, tp), P(ctx, tp), P(ctx, tp), P(None, tp), P(ctx))
    out_specs = (P(ctx, tp), P(ctx, tp), P(ctx, tp))
    return jax.shard_map(
        per_device, mesh=fine, in_specs=in_specs, out_specs=out_specs, check_vma=False
    )
```
